32 devices in a mesh: ctx: 8 (over y, x, core), tp: 4 (over z).
Axes of the slice: x: 2, y: 2, z: 4, core: 2. Of those that a mesh axis runs over, the one named last changes fastest.
Arguments:
- x_in: bfloat16 [4096, 8192], P('ctx', 'tp'), may hold values from -6 to 6
- gate_z: bfloat16 [4096, 8192], P('ctx', 'tp'), may hold values from -6 to 6
- b_in: bfloat16 [4096, 1024], P('ctx', 'tp'), may hold values from -1.5 to 1.5
- c_in: bfloat16 [4096, 1024], P('ctx', 'tp'), may hold values from -1.5 to 1.5
- step_size: float32 [4096, 128], P('ctx', 'tp'), may hold values from 0 to 2
- log_decay: float32 [4096, 128], P('ctx', 'tp'), may hold values from -1 to 0
- skip: float32 [128], P('tp'), may hold values from 0.5 to 2
- norm_gain: float32 [8192], P('tp'), may hold values from 0.1 to 1.9
- out_weight: bfloat16 [8192, 4096], P('tp'), may hold values from -0.0625 to 0.0625
Outputs:
- layer_out: bfloat16 [4096, 4096], P(('ctx', 'tp'))
The draws below stay inside these ranges and needn't reach their ends.
All inputs are finite; a program needn't handle non-finite values.
Results may differ from the reference program's by a relative error of at most 0.023.
Values may be sent and summed in bfloat16 or wider, within the bound.
No kernel may reach another device: no remote copies, remote signals or barrier semaphores. Data moves between devices by JAX's collectives and lax.ppermute only.
A program may use at most 128 MiB of HBM per device.

```python
import math
from functools import partial
import jax
import jax.numpy as jnp
from jax import lax

HEADS = 128
HEAD_DIM = 64
STATE = 128
GROUPS = 8
DOUT = 4096
SPAN = 256
LEN_DEV = 512
DOCUMENT_TOKENS = 4096
DINNER = 8192
N_TP = 4


def fast_heads(key):
    share = 0.5
    return jax.random.uniform(jax.random.fold_in(key, 11), (HEADS,)) < share


def draw_log_decay(key, part):
    fast = fast_heads(key)
    keys = jax.random.split(jax.random.fold_in(key, 23), 6)
    fast_rate = jnp.exp(jax.random.uniform(keys[0], (HEADS,), jnp.float32, math.log(1.0 / 50.0), math.log(1.0 / 30.0)))
    slow_rate = jnp.exp(jax.random.uniform(keys[1], (HEADS,), jnp.float32, math.log(0.05), math.log(0.3))) / LEN_DEV
    speed_factor = jnp.where(fast, fast_rate, slow_rate)
    coarse_estimate = jnp.exp(jax.random.uniform(keys[2], (DOCUMENT_TOKENS, HEADS), jnp.float32, -0.5 * math.log(2.0), 0.5 * math.log(2.0)))
    zone_quantity = jnp.exp(jax.random.uniform(keys[3], (DOCUMENT_TOKENS // SPAN, 1), jnp.float32, -0.5 * math.log(2.0), 0.5 * math.log(2.0)))
    zone_quantity = jnp.repeat(zone_quantity, SPAN, axis=0)
    marked_locations = jax.random.randint(keys[4], (3,), 0, DOCUMENT_TOKENS)
    pulse_amplitude = jnp.any(jnp.arange(DOCUMENT_TOKENS)[:, None] == marked_locations[None, :], axis=1)
    layer_level = jax.random.uniform(keys[5], (DOCUMENT_TOKENS, HEADS), jnp.float32, math.log(1.25), math.log(2.0))
    return (-(speed_factor[None, :] * coarse_estimate * zone_quantity) - jnp.where(pulse_amplitude[:, None], layer_level, 0.0)).astype(jnp.float32)


def draw_step_size(key, part):
    fast = fast_heads(key)
    noise_key = jax.random.fold_in(key, 37)
    base = jnp.where(fast, 1.0, 2.0 / jnp.sqrt(jnp.float32(LEN_DEV)))
    coarse_estimate = jnp.exp(jax.random.uniform(noise_key, (DOCUMENT_TOKENS, HEADS), jnp.float32, -math.log(2.0), math.log(2.0)))
    return (base[None, :] * coarse_estimate).astype(jnp.float32)


def levels(rng, shape, cuts, least, high):
    level = 1.0
    for position, parts in cuts:
        heights = jax.random.uniform(jax.random.fold_in(jax.random.fold_in(rng, 6), position), (parts,), jnp.float32, least / len(cuts), high / len(cuts))
        level = level * jnp.repeat(jnp.exp(heights), shape[position] // parts).reshape((-1,) + (1,) * (len(shape) - 1 - position))
    return level


def gaussian(stream_key, dims, scale, most, pieces=(), kind=jnp.bfloat16):
    drawn = scale * jax.random.normal(stream_key, dims, jnp.float32)
    if pieces:
        drawn = drawn * levels(stream_key, dims, pieces, -0.22, 0.18)
    return jnp.clip(drawn, -most, most).astype(kind)


def setup_inputs(seed: int = 0) -> dict:
    splits = jax.random.split(jax.random.key(seed), 10)
    x_in = gaussian(splits[0], (DOCUMENT_TOKENS, DINNER), 1.0, 6.0, ((0, 8), (1, 4)))
    gate_z = gaussian(splits[1], (DOCUMENT_TOKENS, DINNER), 1.0, 6.0, ((0, 8), (1, 4)))
    b_in = gaussian(splits[2], (DOCUMENT_TOKENS, GROUPS * STATE), 0.25, 1.5, ((0, 8), (1, 4)))
    c_in = gaussian(splits[3], (DOCUMENT_TOKENS, GROUPS * STATE), 0.25, 1.5, ((0, 8), (1, 4)))
    step_size = draw_step_size(jax.random.fold_in(splits[9], 71), 0)
    log_decay = draw_log_decay(jax.random.fold_in(splits[9], 71), 0)
    skip = jnp.clip(0.5 + 1.5 * jax.random.uniform(splits[6], (HEADS,), jnp.float32) ** levels(splits[6], (HEADS,), ((0, 4),), -0.2, 0.2), 0.5, 2.0)
    norm_gain = jnp.clip(1.0 + 0.18 * jax.random.normal(splits[7], (DINNER,), jnp.float32), 0.1, 1.9)
    out_weight = gaussian(splits[8], (DINNER, DOUT), DINNER ** -0.5, 0.0625, ((0, 4),))
    return {"x_in": x_in, "gate_z": gate_z, "b_in": b_in, "c_in": c_in, "step_size": step_size, "log_decay": log_decay, "skip": skip, "norm_gain": norm_gain, "out_weight": out_weight}


def block_pass(states, inputs, per_group):
    scaled, decay_log, b_block, c_block = inputs
    block_len = decay_log.shape[0]
    head_count = decay_log.shape[1]
    group_count = b_block.shape[1]
    running = jnp.cumsum(decay_log, axis=0)
    b_wide = b_block.astype(jnp.float32)
    c_wide = c_block.astype(jnp.float32)
    scores = jnp.einsum('tgn,sgn->gts', c_wide, b_wide, precision=lax.Precision.HIGHEST)
    scores = jnp.repeat(scores, per_group, axis=0)
    run_heads = running.T
    spread = run_heads[:, :, None] - run_heads[:, None, :]
    causal = lax.broadcasted_iota(jnp.int32, (block_len, block_len), 0) >= lax.broadcasted_iota(jnp.int32, (block_len, block_len), 1)
    decays = jnp.where(causal[None], jnp.exp(jnp.where(causal[None], spread, 0.0)), 0.0)
    weights = scores * decays
    within = jnp.einsum('hts,shp->thp', weights, scaled, precision=lax.Precision.HIGHEST)
    grouped = states.reshape(group_count, per_group, states.shape[1], states.shape[2])
    carried = jnp.einsum('tgn,gkpn->tgkp', c_wide, grouped, precision=lax.Precision.HIGHEST)
    carried = carried.reshape(block_len, head_count, states.shape[1]) * jnp.exp(running)[:, :, None]
    tail_decay = jnp.exp(running[-1][None, :] - running)
    weighted = (scaled * tail_decay[:, :, None]).reshape(block_len, group_count, per_group, states.shape[1])
    fresh_in = jnp.einsum('sgn,sgkp->gkpn', b_wide, weighted, precision=lax.Precision.HIGHEST)
    new_states = states * jnp.exp(running[-1])[:, None, None] + fresh_in.reshape(states.shape)
    return (new_states, within + carried)

def reference(x_in, gate_z, b_in, c_in, step_size, log_decay, skip, norm_gain, out_weight):
    total_rows = x_in.shape[0]
    blocks = total_rows // SPAN
    per_group = HEADS // GROUPS
    inputs = x_in.astype(jnp.float32).reshape(total_rows, HEADS, HEAD_DIM)
    scaled = inputs * step_size[:, :, None]
    b_groups = b_in.reshape(blocks, SPAN, GROUPS, STATE)
    c_groups = c_in.reshape(blocks, SPAN, GROUPS, STATE)
    start_state = jnp.zeros((HEADS, HEAD_DIM, STATE), jnp.float32)
    final_state, outputs = lax.scan(partial(block_pass, per_group=per_group), start_state, (scaled.reshape(blocks, SPAN, HEADS, HEAD_DIM), log_decay.reshape(blocks, SPAN, HEADS), b_groups, c_groups))
    outputs = outputs.reshape(total_rows, HEADS, HEAD_DIM)
    mixed = (outputs + skip[None, :, None] * inputs).reshape(total_rows, DINNER)
    mixed = mixed * jax.nn.silu(gate_z.astype(jnp.float32))
    by_group = mixed.reshape(total_rows, GROUPS, DINNER // GROUPS)
    meansq = lax.optimization_barrier(jnp.mean(by_group * by_group, axis=2, keepdims=True))
    normed = ((by_group * lax.rsqrt(meansq + 1e-05)).reshape(total_rows, DINNER) * norm_gain[None, :]).astype(jnp.bfloat16)
    split = DINNER // N_TP

    def add_block(total, block_index):
        piece = lax.dynamic_slice_in_dim(normed, block_index * split, split, 1)
        rows_block = lax.dynamic_slice_in_dim(out_weight, block_index * split, split, 0)
        partial_sum = jnp.dot(piece, rows_block, preferred_element_type=jnp.float32)
        rounded = lax.optimization_barrier(partial_sum.astype(jnp.bfloat16))
        return (total + rounded.astype(jnp.float32), None)
    summed, unused = lax.scan(add_block, jnp.zeros((total_rows, DOUT), jnp.float32), jnp.arange(N_TP, dtype=jnp.int32))
    return summed.astype(jnp.bfloat16)
```

```python
from functools import partial

import jax
import jax.numpy as jnp
from jax import lax
from jax.experimental import pallas as pl
from jax.experimental.pallas import tpu as pltpu
from jax.sharding import PartitionSpec as P

HEAD_DIM = 64
STATE = 128
CHUNK = 128
MIDDLE = CHUNK // 2 - 1
EXTRA = 16
COLUMN_TILE = 512
HALVES = 2
VMEM = 56 * 2**20
F32 = jnp.float32
BF16 = jnp.bfloat16


def params():
    return pltpu.CompilerParams(vmem_limit_bytes=VMEM)


def dot(a, b):
    return jnp.dot(a, b, preferred_element_type=F32)


def dot_exact(a, b):
    return jnp.dot(a, b, preferred_element_type=F32, precision=lax.Precision.HIGHEST)


def head_map(heads, channels):
    head = lax.broadcasted_iota(jnp.int32, (2 * heads, channels), 0) & (heads - 1)
    place = lax.broadcasted_iota(jnp.int32, (2 * heads, channels), 1) >> 6
    return jnp.where(head == place, 1.0, 0.0).astype(BF16)


def high_low(values, heads):
    high = values.astype(BF16).astype(F32)
    lane = lax.broadcasted_iota(jnp.int32, values.shape, 1)
    return jnp.where(lane < heads, high, values - high).astype(BF16)


def twice(values):
    return jnp.concatenate([values, values], axis=1)


def pieces(values, rows):
    first = values.astype(BF16).astype(F32)
    second = (values - first).astype(BF16).astype(F32)
    third = values - first - second
    row = lax.broadcasted_iota(jnp.int32, (rows, values.shape[1]), 0)
    stacked = jnp.where(row == 0, first, jnp.where(row == 1, second, jnp.where(row == 2, third, 0.0)))
    return stacked.astype(BF16)


def state_kernel(groups, core_ref, x_ref, b_ref, step_ref, decay_ref, rhs_ref, inner_ref, outer_ref, send_ref, keep_ref,
                 state, sums, spread):
    chunk = pl.program_id(0)
    heads, channels = step_ref.shape[1], x_ref.shape[1]
    width = channels // groups

    @pl.when(chunk == 0)
    def _():
        state[...] = jnp.zeros_like(state)
        sums[...] = jnp.zeros_like(sums)
        spread[...] = head_map(heads, channels)

    row = lax.broadcasted_iota(jnp.int32, (CHUNK, CHUNK), 0)
    column = lax.broadcasted_iota(jnp.int32, (CHUNK, CHUNK), 1)
    lower = jnp.where(row >= column, 1.0, 0.0)
    running = dot_exact(lower, twice(decay_ref[...]))
    middle, total = running[MIDDLE : MIDDLE + 1], running[CHUNK - 1 : CHUNK]
    before = sums[0:1]
    inner = running - middle
    inner_ref[...] = high_low(jnp.exp(inner), heads)
    outer_ref[...] = high_low(jnp.exp(before + running), heads)
    weight = twice(step_ref[...]) * jnp.exp(-inner)
    factor_row = lax.broadcasted_iota(jnp.int32, (EXTRA, 2 * heads), 0)
    factors = jnp.exp(jnp.where(factor_row == 0, total, jnp.where(factor_row == 1, total - middle, middle)))
    wide = dot(jnp.concatenate([high_low(weight, heads), high_low(factors, heads)], axis=0), spread[...])
    weighted = (x_ref[...].astype(F32) * wide[:CHUNK]).astype(BF16)
    old = state[...]
    rhs_ref[:CHUNK, :] = weighted
    rhs_ref[CHUNK:, :] = (old * wide[CHUNK + 2 : CHUNK + 3]).astype(BF16)
    for g in range(groups):
        cut = slice(g * width, (g + 1) * width)
        fresh = lax.dot_general(
            b_ref[:, g * STATE : (g + 1) * STATE],
            weighted[:, cut],
            (((0,), (0,)), ((), ())),
            preferred_element_type=F32,
        )
        state[:, cut] = old[:, cut] * wide[CHUNK : CHUNK + 1, cut] + fresh * wide[CHUNK + 1 : CHUNK + 2, cut]
    sums[0:1] = before + total

    @pl.when(chunk == pl.num_programs(0) - 1)
    def _():
        end = state[...].astype(BF16)
        logs = dot(pieces(sums[0:1, :heads], EXTRA), spread[:heads, :]).astype(BF16)
        half = channels // 2
        for core in range(2):

            @pl.when(core_ref[0] == core)
            def _():
                own = slice(core * half, (core + 1) * half)
                other = slice((1 - core) * half, (2 - core) * half)
                keep_ref[:STATE, :] = end[:, own]
                keep_ref[STATE:, :] = logs[:, own]
                send_ref[:STATE, :] = end[:, other]
                send_ref[STATE:, :] = logs[:, other]


def log_of(ref):
    return jnp.sum(ref[STATE:, :].astype(F32), axis=0, keepdims=True)


def pair_kernel(core_ref, own_ref, sibling_ref, pair_ref):
    own_log, sibling_log = log_of(own_ref), log_of(sibling_ref)
    early = core_ref[0] == 0
    own_scale = jnp.where(early, jnp.exp(sibling_log), 1.0)
    sibling_scale = jnp.where(early, 1.0, jnp.exp(own_log))
    pair = own_ref[:STATE, :].astype(F32) * own_scale + sibling_ref[:STATE, :].astype(F32) * sibling_scale
    pair_ref[:STATE, :] = pair.astype(BF16)
    pair_ref[STATE:, :] = pieces(own_log + sibling_log, EXTRA)


def join_kernel(late_ref, early_ref, out_ref):
    late_log, early_log = log_of(late_ref), log_of(early_ref)
    out_ref[:STATE, :] = (
        late_ref[:STATE, :].astype(F32) + early_ref[:STATE, :].astype(F32) * jnp.exp(late_log)
    ).astype(BF16)
    out_ref[STATE:, :] = pieces(late_log + early_log, EXTRA)


def last_kernel(core_ref, near_ref, far_ref, own_ref, sibling_ref, keep_ref, send_ref):
    near = near_ref[:STATE, :].astype(F32)
    chip = near + far_ref[:STATE, :].astype(F32) * jnp.exp(log_of(near_ref))
    for core, first, mine, other in ((0, own_ref, 0, 1), (1, sibling_ref, 1, 0)):

        @pl.when(core_ref[0] == core)
        def _():
            after = chip * jnp.exp(log_of(first)) + first[:STATE, :].astype(F32)
            both = (chip.astype(BF16), after.astype(BF16))
            keep_ref[...] = both[mine]
            send_ref[...] = both[other]


def local_kernel(groups, x_ref, gate_ref, b_ref, c_ref, rhs_ref, inner_ref, outer_ref, skip_ref, mixed_ref, scale_ref,
                 spread):
    heads, channels = skip_ref.shape[1], x_ref.shape[1]
    width = channels // groups

    @pl.when(pl.program_id(0) == 0)
    def _():
        spread[...] = head_map(heads, channels)

    row = lax.broadcasted_iota(jnp.int32, (CHUNK, CHUNK), 0)
    column = lax.broadcasted_iota(jnp.int32, (CHUNK, CHUNK), 1)
    skip = high_low(jnp.broadcast_to(twice(skip_ref[...]), (EXTRA, 2 * heads)), heads)
    for g in range(groups):
        cut = slice(g * width, (g + 1) * width)
        part = slice(g * STATE, (g + 1) * STATE)
        to_wide = spread[:, cut]
        scores = lax.dot_general(
            c_ref[:, part], b_ref[:, part], (((1,), (1,)), ((), ())), preferred_element_type=F32
        )
        scores = jnp.where(row >= column, scores, 0.0).astype(BF16)
        within = dot(jnp.concatenate([scores, c_ref[:, part]], axis=1), rhs_ref[:, cut])
        gate = gate_ref[:, cut].astype(F32)
        gate = gate / (1.0 + jnp.exp(-gate))
        passed = x_ref[:, cut].astype(F32) * dot(skip, to_wide)[0:1]
        mixed_ref[:, cut] = (within * dot(inner_ref[...], to_wide) + passed) * gate
        scale_ref[:, cut] = dot(outer_ref[...], to_wide) * gate


def norm_rows(groups, state, mixed, scale, c_rows, gain):
    width = mixed.shape[1] // groups
    parts = []
    for g in range(groups):
        cut = slice(g * width, (g + 1) * width)
        carried = dot(c_rows[:, g * STATE : (g + 1) * STATE], state[:, cut])
        whole = mixed[:, cut] + scale[:, cut] * carried
        meansq = jnp.mean(whole * whole, axis=1, keepdims=True)
        parts.append((whole * lax.rsqrt(meansq + 1e-05) * gain[:, cut]).astype(BF16))
    return parts


def fill_state(core_ref, keep_ref, recv_ref, state):
    half = keep_ref.shape[1]
    for core in range(2):

        @pl.when(core_ref[0] == core)
        def _():
            state[:, core * half : (core + 1) * half] = keep_ref[...]
            state[:, (1 - core) * half : (2 - core) * half] = recv_ref[...]


def first_kernel(groups, place_ref, mixed_ref, scale_ref, c_ref, keep_ref, recv_ref, gain_ref, w_ref, out_ref, normed_ref,
                 state, normed):
    @pl.when(pl.program_id(0) == 0)
    def _():
        fill_state(place_ref, keep_ref, recv_ref, state)
        width = normed.shape[1] // groups
        rows = norm_rows(groups, state, mixed_ref, scale_ref, c_ref, gain_ref)
        for g, part in enumerate(rows):
            normed[:, g * width : (g + 1) * width] = part
        normed_ref[...] = normed[...]

    out_ref[...] = dot(normed[...], w_ref[...]).astype(BF16)


def second_kernel(normed_ref, w_ref, out_ref):
    out_ref[...] = dot(normed_ref[...], w_ref[...]).astype(BF16)


def rest_kernel(groups, blocks, place_ref, mixed_ref, scale_ref, c_ref, keep_ref, recv_ref, gain_ref, w_ref, a_ref, b_ref,
                out_ref, state, normed):
    step = pl.program_id(0)
    size = a_ref.shape[0]

    @pl.when(step == 0)
    def _():
        fill_state(place_ref, keep_ref, recv_ref, state)
        width = normed.shape[1] // groups
        for n in range(1, blocks):
            here = pl.ds(pl.multiple_of(place_ref[1 + n] * size, size), size)
            rows = norm_rows(groups, state, mixed_ref.at[here, :], scale_ref.at[here, :], c_ref.at[here, :], gain_ref)
            for g, part in enumerate(rows):
                normed[(n - 1) * size : n * size, g * width : (g + 1) * width] = part

    product = dot(normed[...], w_ref[...]).astype(BF16)
    for n in range(1, blocks):
        here = pl.ds(pl.multiple_of(place_ref[1 + n] * size, size), size)
        out_ref[here, :] = product[(n - 1) * size : n * size]
    here = pl.ds(pl.multiple_of(place_ref[1] * size, size), size)
    in_first = step < pl.num_programs(0) // 2

    @pl.when(in_first)
    def _():
        out_ref[here, :] = a_ref[...]

    @pl.when(jnp.logical_not(in_first))
    def _():
        out_ref[here, :] = b_ref[...]


def whole_block(shape):
    return pl.BlockSpec(shape, lambda *_: (0,) * len(shape))


def shape_of(shape, kind=BF16):
    return jax.ShapeDtypeStruct(shape, kind)


def block_order(here, count):
    table = []
    for i in range(count):
        order = []
        for step in range(1, count):
            for block, sends in ((count - step + i, i <= step - 1), (step - count + i, i >= count - step)):
                if sends and block not in order:
                    order.append(block)
        table.append(order + [b for b in range(count) if b not in order])
    return jnp.asarray(table, jnp.int32)[here]


def line_reduce(first, partial_sums, size, columns):
    count = lax.axis_size("tp")
    here = lax.axis_index("tp")
    done = []
    for half in range(HALVES):
        cut = columns // HALVES

        def own(block, half=half, cut=cut):
            block = jnp.clip(block, 0, count - 1)
            return lax.dynamic_slice(partial_sums, (block * size, half * cut), (size, cut))

        right = left = None
        for step in range(1, count):
            to_right = [(i, i + 1) for i in range(step)]
            to_left = [(i, i - 1) for i in range(count - step, count)]
            if step == 1 and count > 3:
                both = lax.ppermute(first[half], "tp", to_right + to_left)
                right = jnp.where(here == 1, both, jnp.zeros_like(both))
                left = jnp.where(here == count - 2, both, jnp.zeros_like(both))
                continue
            if step == 1:
                send_right = send_left = first[half]
            else:
                send_right = (own(count - step + here).astype(F32) + right.astype(F32)).astype(BF16)
                send_left = (own(step - count + here).astype(F32) + left.astype(F32)).astype(BF16)
            right = lax.ppermute(send_right, "tp", to_right)
            left = lax.ppermute(send_left, "tp", to_left)
        done.append((own(here).astype(F32) + right.astype(F32) + left.astype(F32)).astype(BF16))
    return jnp.concatenate(done, axis=1)


def on_device(x_in, gate_z, b_in, c_in, step_size, log_decay, skip, norm_gain, out_weight):
    rows, channels = x_in.shape
    heads = step_size.shape[1]
    groups = b_in.shape[1] // STATE
    chunks = rows // CHUNK
    columns = out_weight.shape[1]
    half = channels // 2
    devices = lax.axis_size("ctx")
    chips = devices // 2
    core = lax.rem(lax.axis_index("ctx"), 2).astype(jnp.int32).reshape(1)
    message = (STATE + EXTRA, half)

    by_chunk = lambda width: pl.BlockSpec((CHUNK, width), lambda i, *_: (i, 0))
    rhs, inner, outer, send, own = pl.pallas_call(
        partial(state_kernel, groups),
        grid_spec=pltpu.PrefetchScalarGridSpec(
            num_scalar_prefetch=1,
            grid=(chunks,),
            in_specs=[by_chunk(channels), by_chunk(groups * STATE), by_chunk(heads), by_chunk(heads)],
            out_specs=[
                pl.BlockSpec((CHUNK + STATE, channels), lambda i, *_: (i, 0)),
                by_chunk(2 * heads),
                by_chunk(2 * heads),
                whole_block(message),
                whole_block(message),
            ],
            scratch_shapes=[
                pltpu.VMEM((STATE, channels), F32),
                pltpu.VMEM((8, 2 * heads), F32),
                pltpu.VMEM((2 * heads, channels), BF16),
            ],
        ),
        out_shape=[
            shape_of((chunks * (CHUNK + STATE), channels)),
            shape_of((rows, 2 * heads)),
            shape_of((rows, 2 * heads)),
            shape_of(message),
            shape_of(message),
        ],
        compiler_params=params(),
        name="chunk_states",
    )(core, x_in, b_in, step_size, log_decay)

    swap = [(i, i ^ 1) for i in range(devices)]
    scalar = pl.BlockSpec(memory_space=pltpu.SMEM)
    block = whole_block(message)

    def small(kernel, name, ins, outs):
        return pl.pallas_call(
            kernel,
            in_specs=[scalar if v.dtype == jnp.int32 else whole_block(v.shape) for v in ins],
            out_specs=[whole_block(s) for s in outs],
            out_shape=[shape_of(s) for s in outs],
            compiler_params=params(),
            name=name,
        )(*ins)

    def local_part(first, count, x_in):
        at = lambda width, size=CHUNK: pl.BlockSpec((size, width), lambda i: (first + i, 0))
        to = lambda width: pl.BlockSpec((CHUNK, width), lambda i: (i, 0))
        return pl.pallas_call(
            partial(local_kernel, groups),
            grid=(count,),
            in_specs=[
                at(channels),
                at(channels),
                at(groups * STATE),
                at(groups * STATE),
                at(channels, CHUNK + STATE),
                at(2 * heads),
                at(2 * heads),
                whole_block((1, heads)),
            ],
            out_specs=[to(channels), to(channels)],
            out_shape=[shape_of((count * CHUNK, channels), F32)] * 2,
            scratch_shapes=[pltpu.VMEM((2 * heads, channels), BF16)],
            compiler_params=params(),
            cost_estimate=pl.CostEstimate(flops=count * 2 * 10**9, bytes_accessed=count * 5 * 10**6, transcendentals=0),
            name="local_part",
        )(x_in, gate_z, b_in, c_in, rhs, inner, outer, skip.reshape(1, heads))

    sibling = lax.ppermute(send, "ctx", swap)
    (pair,) = small(pair_kernel, "pair", (core, own, sibling), (message,))
    x_late, pair = lax.optimization_barrier((x_in, pair))
    near, far = None, lax.ppermute(pair, "ctx", [(i, i + 2) for i in range(devices - 2)])
    mixed, scale = local_part(0, chunks, x_late)
    distance = 2
    while distance < chips:
        (near,) = (far,) if near is None else small(join_kernel, "join", (near, far), (message,))
        (outgoing,) = small(join_kernel, "join", (pair, near), (message,))
        far = lax.ppermute(outgoing, "ctx", [(i, i + 2 * distance) for i in range(devices - 2 * distance)])
        distance *= 2
    state_shape = (STATE, half)
    keep, send = small(last_kernel, "incoming", (core, near, far, own, sibling), (state_shape, state_shape))
    recv = lax.ppermute(send, "ctx", swap)

    count = lax.axis_size("tp")
    size = rows // count
    place = jnp.concatenate([core, block_order(lax.axis_index("tp"), count)])
    gain = norm_gain.reshape(1, channels)
    tiles = columns // COLUMN_TILE
    row_block = lambda width: pl.BlockSpec((size, width), lambda j, p: (p[1], 0))
    first_a, normed = pl.pallas_call(
        partial(first_kernel, groups),
        grid_spec=pltpu.PrefetchScalarGridSpec(
            num_scalar_prefetch=1,
            grid=(tiles // 2,),
            in_specs=[
                row_block(channels),
                row_block(channels),
                row_block(groups * STATE),
                whole_block(state_shape),
                whole_block(state_shape),
                whole_block((1, channels)),
                pl.BlockSpec((channels, COLUMN_TILE), lambda j, p: (0, j)),
            ],
            out_specs=[pl.BlockSpec((size, COLUMN_TILE), lambda j, p: (0, j)), whole_block((size, channels))],
            scratch_shapes=[pltpu.VMEM((STATE, channels), BF16), pltpu.VMEM((size, channels), BF16)],
        ),
        out_shape=[shape_of((size, columns // 2)), shape_of((size, channels))],
        compiler_params=params(),
        name="first_block",
    )(place, mixed, scale, c_in, keep, recv, gain, out_weight)
    first_b = pl.pallas_call(
        second_kernel,
        grid=(tiles // 2,),
        in_specs=[
            whole_block((size, channels)),
            pl.BlockSpec((channels, COLUMN_TILE), lambda j: (0, tiles // 2 + j)),
        ],
        out_specs=pl.BlockSpec((size, COLUMN_TILE), lambda j: (0, j)),
        out_shape=shape_of((size, columns // 2)),
        compiler_params=params(),
        cost_estimate=pl.CostEstimate(
            flops=size * channels * columns, bytes_accessed=channels * columns, transcendentals=0
        ),
        name="first_block_rest",
    )(normed, out_weight)
    partial_sums = pl.pallas_call(
        partial(rest_kernel, groups, count),
        grid_spec=pltpu.PrefetchScalarGridSpec(
            num_scalar_prefetch=1,
            grid=(tiles,),
            in_specs=[
                whole_block((rows, channels)),
                whole_block((rows, channels)),
                whole_block((rows, groups * STATE)),
                whole_block(state_shape),
                whole_block(state_shape),
                whole_block((1, channels)),
                pl.BlockSpec((channels, COLUMN_TILE), lambda j, p: (0, j)),
                pl.BlockSpec((size, COLUMN_TILE), lambda j, p: (0, jnp.minimum(j, tiles // 2 - 1))),
                pl.BlockSpec((size, COLUMN_TILE), lambda j, p: (0, jnp.maximum(j - tiles // 2, 0))),
            ],
            out_specs=pl.BlockSpec((rows, COLUMN_TILE), lambda j, p: (0, j)),
            scratch_shapes=[pltpu.VMEM((STATE, channels), BF16), pltpu.VMEM((rows - size, channels), BF16)],
        ),
        out_shape=shape_of((rows, columns)),
        compiler_params=params(),
        cost_estimate=pl.CostEstimate(
            flops=2 * (rows - size) * channels * columns, bytes_accessed=2 * channels * columns, transcendentals=0
        ),
        name="other_blocks",
    )(place, mixed, scale, c_in, keep, recv, gain, out_weight, first_a, first_b)
    return line_reduce((first_a, first_b), partial_sums, size, columns)


def solution(mesh):
    placed = (
        P("ctx", "tp"),
        P("ctx", "tp"),
        P("ctx", "tp"),
        P("ctx", "tp"),
        P("ctx", "tp"),
        P("ctx", "tp"),
        P("tp"),
        P("tp"),
        P("tp", None),
    )
    return jax.shard_map(
        on_device, mesh=mesh, in_specs=placed, out_specs=P(("ctx", "tp"), None), check_vma=False
    )
```

```python
from functools import partial

import jax
import jax.numpy as jnp
from jax import lax
from jax.experimental import pallas as pl
from jax.experimental.pallas import tpu as pltpu
from jax.sharding import PartitionSpec as P

HEAD_DIM = 64
STATE = 128
CHUNK = 128
MIDDLE = CHUNK // 2 - 1
EXTRA = 16
COLUMN_TILE = 512
HALVES = 2
WEIGHT_COPIES = 8
F32 = jnp.float32
BF16 = jnp.bfloat16


def dot(a, b):
    return jnp.dot(a, b, preferred_element_type=F32)


def dot_exact(a, b):
    return jnp.dot(a, b, preferred_element_type=F32, precision=lax.Precision.HIGHEST)


def head_map(heads, channels):
    head = lax.broadcasted_iota(jnp.int32, (2 * heads, channels), 0) & (heads - 1)
    place = lax.broadcasted_iota(jnp.int32, (2 * heads, channels), 1) >> 6
    return jnp.where(head == place, 1.0, 0.0).astype(BF16)


def high_low(values):
    high = values.astype(BF16).astype(F32)
    return jnp.concatenate([high, values - high], axis=0)


def pieces(values, rows):
    first = values.astype(BF16).astype(F32)
    second = (values - first).astype(BF16).astype(F32)
    third = values - first - second
    row = lax.broadcasted_iota(jnp.int32, (rows, values.shape[1]), 0)
    stacked = jnp.where(row == 0, first, jnp.where(row == 1, second, jnp.where(row == 2, third, 0.0)))
    return stacked.astype(BF16)


def load(pairs, semaphores):
    copies = [pltpu.make_async_copy(src, dst, semaphores.at[n]) for n, (src, dst) in enumerate(pairs)]
    for copy in copies:
        copy.start()
    return copies


def rows_of(chunk, size=CHUNK):
    return slice(chunk * size, (chunk + 1) * size)


def state_kernel(groups, core_ref, x_hbm, b_hbm, step_hbm, decay_hbm, rhs_ref, inner_ref, outer_ref, send_ref, keep_ref,
                 x_ref, b_ref, step_ref, decay_ref, semaphores):
    rows, channels = x_ref.shape
    heads = step_ref.shape[0]
    width = channels // groups
    chunks = rows // CHUNK
    small = load([(decay_hbm, decay_ref), (step_hbm, step_ref), (b_hbm, b_ref)], semaphores)
    large = load(
        [(x_hbm.at[rows_of(n), :], x_ref.at[rows_of(n), :]) for n in range(chunks)], semaphores.at[pl.ds(3, chunks)]
    )
    spread = head_map(heads, channels)
    row = lax.broadcasted_iota(jnp.int32, (CHUNK, CHUNK), 0)
    column = lax.broadcasted_iota(jnp.int32, (CHUNK, CHUNK), 1)
    upper = jnp.where(row <= column, 1.0, 0.0)
    lane = lax.broadcasted_iota(jnp.int32, (heads, CHUNK), 1)
    before = jnp.zeros((heads, 1), F32)
    state = [jnp.zeros((STATE, width), F32)] * groups
    for copy in small:
        copy.wait()
    for n in range(chunks):
        here = rows_of(n)
        running = dot_exact(decay_ref[:, here], upper)
        middle, total = running[:, MIDDLE : MIDDLE + 1], running[:, CHUNK - 1 :]
        inner = running - middle
        inner_ref[:, here] = high_low(jnp.exp(inner)).astype(BF16)
        outer_ref[:, here] = high_low(jnp.exp(before + running)).astype(BF16)
        weight = step_ref[:, here] * jnp.exp(-inner)
        factors = jnp.exp(jnp.where(lane == 0, total, jnp.where(lane == 1, total - middle, middle)))
        stacked = jnp.concatenate([jnp.transpose(high_low(weight)), jnp.transpose(high_low(factors))[:EXTRA]], axis=0)
        stacked = stacked.astype(BF16)
        before = before + total
        large[n].wait()
        to_rhs = n * (CHUNK + STATE)
        for g in range(groups):
            cut = slice(g * width, (g + 1) * width)
            wide = dot(stacked, spread[:, cut])
            weighted = (x_ref[here, cut].astype(F32) * wide[:CHUNK]).astype(BF16)
            rhs_ref[to_rhs : to_rhs + CHUNK, cut] = weighted
            rhs_ref[to_rhs + CHUNK : to_rhs + CHUNK + STATE, cut] = (state[g] * wide[CHUNK + 2 : CHUNK + 3]).astype(BF16)
            fresh = lax.dot_general(
                b_ref[here, g * STATE : (g + 1) * STATE],
                weighted,
                (((0,), (0,)), ((), ())),
                preferred_element_type=F32,
            )
            state[g] = state[g] * wide[CHUNK : CHUNK + 1] + fresh * wide[CHUNK + 1 : CHUNK + 2]

    first = before.astype(BF16).astype(F32)
    second = (before - first).astype(BF16).astype(F32)
    third = before - first - second
    stacked = jnp.where(lane == 0, first, jnp.where(lane == 1, second, jnp.where(lane == 2, third, 0.0)))
    logs = dot(jnp.transpose(stacked)[:EXTRA].astype(BF16), spread[:heads, :]).astype(BF16)
    end = jnp.concatenate([part.astype(BF16) for part in state], axis=1)
    half = channels // 2
    for core in range(2):

        @pl.when(core_ref[0] == core)
        def _():
            own = slice(core * half, (core + 1) * half)
            other = slice((1 - core) * half, (2 - core) * half)
            keep_ref[:STATE, :] = end[:, own]
            keep_ref[STATE:, :] = logs[:, own]
            send_ref[:STATE, :] = end[:, other]
            send_ref[STATE:, :] = logs[:, other]


def log_of(ref):
    return jnp.sum(ref[STATE:, :].astype(F32), axis=0, keepdims=True)


def pair_kernel(core_ref, own_ref, sibling_ref, pair_ref):
    own_log, sibling_log = log_of(own_ref), log_of(sibling_ref)
    early = core_ref[0] == 0
    own_scale = jnp.where(early, jnp.exp(sibling_log), 1.0)
    sibling_scale = jnp.where(early, 1.0, jnp.exp(own_log))
    pair = own_ref[:STATE, :].astype(F32) * own_scale + sibling_ref[:STATE, :].astype(F32) * sibling_scale
    pair_ref[:STATE, :] = pair.astype(BF16)
    pair_ref[STATE:, :] = pieces(own_log + sibling_log, EXTRA)


def joined(stretches):
    total, log = stretches[0][:STATE, :].astype(F32), log_of(stretches[0])
    for ref in stretches[1:]:
        total = total + ref[:STATE, :].astype(F32) * jnp.exp(log)
        log = log + log_of(ref)
    return total, log


def join_kernel(*refs):
    total, log = joined(refs[:-1])
    refs[-1][:STATE, :] = total.astype(BF16)
    refs[-1][STATE:, :] = pieces(log, EXTRA)


def last_kernel(core_ref, own_ref, sibling_ref, *refs):
    keep_ref, send_ref = refs[-2:]
    chip = joined(refs[:-2])[0]
    for core, first, mine, other in ((0, own_ref, 0, 1), (1, sibling_ref, 1, 0)):

        @pl.when(core_ref[0] == core)
        def _():
            after = chip * jnp.exp(log_of(first)) + first[:STATE, :].astype(F32)
            both = (chip.astype(BF16), after.astype(BF16))
            keep_ref[...] = both[mine]
            send_ref[...] = both[other]


def widened(parts, spread):
    return lax.dot_general(parts, spread, (((0,), (0,)), ((), ())), preferred_element_type=F32)


def local_kernel(groups, x_hbm, gate_hbm, b_hbm, c_hbm, w_hbm, rhs_ref, inner_ref, outer_ref, skip_ref, mixed_ref, scale_ref,
                 w_ref, x_ref, gate_ref, b_ref, c_ref, semaphores):
    heads = skip_ref.shape[1]
    rows, channels = x_ref.shape
    width = channels // groups
    chunks = rows // CHUNK
    small = load([(b_hbm, b_ref), (c_hbm, c_ref)], semaphores)
    large = []
    for n in range(chunks):
        here = rows_of(n)
        pairs = [(x_hbm.at[here, :], x_ref.at[here, :]), (gate_hbm.at[here, :], gate_ref.at[here, :])]
        large.append(load(pairs, semaphores.at[pl.ds(2 + 2 * n, 2)]))
    size = channels // WEIGHT_COPIES
    weights = [(w_hbm.at[rows_of(n, size), :], w_ref.at[rows_of(n, size), :]) for n in range(WEIGHT_COPIES)]
    weights = load(weights, semaphores.at[pl.ds(2 + 2 * chunks, WEIGHT_COPIES)])

    spread = head_map(heads, channels)
    row = lax.broadcasted_iota(jnp.int32, (CHUNK, CHUNK), 0)
    column = lax.broadcasted_iota(jnp.int32, (CHUNK, CHUNK), 1)
    skip = jnp.sum(dot(pieces(skip_ref[...], EXTRA), spread[:heads, :]), axis=0, keepdims=True)
    for copy in small:
        copy.wait()
    for n in range(chunks):
        here = rows_of(n)
        for copy in large[n]:
            copy.wait()
        for g in range(groups):
            cut = slice(g * width, (g + 1) * width)
            part = slice(g * STATE, (g + 1) * STATE)
            to_wide = spread[:, cut]
            scores = lax.dot_general(
                c_ref[here, part], b_ref[here, part], (((1,), (1,)), ((), ())), preferred_element_type=F32
            )
            scores = jnp.where(row >= column, scores, 0.0).astype(BF16)
            within = dot(jnp.concatenate([scores, c_ref[here, part]], axis=1), rhs_ref[rows_of(n, CHUNK + STATE), cut])
            gate = gate_ref[here, cut].astype(F32)
            gate = gate / (1.0 + jnp.exp(-gate))
            passed = x_ref[here, cut].astype(F32) * skip[:, cut]
            mixed_ref[here, cut] = (within * widened(inner_ref[:, here], to_wide) + passed) * gate
            scale_ref[here, cut] = widened(outer_ref[:, here], to_wide) * gate
    for copy in weights:
        copy.wait()


def norm_rows(groups, state, mixed, scale, c_rows, gain):
    width = mixed.shape[1] // groups
    parts = []
    for g in range(groups):
        cut = slice(g * width, (g + 1) * width)
        carried = dot(c_rows[:, g * STATE : (g + 1) * STATE], state[:, cut])
        whole = mixed[:, cut] + scale[:, cut] * carried
        meansq = jnp.mean(whole * whole, axis=1, keepdims=True)
        parts.append((whole * lax.rsqrt(meansq + 1e-05) * gain[:, cut]).astype(BF16))
    return parts


def fill_state(core_ref, keep_ref, recv_ref, state):
    half = keep_ref.shape[1]
    for core in range(2):

        @pl.when(core_ref[0] == core)
        def _():
            state[:, core * half : (core + 1) * half] = keep_ref[...]
            state[:, (1 - core) * half : (2 - core) * half] = recv_ref[...]


def block_at(here, position, count, size):
    block = 0
    for i in range(count):
        block = jnp.where(here == i, block_order(i, count)[position], block)
    return pl.ds(pl.multiple_of(block * size, size), size)


def first_kernel(groups, count, core_ref, here_ref, mixed_ref, scale_ref, c_ref, keep_ref, recv_ref, gain_ref, w_ref, out_ref,
                 normed_ref, state):
    fill_state(core_ref, keep_ref, recv_ref, state)
    width = normed_ref.shape[1] // groups
    here = block_at(here_ref[0], 0, count, normed_ref.shape[0])
    rows = norm_rows(groups, state, mixed_ref.at[here, :], scale_ref.at[here, :], c_ref.at[here, :], gain_ref)
    for g, part in enumerate(rows):
        normed_ref[:, g * width : (g + 1) * width] = part

    @pl.loop(0, out_ref.shape[1] // COLUMN_TILE)
    def _(j):
        cut = pl.ds(pl.multiple_of(j * COLUMN_TILE, COLUMN_TILE), COLUMN_TILE)
        out_ref[:, cut] = dot(normed_ref[...], w_ref[:, cut]).astype(BF16)


def second_kernel(normed_ref, w_ref, out_ref):
    start = w_ref.shape[1] - out_ref.shape[1]

    @pl.loop(0, out_ref.shape[1] // COLUMN_TILE)
    def _(j):
        cut = pl.ds(pl.multiple_of(j * COLUMN_TILE, COLUMN_TILE), COLUMN_TILE)
        from_ = pl.ds(pl.multiple_of(start + j * COLUMN_TILE, COLUMN_TILE), COLUMN_TILE)
        out_ref[:, cut] = dot(normed_ref[...], w_ref[:, from_]).astype(BF16)


def rest_kernel(groups, count, core_ref, here_ref, mixed_ref, scale_ref, c_ref, keep_ref, recv_ref, gain_ref, w_ref, a_ref,
                b_ref, out_ref, state, normed):
    size, half = a_ref.shape
    blocks = [block_at(here_ref[0], n, count, size) for n in range(count)]
    out_ref[blocks[0], :half] = a_ref[...]
    out_ref[blocks[0], half:] = b_ref[...]
    fill_state(core_ref, keep_ref, recv_ref, state)
    width = normed.shape[1] // groups
    for n in range(1, count):
        here = blocks[n]
        rows = norm_rows(groups, state, mixed_ref.at[here, :], scale_ref.at[here, :], c_ref.at[here, :], gain_ref)
        for g, part in enumerate(rows):
            normed[(n - 1) * size : n * size, g * width : (g + 1) * width] = part

    @pl.loop(0, out_ref.shape[1] // COLUMN_TILE)
    def _(j):
        cut = pl.ds(pl.multiple_of(j * COLUMN_TILE, COLUMN_TILE), COLUMN_TILE)
        product = dot(normed[...], w_ref[:, cut]).astype(BF16)
        for n in range(1, count):
            out_ref[blocks[n], cut] = product[(n - 1) * size : n * size]


def pass_kernel(count, step, column, here_ref, right_ref, left_ref, sums_ref, to_right_ref, to_left_ref):
    size, width = right_ref.shape
    for shift, came, out in ((count - step, right_ref, to_right_ref), (step - count, left_ref, to_left_ref)):
        block = jnp.clip(here_ref[0] + shift, 0, count - 1)
        rows = pl.ds(pl.multiple_of(block * size, size), size)
        own = sums_ref[rows, column : column + width].astype(F32)
        out[...] = (own + came[...].astype(F32)).astype(BF16)


def sum_kernel(column, here_ref, right_ref, left_ref, sums_ref, out_ref):
    size, width = right_ref.shape
    rows = pl.ds(pl.multiple_of(here_ref[0] * size, size), size)
    own = sums_ref[rows, column : column + width].astype(F32)
    out_ref[...] = (own + right_ref[...].astype(F32) + left_ref[...].astype(F32)).astype(BF16)


def block_order(here, count):
    order = []
    for step in range(1, count):
        for block, sends in ((count - step + here, here <= step - 1), (step - count + here, here >= count - step)):
            if sends and block not in order:
                order.append(block)
    return order + [b for b in range(count) if b not in order]


def in_vmem(kernel, name, ins, outs, scratch=(), vmem=8, flops=1):
    vm = pl.BlockSpec(memory_space=pltpu.VMEM)
    specs, arrays = [], []
    for v in ins:
        if isinstance(v, tuple):
            specs.append(pl.BlockSpec(memory_space=pltpu.HBM))
            arrays.append(pltpu.with_memory_space_constraint(v[0], pltpu.HBM))
        elif v.dtype == jnp.int32:
            specs.append(pl.BlockSpec(memory_space=pltpu.SMEM))
            arrays.append(v)
        else:
            specs.append(vm)
            arrays.append(pltpu.with_memory_space_constraint(v, pltpu.VMEM))
    return pl.pallas_call(
        kernel,
        in_specs=specs,
        out_specs=[vm for _ in outs],
        out_shape=[pltpu.VMEM(shape, kind) for shape, kind in outs],
        scratch_shapes=list(scratch),
        compiler_params=pltpu.CompilerParams(vmem_limit_bytes=vmem * 2**20),
        cost_estimate=pl.CostEstimate(flops=flops, bytes_accessed=1, transcendentals=0),
        name=name,
    )(*arrays)


def line_reduce(first, partial_sums, here, size, columns):
    count = lax.axis_size("tp")
    width = columns // HALVES
    block = ((size, width), BF16)
    right = [None] * HALVES
    left = [None] * HALVES
    for step in range(1, count):
        to_right = [(i, i + 1) for i in range(step)]
        to_left = [(i, i - 1) for i in range(count - step, count)]
        for half in range(HALVES):
            if step == 1:
                right[half] = left[half] = lax.ppermute(first[half], "tp", to_right + to_left)
                continue
            ins = (here, right[half], left[half], partial_sums)
            send_right, send_left = in_vmem(partial(pass_kernel, count, step, half * width), "pass_on", ins, (block, block))
            right[half] = lax.ppermute(send_right, "tp", to_right)
            left[half] = lax.ppermute(send_left, "tp", to_left)
    done = []
    for half in range(HALVES):
        ins = (here, right[half], left[half], partial_sums)
        done.extend(in_vmem(partial(sum_kernel, half * width), "sum_up", ins, (block,)))
    return jnp.concatenate(done, axis=1)


def on_device(x_in, gate_z, b_in, c_in, step_size, log_decay, skip, norm_gain, out_weight):
    rows, channels = x_in.shape
    heads = step_size.shape[1]
    groups = b_in.shape[1] // STATE
    chunks = rows // CHUNK
    columns = out_weight.shape[1]
    half = channels // 2
    devices = lax.axis_size("ctx")
    chips = devices // 2
    count = lax.axis_size("tp")
    size = rows // count
    core = lax.rem(lax.axis_index("ctx"), 2).astype(jnp.int32).reshape(1)
    here = lax.axis_index("tp").astype(jnp.int32).reshape(1)
    message = ((STATE + EXTRA, half), BF16)
    by_head = ((2 * heads, rows), BF16)
    whole = ((rows, channels), F32)

    rhs, inner, outer, send, own = in_vmem(
        partial(state_kernel, groups),
        "chunk_states",
        (core, (x_in,), (b_in,), (step_size.T,), (log_decay.T,)),
        (((chunks * (CHUNK + STATE), channels), BF16), by_head, by_head, message, message),
        scratch=[
            pltpu.VMEM((rows, channels), BF16),
            pltpu.VMEM((rows, groups * STATE), BF16),
            pltpu.VMEM((heads, rows), F32),
            pltpu.VMEM((heads, rows), F32),
            pltpu.SemaphoreType.DMA((3 + chunks,)),
        ],
        vmem=20,
    )

    swap = [(i, i ^ 1) for i in range(devices)]
    sibling = lax.ppermute(send, "ctx", swap)
    (pair,) = in_vmem(pair_kernel, "pair", (core, own, sibling), (message,))
    x_late, pair = lax.optimization_barrier((x_in, pair))
    incoming, outgoing, distance = [], pair, 1
    while distance < chips:
        if incoming:
            (outgoing,) = in_vmem(join_kernel, "join", (pair, *incoming), (message,))
        for far in range(distance, min(chips, 4 * distance), distance):
            incoming.append(lax.ppermute(outgoing, "ctx", [(i, i + 2 * far) for i in range(devices - 2 * far)]))
        distance *= 4
    mixed, scale, weight = in_vmem(
        partial(local_kernel, groups),
        "local_part",
        ((x_late,), (gate_z,), (b_in,), (c_in,), (out_weight,), rhs, inner, outer, skip.reshape(1, heads)),
        (whole, whole, (out_weight.shape, BF16)),
        scratch=[
            pltpu.VMEM((rows, channels), BF16),
            pltpu.VMEM((rows, channels), BF16),
            pltpu.VMEM((rows, groups * STATE), BF16),
            pltpu.VMEM((rows, groups * STATE), BF16),
            pltpu.SemaphoreType.DMA((2 + 2 * chunks + WEIGHT_COPIES,)),
        ],
        vmem=20,
        flops=8 * 10**9,
    )
    mixed, scale, weight, *incoming = lax.optimization_barrier((mixed, scale, weight, *incoming))
    state = ((STATE, half), BF16)
    keep, send = in_vmem(last_kernel, "incoming", (core, own, sibling, *incoming), (state, state))
    recv = lax.ppermute(send, "ctx", swap)

    first = ((size, columns // 2), BF16)
    gain = norm_gain.reshape(1, channels)
    inputs = (core, here, mixed, scale, c_in, keep, recv, gain, weight)
    whole_state = pltpu.VMEM((STATE, channels), BF16)
    first_a, normed = in_vmem(
        partial(first_kernel, groups, count), "first_block", inputs, (first, ((size, channels), BF16)), [whole_state]
    )
    (first_b,) = in_vmem(second_kernel, "first_block_rest", (normed, weight), (first,))
    (partial_sums,) = in_vmem(
        partial(rest_kernel, groups, count),
        "other_blocks",
        (*inputs, first_a, first_b),
        (((rows, columns), BF16),),
        [whole_state, pltpu.VMEM((rows - size, channels), BF16)],
        vmem=16,
    )
    return line_reduce((first_a, first_b), partial_sums, here, size, columns)


def solution(mesh):
    placed = (
        P("ctx", "tp"),
        P("ctx", "tp"),
        P("ctx", "tp"),
        P("ctx", "tp"),
        P("ctx", "tp"),
        P("ctx", "tp"),
        P("tp"),
        P("tp"),
        P("tp", None),
    )
    return jax.shard_map(
        on_device, mesh=mesh, in_specs=placed, out_specs=P(("ctx", "tp"), None), check_vma=False
    )
```

```python
from functools import partial

import jax
import jax.numpy as jnp
from jax import lax
from jax.experimental import pallas as pl
from jax.experimental.pallas import tpu as pltpu
from jax.sharding import PartitionSpec as P

HEAD_DIM = 64
STATE = 128
CHUNK = 128
MIDDLE = CHUNK // 2 - 1
EXTRA = 16
COLUMN_TILE = 512
HALVES = 2
WEIGHT_COPIES = 8
F32 = jnp.float32
BF16 = jnp.bfloat16


def dot(a, b):
    return jnp.dot(a, b, preferred_element_type=F32)


def dot_exact(a, b):
    return jnp.dot(a, b, preferred_element_type=F32, precision=lax.Precision.HIGHEST)


def head_map(heads, channels):
    head = lax.broadcasted_iota(jnp.int32, (2 * heads, channels), 0) & (heads - 1)
    place = lax.broadcasted_iota(jnp.int32, (2 * heads, channels), 1) >> 6
    return jnp.where(head == place, 1.0, 0.0).astype(BF16)


def high_low(values):
    high = values.astype(BF16).astype(F32)
    return jnp.concatenate([high, values - high], axis=0)


def pieces(values, rows):
    first = values.astype(BF16).astype(F32)
    second = (values - first).astype(BF16).astype(F32)
    third = values - first - second
    row = lax.broadcasted_iota(jnp.int32, (rows, values.shape[1]), 0)
    stacked = jnp.where(row == 0, first, jnp.where(row == 1, second, jnp.where(row == 2, third, 0.0)))
    return stacked.astype(BF16)


def load(pairs, semaphores):
    copies = [pltpu.make_async_copy(src, dst, semaphores.at[n]) for n, (src, dst) in enumerate(pairs)]
    for copy in copies:
        copy.start()
    return copies


def rows_of(chunk, size=CHUNK):
    return slice(chunk * size, (chunk + 1) * size)


def state_kernel(groups, core_ref, here_ref, x_hbm, b_hbm, step_hbm, decay_hbm, rhs_ref, inner_ref, outer_ref, send_ref, keep_ref,
                 x_ref, b_ref, step_ref, decay_ref, semaphores):
    rows, channels = x_ref.shape
    heads = step_ref.shape[0]
    width = channels // groups
    chunks = rows // CHUNK
    small = load([(decay_hbm, decay_ref), (step_hbm, step_ref), (b_hbm, b_ref)], semaphores)
    large = load(
        [(x_hbm.at[rows_of(n), :], x_ref.at[rows_of(n), :]) for n in range(chunks)], semaphores.at[pl.ds(3, chunks)]
    )
    spread = head_map(heads, channels)
    row = lax.broadcasted_iota(jnp.int32, (CHUNK, CHUNK), 0)
    column = lax.broadcasted_iota(jnp.int32, (CHUNK, CHUNK), 1)
    upper = jnp.where(row <= column, 1.0, 0.0)
    lane = lax.broadcasted_iota(jnp.int32, (heads, CHUNK), 1)
    before = jnp.zeros((heads, 1), F32)
    state = [jnp.zeros((STATE, width), F32)] * groups
    for copy in small:
        copy.wait()
    for n in range(chunks):
        here = rows_of(n)
        running = dot_exact(decay_ref[:, here], upper)
        middle, total = running[:, MIDDLE : MIDDLE + 1], running[:, CHUNK - 1 :]
        inner = running - middle
        inner_ref[:, here] = high_low(jnp.exp(inner)).astype(BF16)
        outer_ref[:, here] = high_low(jnp.exp(before + running)).astype(BF16)
        weight = step_ref[:, here] * jnp.exp(-inner)
        factors = jnp.exp(jnp.where(lane == 0, total, jnp.where(lane == 1, total - middle, middle)))
        stacked = jnp.concatenate([jnp.transpose(high_low(weight)), jnp.transpose(high_low(factors))[:EXTRA]], axis=0)
        stacked = stacked.astype(BF16)
        before = before + total
        large[n].wait()
        to_rhs = n * (CHUNK + STATE)
        for g in range(groups):
            cut = slice(g * width, (g + 1) * width)
            wide = dot(stacked, spread[:, cut])
            weighted = (x_ref[here, cut].astype(F32) * wide[:CHUNK]).astype(BF16)
            rhs_ref[to_rhs : to_rhs + CHUNK, cut] = weighted
            rhs_ref[to_rhs + CHUNK : to_rhs + CHUNK + STATE, cut] = (state[g] * wide[CHUNK + 2 : CHUNK + 3]).astype(BF16)
            fresh = lax.dot_general(
                b_ref[here, g * STATE : (g + 1) * STATE],
                weighted,
                (((0,), (0,)), ((), ())),
                preferred_element_type=F32,
            )
            state[g] = state[g] * wide[CHUNK : CHUNK + 1] + fresh * wide[CHUNK + 1 : CHUNK + 2]

    first = before.astype(BF16).astype(F32)
    second = (before - first).astype(BF16).astype(F32)
    third = before - first - second
    stacked = jnp.where(lane == 0, first, jnp.where(lane == 1, second, jnp.where(lane == 2, third, 0.0)))
    logs = dot(jnp.transpose(stacked)[:EXTRA].astype(BF16), spread[:heads, :]).astype(BF16)
    end = jnp.concatenate([part.astype(BF16) for part in state], axis=1)
    half = channels // 2
    for core in range(2):

        @pl.when(core_ref[0] == core)
        def _():
            own = slice(core * half, (core + 1) * half)
            other = slice((1 - core) * half, (2 - core) * half)
            keep_ref[:STATE, :] = end[:, own]
            keep_ref[STATE:, :] = logs[:, own]
            send_ref[:STATE, :] = end[:, other]
            send_ref[STATE:, :] = logs[:, other]


def log_of(ref):
    return jnp.sum(ref[STATE:, :].astype(F32), axis=0, keepdims=True)


def pair_kernel(core_ref, own_ref, sibling_ref, pair_ref):
    own_log, sibling_log = log_of(own_ref), log_of(sibling_ref)
    early = core_ref[0] == 0
    own_scale = jnp.where(early, jnp.exp(sibling_log), 1.0)
    sibling_scale = jnp.where(early, 1.0, jnp.exp(own_log))
    pair = own_ref[:STATE, :].astype(F32) * own_scale + sibling_ref[:STATE, :].astype(F32) * sibling_scale
    pair_ref[:STATE, :] = pair.astype(BF16)
    pair_ref[STATE:, :] = pieces(own_log + sibling_log, EXTRA)


def joined(stretches):
    total, log = stretches[0][:STATE, :].astype(F32), log_of(stretches[0])
    for ref in stretches[1:]:
        total = total + ref[:STATE, :].astype(F32) * jnp.exp(log)
        log = log + log_of(ref)
    return total, log


def join_kernel(*refs):
    total, log = joined(refs[:-1])
    refs[-1][:STATE, :] = total.astype(BF16)
    refs[-1][STATE:, :] = pieces(log, EXTRA)


def last_kernel(core_ref, own_ref, sibling_ref, after_ref, *refs):
    keep_ref, send_ref = refs[-2:]
    chip = joined(refs[:-2])[0]
    for core, first, mine, other in ((0, own_ref, 0, 1), (1, sibling_ref, 1, 0)):

        @pl.when(core_ref[0] == core)
        def _():
            after = chip * jnp.exp(log_of(first)) + first[:STATE, :].astype(F32)
            both = (chip.astype(BF16), after.astype(BF16))
            keep_ref[...] = both[mine]
            send_ref[...] = both[other]


def widened(parts, spread):
    return lax.dot_general(parts, spread, (((0,), (0,)), ((), ())), preferred_element_type=F32)


def local_kernel(groups, x_hbm, gate_hbm, b_hbm, c_hbm, w_hbm, rhs_ref, inner_ref, outer_ref, skip_ref, after_ref, mixed_ref,
                 scale_ref, w_ref, token_ref, x_ref, gate_ref, b_ref, c_ref, semaphores):
    token_ref[...] = jnp.zeros_like(token_ref)
    heads = skip_ref.shape[1]
    rows, channels = x_ref.shape
    width = channels // groups
    chunks = rows // CHUNK
    small = load([(b_hbm, b_ref), (c_hbm, c_ref)], semaphores)
    large = []
    for n in range(chunks):
        here = rows_of(n)
        pairs = [(x_hbm.at[here, :], x_ref.at[here, :]), (gate_hbm.at[here, :], gate_ref.at[here, :])]
        large.append(load(pairs, semaphores.at[pl.ds(2 + 2 * n, 2)]))
    size = channels // WEIGHT_COPIES
    weights = [(w_hbm.at[rows_of(n, size), :], w_ref.at[rows_of(n, size), :]) for n in range(WEIGHT_COPIES)]
    weights = load(weights, semaphores.at[pl.ds(2 + 2 * chunks, WEIGHT_COPIES)])

    spread = head_map(heads, channels)
    row = lax.broadcasted_iota(jnp.int32, (CHUNK, CHUNK), 0)
    column = lax.broadcasted_iota(jnp.int32, (CHUNK, CHUNK), 1)
    skip = jnp.sum(dot(pieces(skip_ref[...], EXTRA), spread[:heads, :]), axis=0, keepdims=True)
    for copy in small:
        copy.wait()
    for n in range(chunks):
        here = rows_of(n)
        for copy in large[n]:
            copy.wait()
        for g in range(groups):
            cut = slice(g * width, (g + 1) * width)
            part = slice(g * STATE, (g + 1) * STATE)
            to_wide = spread[:, cut]
            scores = lax.dot_general(
                c_ref[here, part], b_ref[here, part], (((1,), (1,)), ((), ())), preferred_element_type=F32
            )
            scores = jnp.where(row >= column, scores, 0.0).astype(BF16)
            within = dot(jnp.concatenate([scores, c_ref[here, part]], axis=1), rhs_ref[rows_of(n, CHUNK + STATE), cut])
            gate = gate_ref[here, cut].astype(F32)
            gate = gate / (1.0 + jnp.exp(-gate))
            passed = x_ref[here, cut].astype(F32) * skip[:, cut]
            mixed_ref[here, cut] = (within * widened(inner_ref[:, here], to_wide) + passed) * gate
            scale_ref[here, cut] = widened(outer_ref[:, here], to_wide) * gate
    for copy in weights:
        copy.wait()


def norm_rows(groups, state, mixed, scale, c_rows, gain):
    width = mixed.shape[1] // groups
    parts = []
    for g in range(groups):
        cut = slice(g * width, (g + 1) * width)
        carried = dot(c_rows[:, g * STATE : (g + 1) * STATE], state[:, cut])
        whole = mixed[:, cut] + scale[:, cut] * carried
        meansq = jnp.mean(whole * whole, axis=1, keepdims=True)
        parts.append((whole * lax.rsqrt(meansq + 1e-05) * gain[:, cut]).astype(BF16))
    return parts


def fill_state(core_ref, keep_ref, recv_ref, state):
    half = keep_ref.shape[1]
    for core in range(2):

        @pl.when(core_ref[0] == core)
        def _():
            state[:, core * half : (core + 1) * half] = keep_ref[...]
            state[:, (1 - core) * half : (2 - core) * half] = recv_ref[...]


def block_at(here, position, count, size):
    block = 0
    for i in range(count):
        block = jnp.where(here == i, block_order(i, count)[position], block)
    return pl.ds(pl.multiple_of(block * size, size), size)


def first_kernel(groups, count, core_ref, here_ref, mixed_ref, scale_ref, c_ref, keep_ref, recv_ref, gain_ref, w_ref, out_ref,
                 normed_ref, state):
    fill_state(core_ref, keep_ref, recv_ref, state)
    width = normed_ref.shape[1] // groups
    here = block_at(here_ref[0], 0, count, normed_ref.shape[0])
    rows = norm_rows(groups, state, mixed_ref.at[here, :], scale_ref.at[here, :], c_ref.at[here, :], gain_ref)
    for g, part in enumerate(rows):
        normed_ref[:, g * width : (g + 1) * width] = part

    @pl.loop(0, out_ref.shape[1] // COLUMN_TILE)
    def _(j):
        cut = pl.ds(pl.multiple_of(j * COLUMN_TILE, COLUMN_TILE), COLUMN_TILE)
        out_ref[:, cut] = dot(normed_ref[...], w_ref[:, cut]).astype(BF16)


def second_kernel(normed_ref, w_ref, out_ref):
    start = w_ref.shape[1] - out_ref.shape[1]

    @pl.loop(0, out_ref.shape[1] // COLUMN_TILE)
    def _(j):
        cut = pl.ds(pl.multiple_of(j * COLUMN_TILE, COLUMN_TILE), COLUMN_TILE)
        from_ = pl.ds(pl.multiple_of(start + j * COLUMN_TILE, COLUMN_TILE), COLUMN_TILE)
        out_ref[:, cut] = dot(normed_ref[...], w_ref[:, from_]).astype(BF16)


def rest_kernel(groups, count, core_ref, here_ref, mixed_ref, scale_ref, c_ref, keep_ref, recv_ref, gain_ref, w_ref, a_ref,
                b_ref, out_ref, state, normed):
    size, half = a_ref.shape
    blocks = [block_at(here_ref[0], n, count, size) for n in range(count)]
    out_ref[blocks[0], :half] = a_ref[...]
    out_ref[blocks[0], half:] = b_ref[...]
    fill_state(core_ref, keep_ref, recv_ref, state)
    width = normed.shape[1] // groups
    for n in range(1, count):
        here = blocks[n]
        rows = norm_rows(groups, state, mixed_ref.at[here, :], scale_ref.at[here, :], c_ref.at[here, :], gain_ref)
        for g, part in enumerate(rows):
            normed[(n - 1) * size : n * size, g * width : (g + 1) * width] = part

    @pl.loop(0, out_ref.shape[1] // COLUMN_TILE)
    def _(j):
        cut = pl.ds(pl.multiple_of(j * COLUMN_TILE, COLUMN_TILE), COLUMN_TILE)
        product = dot(normed[...], w_ref[:, cut]).astype(BF16)
        for n in range(1, count):
            out_ref[blocks[n], cut] = product[(n - 1) * size : n * size]


def pass_kernel(count, step, column, here_ref, right_ref, left_ref, sums_ref, to_right_ref, to_left_ref):
    size, width = right_ref.shape
    for shift, came, out in ((count - step, right_ref, to_right_ref), (step - count, left_ref, to_left_ref)):
        block = jnp.clip(here_ref[0] + shift, 0, count - 1)
        rows = pl.ds(pl.multiple_of(block * size, size), size)
        own = sums_ref[rows, column : column + width].astype(F32)
        out[...] = (own + came[...].astype(F32)).astype(BF16)


def sum_kernel(column, here_ref, right_ref, left_ref, sums_ref, out_ref):
    size, width = right_ref.shape
    rows = pl.ds(pl.multiple_of(here_ref[0] * size, size), size)
    own = sums_ref[rows, column : column + width].astype(F32)
    out_ref[...] = (own + right_ref[...].astype(F32) + left_ref[...].astype(F32)).astype(BF16)


def block_order(here, count):
    order = []
    for step in range(1, count):
        for block, sends in ((count - step + here, here <= step - 1), (step - count + here, here >= count - step)):
            if sends and block not in order:
                order.append(block)
    return order + [b for b in range(count) if b not in order]


def in_vmem(kernel, name, ins, outs, scratch=(), vmem=4, flops=1):
    vm = pl.BlockSpec(memory_space=pltpu.VMEM)
    specs, arrays = [], []
    for v in ins:
        if isinstance(v, tuple):
            specs.append(pl.BlockSpec(memory_space=pltpu.HBM))
            arrays.append(pltpu.with_memory_space_constraint(v[0], pltpu.HBM))
        elif v.dtype == jnp.int32:
            specs.append(pl.BlockSpec(memory_space=pltpu.SMEM))
            arrays.append(v)
        else:
            specs.append(vm)
            arrays.append(pltpu.with_memory_space_constraint(v, pltpu.VMEM))
    return pl.pallas_call(
        kernel,
        in_specs=specs,
        out_specs=[vm for _ in outs],
        out_shape=[pltpu.VMEM(shape, kind) for shape, kind in outs],
        scratch_shapes=list(scratch),
        compiler_params=pltpu.CompilerParams(vmem_limit_bytes=vmem * 2**20),
        cost_estimate=pl.CostEstimate(flops=flops, bytes_accessed=1, transcendentals=0),
        name=name,
    )(*arrays)


def line_reduce(first, partial_sums, here, size, columns):
    count = lax.axis_size("tp")
    width = columns // HALVES
    block = ((size, width), BF16)
    right = [None] * HALVES
    left = [None] * HALVES
    for step in range(1, count):
        to_right = [(i, i + 1) for i in range(step)]
        to_left = [(i, i - 1) for i in range(count - step, count)]
        for half in range(HALVES):
            if step == 1:
                right[half] = left[half] = lax.ppermute(first[half], "tp", to_right + to_left)
                continue
            ins = (here, right[half], left[half], partial_sums)
            send_right, send_left = in_vmem(partial(pass_kernel, count, step, half * width), "pass_on", ins, (block, block))
            right[half] = lax.ppermute(send_right, "tp", to_right)
            left[half] = lax.ppermute(send_left, "tp", to_left)
    done = []
    for half in range(HALVES):
        ins = (here, right[half], left[half], partial_sums)
        done.extend(in_vmem(partial(sum_kernel, half * width), "sum_up", ins, (block,)))
    return jnp.concatenate(done, axis=1)


def on_device(x_in, gate_z, b_in, c_in, step_size, log_decay, skip, norm_gain, out_weight):
    rows, channels = x_in.shape
    heads = step_size.shape[1]
    groups = b_in.shape[1] // STATE
    chunks = rows // CHUNK
    columns = out_weight.shape[1]
    half = channels // 2
    devices = lax.axis_size("ctx")
    chips = devices // 2
    count = lax.axis_size("tp")
    size = rows // count
    core = lax.rem(lax.axis_index("ctx"), 2).astype(jnp.int32).reshape(1)
    here = lax.axis_index("tp").astype(jnp.int32).reshape(1)
    message = ((STATE + EXTRA, half), BF16)
    by_head = ((2 * heads, rows), BF16)
    whole = ((rows, channels), F32)

    rhs, inner, outer, send, own = in_vmem(
        partial(state_kernel, groups),
        "chunk_states",
        (core, here, (x_in,), (b_in,), (step_size.T,), (log_decay.T,)),
        (((chunks * (CHUNK + STATE), channels), BF16), by_head, by_head, message, message),
        scratch=[
            pltpu.VMEM((rows, channels), BF16),
            pltpu.VMEM((rows, groups * STATE), BF16),
            pltpu.VMEM((heads, rows), F32),
            pltpu.VMEM((heads, rows), F32),
            pltpu.SemaphoreType.DMA((3 + chunks,)),
        ],
        vmem=8,
    )

    swap = [(i, i ^ 1) for i in range(devices)]
    sibling = lax.ppermute(send, "ctx", swap)
    (pair,) = in_vmem(pair_kernel, "pair", (core, own, sibling), (message,))
    incoming, outgoing, distance = [], pair, 1
    while distance < chips:
        if incoming:
            (outgoing,) = in_vmem(join_kernel, "join", (pair, *incoming), (message,))
        for far in range(distance, min(chips, 4 * distance), distance):
            incoming.append(lax.ppermute(outgoing, "ctx", [(i, i + 2 * far) for i in range(devices - 2 * far)]))
        distance *= 4
    mixed, scale, weight, token = in_vmem(
        partial(local_kernel, groups),
        "local_part",
        ((x_in,), (gate_z,), (b_in,), (c_in,), (out_weight,), rhs, inner, outer, skip.reshape(1, heads), pair),
        (whole, whole, (out_weight.shape, BF16), ((EXTRA, STATE), BF16)),
        scratch=[
            pltpu.VMEM((rows, channels), BF16),
            pltpu.VMEM((rows, channels), BF16),
            pltpu.VMEM((rows, groups * STATE), BF16),
            pltpu.VMEM((rows, groups * STATE), BF16),
            pltpu.SemaphoreType.DMA((2 + 2 * chunks + WEIGHT_COPIES,)),
        ],
        vmem=10,
        flops=8 * 10**9,
    )
    state = ((STATE, half), BF16)
    keep, send = in_vmem(last_kernel, "incoming", (core, own, sibling, token, *incoming), (state, state))
    recv = lax.ppermute(send, "ctx", swap)

    first = ((size, columns // 2), BF16)
    gain = norm_gain.reshape(1, channels)
    inputs = (core, here, mixed, scale, c_in, keep, recv, gain, weight)
    whole_state = pltpu.VMEM((STATE, channels), BF16)
    first_a, normed = in_vmem(
        partial(first_kernel, groups, count), "first_block", inputs, (first, ((size, channels), BF16)), [whole_state]
    )
    (first_b,) = in_vmem(second_kernel, "first_block_rest", (normed, weight), (first,))
    (partial_sums,) = in_vmem(
        partial(rest_kernel, groups, count),
        "other_blocks",
        (*inputs, first_a, first_b),
        (((rows, columns), BF16),),
        [whole_state, pltpu.VMEM((rows - size, channels), BF16)],
        vmem=6,
    )
    return line_reduce((first_a, first_b), partial_sums, here, size, columns)


def solution(mesh):
    placed = (
        P("ctx", "tp"),
        P("ctx", "tp"),
        P("ctx", "tp"),
        P("ctx", "tp"),
        P("ctx", "tp"),
        P("ctx", "tp"),
        P("tp"),
        P("tp"),
        P("tp", None),
    )
    return jax.shard_map(
        on_device, mesh=mesh, in_specs=placed, out_specs=P(("ctx", "tp"), None), check_vma=False
    )
```

```python
from functools import partial

import jax
import jax.numpy as jnp
from jax import lax
from jax.experimental import pallas as pl
from jax.experimental.pallas import tpu as pltpu
from jax.sharding import PartitionSpec as P

HEAD_DIM = 64
STATE = 128
CHUNK = 128
MIDDLE = CHUNK // 2 - 1
EXTRA = 16
COLUMN_TILE = 512
HALVES = 2
WEIGHT_COPIES = 8
SUM_COPIES = 4
F32 = jnp.float32
BF16 = jnp.bfloat16


def dot(a, b):
    return jnp.dot(a, b, preferred_element_type=F32)


def dot_exact(a, b):
    return jnp.dot(a, b, preferred_element_type=F32, precision=lax.Precision.HIGHEST)


def head_map(channels):
    head = lax.broadcasted_iota(jnp.int32, (128, channels), 0) & 63
    place = lax.broadcasted_iota(jnp.int32, (128, channels), 1) >> 6
    return jnp.where(head == place, 1.0, 0.0).astype(BF16)


def padded(values):
    return jnp.concatenate([values, jnp.zeros((64 - values.shape[0], values.shape[1]), F32)], axis=0)


def by_row(values):
    high = values.astype(BF16).astype(F32)
    return jnp.transpose(jnp.concatenate([padded(high), padded(values - high)], axis=0)).astype(BF16)


def pieces(values, axis):
    first = values.astype(BF16).astype(F32)
    second = (values - first).astype(BF16).astype(F32)
    third = values - first - second
    shape = (EXTRA, values.shape[1]) if axis == 0 else (values.shape[0], 128)
    at = lax.broadcasted_iota(jnp.int32, shape, axis)
    return jnp.where(at == 0, first, jnp.where(at == 1, second, jnp.where(at == 2, third, 0.0)))


def running_sums(decay):
    row = lax.broadcasted_iota(jnp.int32, (CHUNK, CHUNK), 0)
    column = lax.broadcasted_iota(jnp.int32, (CHUNK, CHUNK), 1)
    upper = jnp.where(row <= column, 1.0, 0.0)
    return [dot_exact(decay[:, rows_of(n)], upper) for n in range(decay.shape[1] // CHUNK)]


def load(pairs, semaphores):
    copies = [pltpu.make_async_copy(src, dst, semaphores.at[n]) for n, (src, dst) in enumerate(pairs)]
    for copy in copies:
        copy.start()
    return copies


def rows_of(chunk, size=CHUNK):
    return slice(chunk * size, (chunk + 1) * size)


def put_message(ref, state, logs):
    for j in range(state.shape[1] // 128):
        ref[j * STATE : (j + 1) * STATE, :] = state[:, j * 128 : (j + 1) * 128].astype(BF16)
    ref[state.shape[1] :, :] = logs.astype(BF16)


def state_of(ref):
    count = (ref.shape[0] - EXTRA) // STATE
    return jnp.concatenate([ref[j * STATE : (j + 1) * STATE, :] for j in range(count)], axis=1).astype(F32)


def logs_of(ref):
    return ref[ref.shape[0] - EXTRA :, :]


def wide_log(logs, spread):
    return jnp.sum(dot(logs, spread), axis=0, keepdims=True)


def end_state(groups, half, x_ref, b_ref, step_ref, decay_ref, weighted, message_ref, spread):
    rows, width = weighted.shape
    heads = width // HEAD_DIM
    of_heads = pl.ds(pl.multiple_of(half * heads, heads), heads)
    of_channels = pl.ds(pl.multiple_of(half * width, width), width)
    of_group = pl.ds(pl.multiple_of((half * groups // 2) * STATE, STATE), STATE)
    before, running = jnp.zeros((heads, 1), F32), []
    for sums in running_sums(decay_ref[of_heads, :]):
        running.append(before + sums)
        before = before + sums[:, CHUNK - 1 :]
    for n, sums in enumerate(running):
        here = rows_of(n)
        factor = dot(by_row(step_ref[of_heads, here] * jnp.exp(before - sums)), spread)
        weighted[here, :] = (x_ref[here, of_channels].astype(F32) * factor).astype(BF16)
    state = lax.dot_general(
        b_ref[:, of_group], weighted[...], (((0,), (0,)), ((), ())), preferred_element_type=F32
    )
    logs = jnp.concatenate([pieces(before, 1), jnp.zeros((128 - heads, 128), F32)], axis=0)
    put_message(message_ref, state, jnp.transpose(logs)[:EXTRA])


def send_kernel(groups, core_ref, here_ref, x_hbm, b_hbm, step_hbm, decay_hbm, send_ref, x_ref, b_ref, step_ref, decay_ref,
                spread_ref, weighted, semaphores):
    width = weighted.shape[1]
    other = 1 - core_ref[0]
    of_channels = [pl.ds(pl.multiple_of(half * width, width), width) for half in (other, core_ref[0])]
    copies = load(
        [(decay_hbm, decay_ref), (step_hbm, step_ref), (b_hbm, b_ref)]
        + [(x_hbm.at[:, cut], x_ref.at[:, cut]) for cut in of_channels],
        semaphores,
    )
    spread = head_map(width)
    spread_ref[...] = spread
    for copy in copies[:4]:
        copy.wait()
    end_state(groups, other, x_ref, b_ref, step_ref, decay_ref, weighted, send_ref, spread)
    copies[4].wait()


def keep_kernel(groups, core_ref, x_ref, b_ref, step_ref, decay_ref, spread_ref, keep_ref, weighted):
    end_state(groups, core_ref[0], x_ref, b_ref, step_ref, decay_ref, weighted, keep_ref, spread_ref[...])


def pair_kernel(core_ref, spread_ref, own_ref, sibling_ref, pair_ref):
    spread = spread_ref[...]
    own_log, sibling_log = wide_log(logs_of(own_ref), spread), wide_log(logs_of(sibling_ref), spread)
    early = core_ref[0] == 0
    own_scale = jnp.where(early, jnp.exp(sibling_log), 1.0)
    sibling_scale = jnp.where(early, 1.0, jnp.exp(own_log))
    logs = logs_of(own_ref).astype(F32) + logs_of(sibling_ref).astype(F32)
    logs = pieces(jnp.sum(logs, axis=0, keepdims=True), 0)
    put_message(pair_ref, state_of(own_ref) * own_scale + state_of(sibling_ref) * sibling_scale, logs)


def joined(stretches, spread):
    total, log = state_of(stretches[0]), 0.0
    for late, early in zip(stretches, stretches[1:]):
        log = log + wide_log(logs_of(late), spread)
        total = total + state_of(early) * jnp.exp(log)
    return total


def join_kernel(spread_ref, *refs):
    logs = sum(jnp.sum(logs_of(ref).astype(F32), axis=0, keepdims=True) for ref in refs[:-1])
    put_message(refs[-1], joined(refs[:-1], spread_ref[...]), pieces(logs, 0))


def last_kernel(core_ref, after_ref, spread_ref, own_ref, sibling_ref, *refs):
    keep_ref, send_ref = refs[-2:]
    spread = spread_ref[...]
    chip = joined(refs[:-2], spread)
    for core, first, mine, other in ((0, own_ref, 0, 1), (1, sibling_ref, 1, 0)):

        @pl.when(core_ref[0] == core)
        def _():
            after = chip * jnp.exp(wide_log(logs_of(first), spread)) + state_of(first)
            both = (chip.astype(BF16), after.astype(BF16))
            keep_ref[...] = both[mine]
            send_ref[...] = both[other]


def local_kernel(groups, gate_hbm, c_hbm, w_hbm, x_ref, b_ref, step_ref, decay_ref, skip_ref, after_ref, mixed_ref, scale_ref,
                 w_ref, c_ref, token_ref, gate_ref, semaphores):
    token_ref[...] = jnp.zeros_like(token_ref)
    rows, channels = x_ref.shape
    heads = step_ref.shape[0]
    width = channels // groups
    chunks = rows // CHUNK
    small = load([(c_hbm, c_ref)], semaphores)
    gates = [(gate_hbm.at[rows_of(n), :], gate_ref.at[rows_of(n), :]) for n in range(chunks)]
    gates = load(gates, semaphores.at[pl.ds(1, chunks)])
    size = channels // WEIGHT_COPIES
    weights = [(w_hbm.at[rows_of(n, size), :], w_ref.at[rows_of(n, size), :]) for n in range(WEIGHT_COPIES)]
    weights = load(weights, semaphores.at[pl.ds(1 + chunks, WEIGHT_COPIES)])

    spread = head_map(channels)
    row = lax.broadcasted_iota(jnp.int32, (CHUNK, CHUNK), 0)
    column = lax.broadcasted_iota(jnp.int32, (CHUNK, CHUNK), 1)
    lane = lax.broadcasted_iota(jnp.int32, (heads, CHUNK), 1)
    skip = jnp.concatenate([pieces(skip_ref[...], 0), jnp.zeros((EXTRA, 128 - heads), F32)], axis=1)
    skip = wide_log(skip.astype(BF16), spread)
    before = jnp.zeros((heads, 1), F32)
    state = [jnp.zeros((STATE, width), F32)] * groups
    small[0].wait()
    for n, running in enumerate(running_sums(decay_ref[...])):
        here = rows_of(n)
        middle, total = running[:, MIDDLE : MIDDLE + 1], running[:, CHUNK - 1 :]
        inner = running - middle
        factors = jnp.exp(jnp.where(lane == 0, total, jnp.where(lane == 1, total - middle, middle)))
        factors = jnp.concatenate(
            [
                by_row(step_ref[:, here] * jnp.exp(-inner)),
                by_row(jnp.exp(inner)),
                by_row(jnp.exp(before + running)),
                by_row(factors)[:EXTRA],
            ],
            axis=0,
        )
        before = before + total
        gates[n].wait()
        for g in range(groups):
            cut = slice(g * width, (g + 1) * width)
            part = slice(g * STATE, (g + 1) * STATE)
            wide = dot(factors, spread[:, cut])
            to_state, to_fresh, to_middle = (wide[3 * CHUNK + n : 3 * CHUNK + n + 1] for n in range(3))
            x = x_ref[here, cut].astype(F32)
            weighted = (x * wide[:CHUNK]).astype(BF16)
            started = jnp.concatenate([weighted, (state[g] * to_middle).astype(BF16)], axis=0)
            scores = lax.dot_general(
                c_ref[here, part], b_ref[here, part], (((1,), (1,)), ((), ())), preferred_element_type=F32
            )
            scores = jnp.where(row >= column, scores, 0.0).astype(BF16)
            within = dot(jnp.concatenate([scores, c_ref[here, part]], axis=1), started)
            if n < chunks - 1:
                fresh = lax.dot_general(
                    b_ref[here, part], weighted, (((0,), (0,)), ((), ())), preferred_element_type=F32
                )
                state[g] = state[g] * to_state + fresh * to_fresh
            gate = gate_ref[here, cut].astype(F32)
            gate = gate / (1.0 + jnp.exp(-gate))
            mixed_ref[here, cut] = (within * wide[CHUNK : 2 * CHUNK] + x * skip[:, cut]) * gate
            scale_ref[here, cut] = wide[2 * CHUNK : 3 * CHUNK] * gate
    for copy in weights:
        copy.wait()


def norm_rows(groups, state, mixed, scale, c_rows, gain):
    width = mixed.shape[1] // groups
    parts = []
    for g in range(groups):
        cut = slice(g * width, (g + 1) * width)
        carried = dot(c_rows[:, g * STATE : (g + 1) * STATE], state[:, cut])
        whole = mixed[:, cut] + scale[:, cut] * carried
        meansq = jnp.mean(whole * whole, axis=1, keepdims=True)
        parts.append((whole * lax.rsqrt(meansq + 1e-05) * gain[:, cut]).astype(BF16))
    return parts


def fill_state(core_ref, keep_ref, recv_ref, state):
    half = keep_ref.shape[1]
    for core in range(2):

        @pl.when(core_ref[0] == core)
        def _():
            state[:, core * half : (core + 1) * half] = keep_ref[...]
            state[:, (1 - core) * half : (2 - core) * half] = recv_ref[...]


def block_at(here, position, count, size):
    block = 0
    for i in range(count):
        block = jnp.where(here == i, block_order(i, count)[position], block)
    return pl.ds(pl.multiple_of(block * size, size), size)


def first_kernel(groups, count, core_ref, here_ref, mixed_ref, scale_ref, c_ref, keep_ref, recv_ref, gain_ref, w_ref, out_ref,
                 normed_ref, state):
    fill_state(core_ref, keep_ref, recv_ref, state)
    width = normed_ref.shape[1] // groups
    here = block_at(here_ref[0], 0, count, normed_ref.shape[0])
    rows = norm_rows(groups, state, mixed_ref.at[here, :], scale_ref.at[here, :], c_ref.at[here, :], gain_ref)
    for g, part in enumerate(rows):
        normed_ref[:, g * width : (g + 1) * width] = part

    @pl.loop(0, out_ref.shape[1] // COLUMN_TILE)
    def _(j):
        cut = pl.ds(pl.multiple_of(j * COLUMN_TILE, COLUMN_TILE), COLUMN_TILE)
        out_ref[:, cut] = dot(normed_ref[...], w_ref[:, cut]).astype(BF16)


def second_kernel(normed_ref, w_ref, out_ref):
    start = w_ref.shape[1] - out_ref.shape[1]

    @pl.loop(0, out_ref.shape[1] // COLUMN_TILE)
    def _(j):
        cut = pl.ds(pl.multiple_of(j * COLUMN_TILE, COLUMN_TILE), COLUMN_TILE)
        from_ = pl.ds(pl.multiple_of(start + j * COLUMN_TILE, COLUMN_TILE), COLUMN_TILE)
        out_ref[:, cut] = dot(normed_ref[...], w_ref[:, from_]).astype(BF16)


def rest_kernel(groups, count, core_ref, here_ref, mixed_ref, scale_ref, c_ref, keep_ref, recv_ref, gain_ref, w_ref, a_ref,
                b_ref, out_ref, state, normed):
    size, half = a_ref.shape
    blocks = [block_at(here_ref[0], n, count, size) for n in range(count)]
    out_ref[blocks[0], :half] = a_ref[...]
    out_ref[blocks[0], half:] = b_ref[...]
    fill_state(core_ref, keep_ref, recv_ref, state)
    width = normed.shape[1] // groups
    for n in range(1, count):
        here = blocks[n]
        rows = norm_rows(groups, state, mixed_ref.at[here, :], scale_ref.at[here, :], c_ref.at[here, :], gain_ref)
        for g, part in enumerate(rows):
            normed[(n - 1) * size : n * size, g * width : (g + 1) * width] = part

    @pl.loop(0, out_ref.shape[1] // COLUMN_TILE)
    def _(j):
        cut = pl.ds(pl.multiple_of(j * COLUMN_TILE, COLUMN_TILE), COLUMN_TILE)
        product = dot(normed[...], w_ref[:, cut]).astype(BF16)
        for n in range(1, count):
            out_ref[blocks[n], cut] = product[(n - 1) * size : n * size]


def pass_kernel(count, step, column, here_ref, right_ref, left_ref, sums_ref, to_right_ref, to_left_ref):
    size, width = right_ref.shape
    for shift, came, out in ((count - step, right_ref, to_right_ref), (step - count, left_ref, to_left_ref)):
        block = jnp.clip(here_ref[0] + shift, 0, count - 1)
        rows = pl.ds(pl.multiple_of(block * size, size), size)
        own = sums_ref[rows, column : column + width].astype(F32)
        out[...] = (own + came[...].astype(F32)).astype(BF16)


def sum_kernel(column, here_ref, right_ref, left_ref, sums_ref, *refs):
    out_hbm, total, semaphores = refs[-3:]
    size, width = right_ref.shape
    rows = pl.ds(pl.multiple_of(here_ref[0] * size, size), size)
    copies = []
    for n in range(SUM_COPIES):
        part = rows_of(n, size // SUM_COPIES)
        own = sums_ref[rows, column : column + width][part, :].astype(F32)
        total[part, :] = (own + right_ref[part, :].astype(F32) + left_ref[part, :].astype(F32)).astype(BF16)
        to = out_hbm.at[part, column : column + width]
        copies.extend(load([(total.at[part, :], to)], semaphores.at[pl.ds(n, 1)]))
    for copy in copies:
        copy.wait()


def block_order(here, count):
    order = []
    for step in range(1, count):
        for block, sends in ((count - step + here, here <= step - 1), (step - count + here, here >= count - step)):
            if sends and block not in order:
                order.append(block)
    return order + [b for b in range(count) if b not in order]


def in_vmem(kernel, name, ins, outs, scratch=(), vmem=4, flops=1, result=None):
    vm = pl.BlockSpec(memory_space=pltpu.VMEM)
    specs, arrays = [], []
    for v in ins:
        if isinstance(v, tuple):
            specs.append(pl.BlockSpec(memory_space=pltpu.HBM))
            arrays.append(pltpu.with_memory_space_constraint(v[0], pltpu.HBM))
        elif v.dtype == jnp.int32:
            specs.append(pl.BlockSpec(memory_space=pltpu.SMEM))
            arrays.append(v)
        else:
            specs.append(vm)
            arrays.append(pltpu.with_memory_space_constraint(v, pltpu.VMEM))
    in_hbm = outs is None
    return pl.pallas_call(
        kernel,
        in_specs=specs,
        out_specs=[pl.BlockSpec(memory_space=pltpu.HBM)] if in_hbm else [vm for _ in outs],
        out_shape=[pltpu.HBM(*result)] if in_hbm else [pltpu.VMEM(shape, kind) for shape, kind in outs],
        scratch_shapes=list(scratch),
        input_output_aliases={len(ins) - 1: 0} if in_hbm and isinstance(ins[-1], tuple) else {},
        compiler_params=pltpu.CompilerParams(vmem_limit_bytes=vmem * 2**20),
        cost_estimate=pl.CostEstimate(flops=flops, bytes_accessed=1, transcendentals=0),
        name=name,
    )(*arrays)


def line_reduce(first, partial_sums, here, size, columns):
    count = lax.axis_size("tp")
    width = columns // HALVES
    block = ((size, width), BF16)
    right = [None] * HALVES
    left = [None] * HALVES
    for step in range(1, count):
        to_right = [(i, i + 1) for i in range(step)]
        to_left = [(i, i - 1) for i in range(count - step, count)]
        for half in range(HALVES):
            if step == 1:
                right[half] = left[half] = lax.ppermute(first[half], "tp", to_right + to_left)
                continue
            ins = (here, right[half], left[half], partial_sums)
            send_right, send_left = in_vmem(partial(pass_kernel, count, step, half * width), "pass_on", ins, (block, block))
            right[half] = lax.ppermute(send_right, "tp", to_right)
            left[half] = lax.ppermute(send_left, "tp", to_left)
    out = ()
    for half in range(HALVES):
        ins = (here, right[half], left[half], partial_sums, *out)
        scratch = [pltpu.VMEM((size, width), BF16), pltpu.SemaphoreType.DMA((SUM_COPIES,))]
        kernel = partial(sum_kernel, half * width)
        out = (tuple(in_vmem(kernel, "sum_up", ins, None, scratch, result=((size, columns), BF16))),)
    return out[0][0]


def on_device(x_in, gate_z, b_in, c_in, step_size, log_decay, skip, norm_gain, out_weight):
    rows, channels = x_in.shape
    heads = step_size.shape[1]
    groups = b_in.shape[1] // STATE
    chunks = rows // CHUNK
    columns = out_weight.shape[1]
    half = channels // 2
    devices = lax.axis_size("ctx")
    chips = devices // 2
    count = lax.axis_size("tp")
    size = rows // count
    core = lax.rem(lax.axis_index("ctx"), 2).astype(jnp.int32).reshape(1)
    here = lax.axis_index("tp").astype(jnp.int32).reshape(1)
    message = ((half + EXTRA, 128), BF16)
    whole = ((rows, channels), F32)
    by_head = ((heads, rows), F32)
    maps = ((rows, groups * STATE), BF16)
    weighted = pltpu.VMEM((rows, half), BF16)

    send, x_here, b_here, step, decay, spread = in_vmem(
        partial(send_kernel, groups),
        "end_state_sent",
        (core, here, (x_in,), (b_in,), (step_size.T,), (log_decay.T,)),
        (message, ((rows, channels), BF16), maps, by_head, by_head, ((128, half), BF16)),
        scratch=[weighted, pltpu.SemaphoreType.DMA((5,))],
        vmem=6,
    )
    swap = [(i, i ^ 1) for i in range(devices)]
    sibling = lax.ppermute(send, "ctx", swap)
    (own,) = in_vmem(
        partial(keep_kernel, groups), "end_state_kept", (core, x_here, b_here, step, decay, spread), (message,), [weighted],
        vmem=6, flops=10**9,
    )
    (pair,) = in_vmem(pair_kernel, "pair", (core, spread, own, sibling), (message,))
    incoming, outgoing, distance = [], pair, 1
    while distance < chips:
        if incoming:
            (outgoing,) = in_vmem(join_kernel, "join", (spread, pair, *incoming), (message,))
        reach = list(range(distance, min(chips, 4 * distance), distance))
        arrived = {}
        for far in reversed(reach):
            arrived[far] = lax.ppermute(outgoing, "ctx", [(i, i + 2 * far) for i in range(devices - 2 * far)])
        incoming.extend(arrived[far] for far in reach)
        distance *= 4
    mixed, scale, weight, c_here, token = in_vmem(
        partial(local_kernel, groups),
        "local_part",
        ((gate_z,), (c_in,), (out_weight,), x_here, b_here, step, decay, skip.reshape(1, heads), pair),
        (whole, whole, (out_weight.shape, BF16), maps, ((EXTRA, 128), BF16)),
        scratch=[pltpu.VMEM((rows, channels), BF16), pltpu.SemaphoreType.DMA((1 + chunks + WEIGHT_COPIES,))],
        vmem=12,
        flops=8 * 10**9,
    )
    state = ((STATE, half), BF16)
    keep, send = in_vmem(last_kernel, "incoming", (core, token, spread, own, sibling, *incoming), (state, state))
    recv = lax.ppermute(send, "ctx", swap)

    first = ((size, columns // 2), BF16)
    gain = norm_gain.reshape(1, channels)
    inputs = (core, here, mixed, scale, c_here, keep, recv, gain, weight)
    whole_state = pltpu.VMEM((STATE, channels), BF16)
    first_a, normed = in_vmem(
        partial(first_kernel, groups, count), "first_block", inputs, (first, ((size, channels), BF16)), [whole_state]
    )
    (first_b,) = in_vmem(second_kernel, "first_block_rest", (normed, weight), (first,))
    (partial_sums,) = in_vmem(
        partial(rest_kernel, groups, count),
        "other_blocks",
        (*inputs, first_a, first_b),
        (((rows, columns), BF16),),
        [whole_state, pltpu.VMEM((rows - size, channels), BF16)],
        vmem=6,
    )
    return line_reduce((first_a, first_b), partial_sums, here, size, columns)


def solution(mesh):
    placed = (
        P("ctx", "tp"),
        P("ctx", "tp"),
        P("ctx", "tp"),
        P("ctx", "tp"),
        P("ctx", "tp"),
        P("ctx", "tp"),
        P("tp"),
        P("tp"),
        P("tp", None),
    )
    return jax.shard_map(
        on_device, mesh=mesh, in_specs=placed, out_specs=P(("ctx", "tp"), None), check_vma=False
    )
```

```python
from functools import partial

import jax
import jax.numpy as jnp
from jax import lax
from jax.experimental import pallas as pl
from jax.experimental.pallas import tpu as pltpu
from jax.sharding import PartitionSpec as P

HEAD_DIM = 64
STATE = 128
CHUNK = 128
MIDDLE = CHUNK // 2 - 1
EXTRA = 16
COLUMN_TILE = 512
HALVES = 2
WEIGHT_COPIES = 8
SUM_COPIES = 4
PIECES = 2
F32 = jnp.float32
BF16 = jnp.bfloat16


def dot(a, b):
    return jnp.dot(a, b, preferred_element_type=F32)


def dot_exact(a, b):
    return jnp.dot(a, b, preferred_element_type=F32, precision=lax.Precision.HIGHEST)


def head_map(channels):
    head = lax.broadcasted_iota(jnp.int32, (128, channels), 0) & 63
    place = lax.broadcasted_iota(jnp.int32, (128, channels), 1) >> 6
    return jnp.where(head == place, 1.0, 0.0).astype(BF16)


def padded(values):
    return jnp.concatenate([values, jnp.zeros((64 - values.shape[0], values.shape[1]), F32)], axis=0)


def by_row(values):
    high = values.astype(BF16).astype(F32)
    return jnp.transpose(jnp.concatenate([padded(high), padded(values - high)], axis=0)).astype(BF16)


def pieces(values, axis):
    first = values.astype(BF16).astype(F32)
    second = (values - first).astype(BF16).astype(F32)
    third = values - first - second
    shape = (EXTRA, values.shape[1]) if axis == 0 else (values.shape[0], 128)
    at = lax.broadcasted_iota(jnp.int32, shape, axis)
    return jnp.where(at == 0, first, jnp.where(at == 1, second, jnp.where(at == 2, third, 0.0)))


def running_sums(decay):
    row = lax.broadcasted_iota(jnp.int32, (CHUNK, CHUNK), 0)
    column = lax.broadcasted_iota(jnp.int32, (CHUNK, CHUNK), 1)
    upper = jnp.where(row <= column, 1.0, 0.0)
    return [dot_exact(decay[:, rows_of(n)], upper) for n in range(decay.shape[1] // CHUNK)]


def load(pairs, semaphores):
    copies = [pltpu.make_async_copy(src, dst, semaphores.at[n]) for n, (src, dst) in enumerate(pairs)]
    for copy in copies:
        copy.start()
    return copies


def rows_of(chunk, size=CHUNK):
    return slice(chunk * size, (chunk + 1) * size)


def put_message(ref, state, logs):
    for j in range(state.shape[1] // 128):
        ref[j * STATE : (j + 1) * STATE, :] = state[:, j * 128 : (j + 1) * 128].astype(BF16)
    ref[state.shape[1] :, :] = logs.astype(BF16)


def state_of(ref):
    count = (ref.shape[0] - EXTRA) // STATE
    return jnp.concatenate([ref[j * STATE : (j + 1) * STATE, :] for j in range(count)], axis=1).astype(F32)


def logs_of(ref):
    return ref[ref.shape[0] - EXTRA :, :]


def wide_log(logs, spread):
    return jnp.sum(dot(logs, spread), axis=0, keepdims=True)


def end_state(groups, half, x_ref, b_ref, step_ref, decay_ref, weighted, message_ref, spread):
    rows, width = weighted.shape
    heads = width // HEAD_DIM
    of_heads = pl.ds(pl.multiple_of(half * heads, heads), heads)
    of_channels = pl.ds(pl.multiple_of(half * width, width), width)
    of_group = pl.ds(pl.multiple_of((half * groups // 2) * STATE, STATE), STATE)
    before, running = jnp.zeros((heads, 1), F32), []
    for sums in running_sums(decay_ref[of_heads, :]):
        running.append(before + sums)
        before = before + sums[:, CHUNK - 1 :]
    for n, sums in enumerate(running):
        here = rows_of(n)
        factor = dot(by_row(step_ref[of_heads, here] * jnp.exp(before - sums)), spread)
        weighted[here, :] = (x_ref[here, of_channels].astype(F32) * factor).astype(BF16)
    state = lax.dot_general(
        b_ref[:, of_group], weighted[...], (((0,), (0,)), ((), ())), preferred_element_type=F32
    )
    logs = jnp.concatenate([pieces(before, 1), jnp.zeros((128 - heads, 128), F32)], axis=0)
    put_message(message_ref, state, jnp.transpose(logs)[:EXTRA])


def send_kernel(groups, ctx_ref, here_ref, x_hbm, b_hbm, step_hbm, decay_hbm, send_ref, x_ref, b_ref, step_ref, decay_ref,
                spread_ref, weighted, semaphores):
    width = weighted.shape[1]
    other = 1 - (ctx_ref[0] & 1)
    of_channels = [pl.ds(pl.multiple_of(half * width, width), width) for half in (other, 1 - other)]
    copies = load(
        [(decay_hbm, decay_ref), (step_hbm, step_ref), (b_hbm, b_ref)]
        + [(x_hbm.at[:, cut], x_ref.at[:, cut]) for cut in of_channels],
        semaphores,
    )
    spread = head_map(width)
    spread_ref[...] = spread
    for copy in copies[:4]:
        copy.wait()
    end_state(groups, other, x_ref, b_ref, step_ref, decay_ref, weighted, send_ref, spread)
    copies[4].wait()


def keep_kernel(groups, ctx_ref, x_ref, b_ref, step_ref, decay_ref, spread_ref, keep_ref, weighted):
    end_state(groups, (ctx_ref[0] & 1), x_ref, b_ref, step_ref, decay_ref, weighted, keep_ref, spread_ref[...])


def pair_kernel(ctx_ref, spread_ref, own_ref, sibling_ref, *pieces_refs):
    spread = spread_ref[...]
    own_log, sibling_log = wide_log(logs_of(own_ref), spread), wide_log(logs_of(sibling_ref), spread)
    early = (ctx_ref[0] & 1) == 0
    own_scale = jnp.where(early, jnp.exp(sibling_log), 1.0)
    sibling_scale = jnp.where(early, 1.0, jnp.exp(own_log))
    logs = logs_of(own_ref).astype(F32) + logs_of(sibling_ref).astype(F32)
    logs = pieces(jnp.sum(logs, axis=0, keepdims=True), 0)
    state = state_of(own_ref) * own_scale + state_of(sibling_ref) * sibling_scale
    width = state.shape[1] // len(pieces_refs)
    for n, ref in enumerate(pieces_refs):
        put_message(ref, state[:, n * width : (n + 1) * width], logs)


def is_upper(ctx_ref, level):
    return ((ctx_ref[0] >> (1 + level)) & 1) == 1


def piece_of(spread_ref, piece, ref):
    width = ref.shape[0] - EXTRA
    return spread_ref[:, piece * width : (piece + 1) * width]


def fold_kernel(level, piece, ctx_ref, after_ref, spread_ref, total_ref, other_ref, out_ref):
    spread = piece_of(spread_ref, piece, total_ref)
    upper = is_upper(ctx_ref, level)
    total_scale = jnp.where(upper, 1.0, jnp.exp(wide_log(logs_of(other_ref), spread)))
    other_scale = jnp.where(upper, jnp.exp(wide_log(logs_of(total_ref), spread)), 1.0)
    logs = logs_of(total_ref).astype(F32) + logs_of(other_ref).astype(F32)
    logs = pieces(jnp.sum(logs, axis=0, keepdims=True), 0)
    put_message(out_ref, state_of(total_ref) * total_scale + state_of(other_ref) * other_scale, logs)


def last_kernel(levels, ctx_ref, after_ref, spread_ref, own_ref, sibling_ref, *refs):
    keep_ref, send_ref = refs[-2:]
    count = len(refs[:-2]) // levels
    parts = []
    for piece in range(count):
        state = log = 0.0
        for level in range(levels):
            ref = refs[level * count + piece]
            upper = is_upper(ctx_ref, level)
            spread = piece_of(spread_ref, piece, ref)
            state = state + jnp.where(upper, state_of(ref), 0.0) * jnp.exp(log)
            log = log + jnp.where(upper, wide_log(logs_of(ref), spread), 0.0)
        parts.append(state)
    chip = jnp.concatenate(parts, axis=1)
    for core, first, mine, other in ((0, own_ref, 0, 1), (1, sibling_ref, 1, 0)):

        @pl.when((ctx_ref[0] & 1) == core)
        def _():
            after = chip * jnp.exp(wide_log(logs_of(first), spread_ref[...])) + state_of(first)
            both = (chip.astype(BF16), after.astype(BF16))
            keep_ref[...] = both[mine]
            send_ref[...] = both[other]


def local_kernel(groups, part_index, gate_hbm, c_hbm, w_hbm, x_ref, b_ref, step_ref, decay_ref, skip_ref, after_ref, *refs):
    if part_index:
        refs = refs[5:]
    mixed_ref, scale_ref, c_ref, state_ref, before_ref, w_ref, token_ref, gate_ref, semaphores = refs
    token_ref[...] = jnp.zeros_like(token_ref)
    channels = x_ref.shape[1]
    heads = step_ref.shape[0]
    width = channels // groups
    chunks = gate_ref.shape[0] // CHUNK
    mine = range(part_index * chunks, (part_index + 1) * chunks)
    own_rows = rows_of(part_index, chunks * CHUNK)
    small = load([(c_hbm.at[own_rows, :], c_ref.at[own_rows, :])], semaphores)
    gates = [(gate_hbm.at[rows_of(n), :], gate_ref.at[rows_of(n - mine[0]), :]) for n in mine]
    gates = load(gates, semaphores.at[pl.ds(1, chunks)])
    size = channels // WEIGHT_COPIES
    columns = rows_of(part_index, w_ref.shape[1])
    weights = [(w_hbm.at[rows_of(n, size), columns], w_ref.at[rows_of(n, size), :]) for n in range(WEIGHT_COPIES)]
    weights = load(weights, semaphores.at[pl.ds(1 + chunks, WEIGHT_COPIES)])

    spread = head_map(channels)
    row = lax.broadcasted_iota(jnp.int32, (CHUNK, CHUNK), 0)
    column = lax.broadcasted_iota(jnp.int32, (CHUNK, CHUNK), 1)
    lane = lax.broadcasted_iota(jnp.int32, (heads, CHUNK), 1)
    skip = jnp.concatenate([pieces(skip_ref[...], 0), jnp.zeros((EXTRA, 128 - heads), F32)], axis=1)
    skip = wide_log(skip.astype(BF16), spread)
    before = jnp.zeros((heads, 1), F32)
    state = [jnp.zeros((STATE, width), F32)] * groups
    if part_index:
        before = before_ref[:, 0:1]
        state = [state_ref[:, rows_of(g, width)] for g in range(groups)]
    small[0].wait()
    for n, running in zip(mine, running_sums(decay_ref[:, own_rows])):
        here = rows_of(n)
        middle, total = running[:, MIDDLE : MIDDLE + 1], running[:, CHUNK - 1 :]
        inner = running - middle
        factors = jnp.exp(jnp.where(lane == 0, total, jnp.where(lane == 1, total - middle, middle)))
        factors = jnp.concatenate(
            [
                by_row(step_ref[:, here] * jnp.exp(-inner)),
                by_row(jnp.exp(inner)),
                by_row(jnp.exp(before + running)),
                by_row(factors)[:EXTRA],
            ],
            axis=0,
        )
        before = before + total
        gates[n - mine[0]].wait()
        for g in range(groups):
            cut = slice(g * width, (g + 1) * width)
            part = slice(g * STATE, (g + 1) * STATE)
            wide = dot(factors, spread[:, cut])
            to_state, to_fresh, to_middle = (wide[3 * CHUNK + n : 3 * CHUNK + n + 1] for n in range(3))
            x = x_ref[here, cut].astype(F32)
            weighted = (x * wide[:CHUNK]).astype(BF16)
            started = jnp.concatenate([weighted, (state[g] * to_middle).astype(BF16)], axis=0)
            scores = lax.dot_general(
                c_ref[here, part], b_ref[here, part], (((1,), (1,)), ((), ())), preferred_element_type=F32
            )
            scores = jnp.where(row >= column, scores, 0.0).astype(BF16)
            within = dot(jnp.concatenate([scores, c_ref[here, part]], axis=1), started)
            if n + 1 < x_ref.shape[0] // CHUNK:
                fresh = lax.dot_general(
                    b_ref[here, part], weighted, (((0,), (0,)), ((), ())), preferred_element_type=F32
                )
                state[g] = state[g] * to_state + fresh * to_fresh
            gate = gate_ref[rows_of(n - mine[0]), cut].astype(F32)
            gate = gate / (1.0 + jnp.exp(-gate))
            mixed_ref[here, cut] = (within * wide[CHUNK : 2 * CHUNK] + x * skip[:, cut]) * gate
            scale_ref[here, cut] = wide[2 * CHUNK : 3 * CHUNK] * gate
    before_ref[...] = jnp.broadcast_to(before, before_ref.shape)
    for g in range(groups):
        state_ref[:, rows_of(g, width)] = state[g]
    for copy in weights:
        copy.wait()


def norm_rows(groups, state, mixed, scale, c_rows, gain):
    width = mixed.shape[1] // groups
    parts = []
    for g in range(groups):
        cut = slice(g * width, (g + 1) * width)
        carried = dot(c_rows[:, g * STATE : (g + 1) * STATE], state[:, cut])
        whole = mixed[:, cut] + scale[:, cut] * carried
        meansq = jnp.mean(whole * whole, axis=1, keepdims=True)
        parts.append((whole * lax.rsqrt(meansq + 1e-05) * gain[:, cut]).astype(BF16))
    return parts


def fill_state(ctx_ref, keep_ref, recv_ref, state):
    half = keep_ref.shape[1]
    for core in range(2):

        @pl.when((ctx_ref[0] & 1) == core)
        def _():
            state[:, core * half : (core + 1) * half] = keep_ref[...]
            state[:, (1 - core) * half : (2 - core) * half] = recv_ref[...]


def block_at(here, position, count, size):
    block = 0
    for i in range(count):
        block = jnp.where(here == i, block_order(i, count)[position], block)
    return pl.ds(pl.multiple_of(block * size, size), size)


def first_kernel(groups, count, ctx_ref, here_ref, mixed_ref, scale_ref, c_ref, keep_ref, recv_ref, gain_ref, w_ref, out_ref,
                 normed_ref, state):
    fill_state(ctx_ref, keep_ref, recv_ref, state)
    width = normed_ref.shape[1] // groups
    here = block_at(here_ref[0], 0, count, normed_ref.shape[0])
    rows = norm_rows(groups, state, mixed_ref.at[here, :], scale_ref.at[here, :], c_ref.at[here, :], gain_ref)
    for g, part in enumerate(rows):
        normed_ref[:, g * width : (g + 1) * width] = part

    @pl.loop(0, out_ref.shape[1] // COLUMN_TILE)
    def _(j):
        cut = pl.ds(pl.multiple_of(j * COLUMN_TILE, COLUMN_TILE), COLUMN_TILE)
        out_ref[:, cut] = dot(normed_ref[...], w_ref[:, cut]).astype(BF16)


def second_kernel(normed_ref, w_ref, out_ref):
    @pl.loop(0, out_ref.shape[1] // COLUMN_TILE)
    def _(j):
        cut = pl.ds(pl.multiple_of(j * COLUMN_TILE, COLUMN_TILE), COLUMN_TILE)
        out_ref[:, cut] = dot(normed_ref[...], w_ref[:, cut]).astype(BF16)


def rest_kernel(groups, count, ctx_ref, here_ref, mixed_ref, scale_ref, c_ref, keep_ref, recv_ref, gain_ref, wa_ref, wb_ref,
                a_ref, b_ref, out_ref, state, normed):
    size, half = a_ref.shape
    blocks = [block_at(here_ref[0], n, count, size) for n in range(count)]
    out_ref[blocks[0], :half] = a_ref[...]
    out_ref[blocks[0], half:] = b_ref[...]
    fill_state(ctx_ref, keep_ref, recv_ref, state)
    width = normed.shape[1] // groups
    for n in range(1, count):
        here = blocks[n]
        rows = norm_rows(groups, state, mixed_ref.at[here, :], scale_ref.at[here, :], c_ref.at[here, :], gain_ref)
        for g, part in enumerate(rows):
            normed[(n - 1) * size : n * size, g * width : (g + 1) * width] = part

    for first_column, w_ref in ((0, wa_ref), (half, wb_ref)):

        @pl.loop(0, half // COLUMN_TILE)
        def _(j):
            cut = pl.ds(pl.multiple_of(j * COLUMN_TILE, COLUMN_TILE), COLUMN_TILE)
            to = pl.ds(pl.multiple_of(first_column + j * COLUMN_TILE, COLUMN_TILE), COLUMN_TILE)
            product = dot(normed[...], w_ref[:, cut]).astype(BF16)
            for n in range(1, count):
                out_ref[blocks[n], to] = product[(n - 1) * size : n * size]


def pass_kernel(count, step, column, here_ref, *refs):
    sums_ref, even_out, odd_out = refs[-3:]
    arrived = refs[:-3]
    size, width = even_out.shape
    here = here_ref[0]

    def send(shift, came, out):
        block = jnp.clip(here + shift, 0, count - 1)
        rows = pl.ds(pl.multiple_of(block * size, size), size)
        own = sums_ref[rows, column : column + width].astype(F32)
        for ref in came:
            own = own + ref[...].astype(F32)
        out[...] = own.astype(BF16)

    for parity, to_right, to_left, from_left, from_right in (
        (0, even_out, odd_out, arrived[1:], arrived[:1]),
        (1, odd_out, even_out, arrived[:1], arrived[1:]),
    ):

        @pl.when((here & 1) == parity)
        def _():
            send(count - step, from_left, to_right)
            send(step - count, from_right, to_left)


def sum_kernel(column, here_ref, even_ref, odd_ref, sums_ref, *refs):
    out_hbm, total, semaphores = refs[-3:]
    size, width = even_ref.shape
    rows = pl.ds(pl.multiple_of(here_ref[0] * size, size), size)
    copies = []
    for n in range(SUM_COPIES):
        part = rows_of(n, size // SUM_COPIES)
        own = sums_ref[rows, column : column + width][part, :].astype(F32)
        total[part, :] = (own + even_ref[part, :].astype(F32) + odd_ref[part, :].astype(F32)).astype(BF16)
        to = out_hbm.at[part, column : column + width]
        copies.extend(load([(total.at[part, :], to)], semaphores.at[pl.ds(n, 1)]))
    for copy in copies:
        copy.wait()


def block_order(here, count):
    order = []
    for step in range(1, count):
        for block, sends in ((count - step + here, here <= step - 1), (step - count + here, here >= count - step)):
            if sends and block not in order:
                order.append(block)
    return order + [b for b in range(count) if b not in order]


def in_vmem(kernel, name, ins, outs, scratch=(), vmem=4, flops=1, result=None, aliases=None):
    vm = pl.BlockSpec(memory_space=pltpu.VMEM)
    specs, arrays = [], []
    for v in ins:
        if isinstance(v, tuple):
            specs.append(pl.BlockSpec(memory_space=pltpu.HBM))
            arrays.append(pltpu.with_memory_space_constraint(v[0], pltpu.HBM))
        elif v.dtype == jnp.int32:
            specs.append(pl.BlockSpec(memory_space=pltpu.SMEM))
            arrays.append(v)
        else:
            specs.append(vm)
            arrays.append(pltpu.with_memory_space_constraint(v, pltpu.VMEM))
    in_hbm = outs is None
    return pl.pallas_call(
        kernel,
        in_specs=specs,
        out_specs=[pl.BlockSpec(memory_space=pltpu.HBM)] if in_hbm else [vm for _ in outs],
        out_shape=[pltpu.HBM(*result)] if in_hbm else [pltpu.VMEM(shape, kind) for shape, kind in outs],
        scratch_shapes=list(scratch),
        input_output_aliases={len(ins) - 1: 0} if in_hbm and isinstance(ins[-1], tuple) else aliases or {},
        compiler_params=pltpu.CompilerParams(vmem_limit_bytes=vmem * 2**20),
        cost_estimate=pl.CostEstimate(flops=flops, bytes_accessed=1, transcendentals=0),
        name=name,
    )(*arrays)


def line_reduce(first, partial_sums, here, size, columns):
    count = lax.axis_size("tp")
    width = columns // HALVES
    block = ((size, width), BF16)
    even_edges = [(i, i ^ 1) for i in range(count)]
    odd_edges = [(i, ((i + 1) ^ 1) - 1) for i in range(1, count - 1)]
    arrived = [()] * HALVES
    for step in range(1, count):
        for half in range(HALVES):
            if step == 1:
                arrived[half] = (lax.ppermute(first[half], "tp", even_edges),)
                continue
            even, odd = in_vmem(
                partial(pass_kernel, count, step, half * width), "pass_on", (here, *arrived[half], partial_sums), (block, block)
            )
            arrived[half] = (lax.ppermute(even, "tp", even_edges), lax.ppermute(odd, "tp", odd_edges))
    out = ()
    for half in range(HALVES):
        ins = (here, *arrived[half], partial_sums, *out)
        scratch = [pltpu.VMEM((size, width), BF16), pltpu.SemaphoreType.DMA((SUM_COPIES,))]
        kernel = partial(sum_kernel, half * width)
        out = (tuple(in_vmem(kernel, "sum_up", ins, None, scratch, result=((size, columns), BF16))),)
    return out[0][0]


def on_device(x_in, gate_z, b_in, c_in, step_size, log_decay, skip, norm_gain, out_weight):
    rows, channels = x_in.shape
    heads = step_size.shape[1]
    groups = b_in.shape[1] // STATE
    chunks = rows // CHUNK
    columns = out_weight.shape[1]
    half = channels // 2
    devices = lax.axis_size("ctx")
    chips = devices // 2
    count = lax.axis_size("tp")
    size = rows // count
    ctx = lax.axis_index("ctx").astype(jnp.int32).reshape(1)
    here = lax.axis_index("tp").astype(jnp.int32).reshape(1)
    message = ((half + EXTRA, 128), BF16)
    whole = ((rows, channels), F32)
    by_head = ((heads, rows), F32)
    maps = ((rows, groups * STATE), BF16)
    weighted = pltpu.VMEM((rows, half), BF16)

    send, x_here, b_here, step, decay, spread = in_vmem(
        partial(send_kernel, groups),
        "end_state_sent",
        (ctx, here, (x_in,), (b_in,), (step_size.T,), (log_decay.T,)),
        (message, ((rows, channels), BF16), maps, by_head, by_head, ((128, half), BF16)),
        scratch=[weighted, pltpu.SemaphoreType.DMA((5,))],
        vmem=6,
    )
    swap = [(i, i ^ 1) for i in range(devices)]
    sibling = lax.ppermute(send, "ctx", swap)
    (own,) = in_vmem(
        partial(keep_kernel, groups), "end_state_kept", (ctx, x_here, b_here, step, decay, spread), (message,), [weighted],
        vmem=6, flops=10**9,
    )
    piece = ((half // PIECES + EXTRA, 128), BF16)
    totals = in_vmem(pair_kernel, "pair", (ctx, spread, own, sibling), (piece,) * PIECES)
    levels = chips.bit_length() - 1

    def swap_chips(level, blocks):
        return [lax.ppermute(v, "ctx", [(i, i ^ (2 << level)) for i in range(devices)]) for v in blocks]

    def local_part(part_index, after, carried):
        return in_vmem(
            partial(local_kernel, groups, part_index),
            "local_part",
            ((gate_z,), (c_in,), (out_weight,), x_here, b_here, step, decay, skip.reshape(1, heads), after, *carried),
            (
                whole,
                whole,
                maps,
                ((STATE, channels), F32),
                ((heads, 128), F32),
                ((channels, columns // 2), BF16),
                ((EXTRA, 128), BF16),
            ),
            scratch=[
                pltpu.VMEM((rows // 2, channels), BF16),
                pltpu.SemaphoreType.DMA((1 + chunks // 2 + WEIGHT_COPIES,)),
            ],
            vmem=10,
            flops=4 * 10**9,
            aliases={9 + n: n for n in range(len(carried))},
        )

    received = swap_chips(0, totals)
    *carried, weight_a, token = local_part(0, totals[-1], ())
    arrived = list(received)
    for level in range(1, levels):
        folded = []
        for n in range(PIECES):
            kernel = partial(fold_kernel, level - 1, n)
            after = folded[-1] if folded else token
            folded.extend(in_vmem(kernel, "fold", (ctx, after, spread, totals[n], received[n]), (piece,)))
        totals = folded
        received = swap_chips(level, totals)
        arrived.extend(received)
    mixed, scale, c_here, _, _, weight_b, token = local_part(1, totals[-1], carried)
    state = ((STATE, half), BF16)
    keep, send = in_vmem(
        partial(last_kernel, levels), "incoming", (ctx, token, spread, own, sibling, *arrived), (state, state)
    )
    recv = lax.ppermute(send, "ctx", swap)

    first = ((size, columns // 2), BF16)
    gain = norm_gain.reshape(1, channels)
    inputs = (ctx, here, mixed, scale, c_here, keep, recv, gain, weight_a)
    whole_state = pltpu.VMEM((STATE, channels), BF16)
    first_a, normed = in_vmem(
        partial(first_kernel, groups, count), "first_block", inputs, (first, ((size, channels), BF16)), [whole_state]
    )
    (first_b,) = in_vmem(second_kernel, "first_block_rest", (normed, weight_b), (first,))
    (partial_sums,) = in_vmem(
        partial(rest_kernel, groups, count),
        "other_blocks",
        (*inputs, weight_b, first_a, first_b),
        (((rows, columns), BF16),),
        [whole_state, pltpu.VMEM((rows - size, channels), BF16)],
        vmem=6,
    )
    return line_reduce((first_a, first_b), partial_sums, here, size, columns)


def solution(mesh):
    placed = (
        P("ctx", "tp"),
        P("ctx", "tp"),
        P("ctx", "tp"),
        P("ctx", "tp"),
        P("ctx", "tp"),
        P("ctx", "tp"),
        P("tp"),
        P("tp"),
        P("tp", None),
    )
    return jax.shard_map(
        on_device, mesh=mesh, in_specs=placed, out_specs=P(("ctx", "tp"), None), check_vma=False
    )
```

```python
from functools import partial

import jax
import jax.numpy as jnp
from jax import lax
from jax.experimental import pallas as pl
from jax.experimental.pallas import tpu as pltpu
from jax.sharding import PartitionSpec as P

HEAD_DIM = 64
STATE = 128
CHUNK = 128
MIDDLE = CHUNK // 2 - 1
EXTRA = 16
COLUMN_TILE = 512
PARTS = 4
WEIGHT_COPIES = 8
SUM_COPIES = 4
PIECES = 2
F32 = jnp.float32
BF16 = jnp.bfloat16


def dot(a, b):
    return jnp.dot(a, b, preferred_element_type=F32)


def dot_exact(a, b):
    return jnp.dot(a, b, preferred_element_type=F32, precision=lax.Precision.HIGHEST)


def head_map(channels):
    head = lax.broadcasted_iota(jnp.int32, (128, channels), 0) & 63
    place = lax.broadcasted_iota(jnp.int32, (128, channels), 1) >> 6
    return jnp.where(head == place, 1.0, 0.0).astype(BF16)


def padded(values):
    return jnp.concatenate([values, jnp.zeros((64 - values.shape[0], values.shape[1]), F32)], axis=0)


def by_row(values):
    high = values.astype(BF16).astype(F32)
    return jnp.transpose(jnp.concatenate([padded(high), padded(values - high)], axis=0)).astype(BF16)


def pieces(values, axis):
    first = values.astype(BF16).astype(F32)
    second = (values - first).astype(BF16).astype(F32)
    third = values - first - second
    shape = (EXTRA, values.shape[1]) if axis == 0 else (values.shape[0], 128)
    at = lax.broadcasted_iota(jnp.int32, shape, axis)
    return jnp.where(at == 0, first, jnp.where(at == 1, second, jnp.where(at == 2, third, 0.0)))


def running_sums(decay):
    row = lax.broadcasted_iota(jnp.int32, (CHUNK, CHUNK), 0)
    column = lax.broadcasted_iota(jnp.int32, (CHUNK, CHUNK), 1)
    upper = jnp.where(row <= column, 1.0, 0.0)
    return [dot_exact(decay[:, rows_of(n)], upper) for n in range(decay.shape[1] // CHUNK)]


def load(pairs, semaphores):
    copies = [pltpu.make_async_copy(src, dst, semaphores.at[n]) for n, (src, dst) in enumerate(pairs)]
    for copy in copies:
        copy.start()
    return copies


def rows_of(chunk, size=CHUNK):
    return slice(chunk * size, (chunk + 1) * size)


def put_message(ref, state, logs):
    for j in range(state.shape[1] // 128):
        ref[j * STATE : (j + 1) * STATE, :] = state[:, j * 128 : (j + 1) * 128].astype(BF16)
    ref[state.shape[1] :, :] = logs.astype(BF16)


def state_of(ref):
    count = (ref.shape[0] - EXTRA) // STATE
    return jnp.concatenate([ref[j * STATE : (j + 1) * STATE, :] for j in range(count)], axis=1).astype(F32)


def logs_of(ref):
    return ref[ref.shape[0] - EXTRA :, :]


def wide_log(logs, spread):
    return jnp.sum(dot(logs, spread), axis=0, keepdims=True)


def end_state(groups, half, x_ref, b_ref, step_ref, decay_ref, weighted, message_ref, spread, x_copies=(), b_copies=()):
    rows, width = weighted.shape
    heads = width // HEAD_DIM
    of_heads = pl.ds(pl.multiple_of(half * heads, heads), heads)
    of_channels = pl.ds(pl.multiple_of(half * width, width), width)
    of_group = pl.ds(pl.multiple_of((half * groups // 2) * STATE, STATE), STATE)
    before, running = jnp.zeros((heads, 1), F32), []
    for sums in running_sums(decay_ref[of_heads, :]):
        running.append(before + sums)
        before = before + sums[:, CHUNK - 1 :]
    factors = [by_row(step_ref[of_heads, rows_of(n)] * jnp.exp(before - sums)) for n, sums in enumerate(running)]
    for n, factor in enumerate(factors):
        here = rows_of(n)
        factor = dot(factor, spread)
        for copy in x_copies[n : n + 1]:
            copy.wait()
        weighted[here, :] = (x_ref[here, of_channels].astype(F32) * factor).astype(BF16)
    for copy in b_copies:
        copy.wait()
    state = lax.dot_general(
        b_ref[:, of_group], weighted[...], (((0,), (0,)), ((), ())), preferred_element_type=F32
    )
    logs = jnp.concatenate([pieces(before, 1), jnp.zeros((128 - heads, 128), F32)], axis=0)
    put_message(message_ref, state, jnp.transpose(logs)[:EXTRA])


def send_kernel(groups, ctx_ref, here_ref, x_hbm, b_hbm, step_hbm, decay_hbm, send_ref, x_ref, b_ref, step_ref, decay_ref,
                spread_ref, weighted, semaphores):
    width = weighted.shape[1]
    other = 1 - (ctx_ref[0] & 1)
    first, second = [pl.ds(pl.multiple_of(half * width, width), width) for half in (other, 1 - other)]
    rows = [rows_of(n) for n in range(x_ref.shape[0] // CHUNK)]
    copies = load(
        [(decay_hbm, decay_ref), (step_hbm, step_ref)]
        + [(x_hbm.at[here, first], x_ref.at[here, first]) for here in rows]
        + [(b_hbm, b_ref), (x_hbm.at[:, second], x_ref.at[:, second])],
        semaphores,
    )
    spread = head_map(width)
    spread_ref[...] = spread
    for copy in copies[:2]:
        copy.wait()
    end_state(
        groups, other, x_ref, b_ref, step_ref, decay_ref, weighted, send_ref, spread, copies[2:-2], copies[-2:-1]
    )
    copies[-1].wait()


def keep_kernel(groups, ctx_ref, x_ref, b_ref, step_ref, decay_ref, spread_ref, keep_ref, weighted):
    end_state(groups, (ctx_ref[0] & 1), x_ref, b_ref, step_ref, decay_ref, weighted, keep_ref, spread_ref[...])


def pair_kernel(ctx_ref, spread_ref, own_ref, sibling_ref, *pieces_refs):
    spread = spread_ref[...]
    own_log, sibling_log = wide_log(logs_of(own_ref), spread), wide_log(logs_of(sibling_ref), spread)
    early = (ctx_ref[0] & 1) == 0
    own_scale = jnp.where(early, jnp.exp(sibling_log), 1.0)
    sibling_scale = jnp.where(early, 1.0, jnp.exp(own_log))
    logs = logs_of(own_ref).astype(F32) + logs_of(sibling_ref).astype(F32)
    logs = pieces(jnp.sum(logs, axis=0, keepdims=True), 0)
    state = state_of(own_ref) * own_scale + state_of(sibling_ref) * sibling_scale
    width = state.shape[1] // len(pieces_refs)
    for n, ref in enumerate(pieces_refs):
        put_message(ref, state[:, n * width : (n + 1) * width], logs)


def is_upper(ctx_ref, level):
    return ((ctx_ref[0] >> (1 + level)) & 1) == 1


def piece_of(spread_ref, piece, ref):
    width = ref.shape[0] - EXTRA
    return spread_ref[:, piece * width : (piece + 1) * width]


def fold_kernel(level, piece, ctx_ref, after_ref, spread_ref, total_ref, other_ref, out_ref):
    spread = piece_of(spread_ref, piece, total_ref)
    upper = is_upper(ctx_ref, level)
    total_scale = jnp.where(upper, 1.0, jnp.exp(wide_log(logs_of(other_ref), spread)))
    other_scale = jnp.where(upper, jnp.exp(wide_log(logs_of(total_ref), spread)), 1.0)
    logs = logs_of(total_ref).astype(F32) + logs_of(other_ref).astype(F32)
    logs = pieces(jnp.sum(logs, axis=0, keepdims=True), 0)
    put_message(out_ref, state_of(total_ref) * total_scale + state_of(other_ref) * other_scale, logs)


def last_kernel(levels, ctx_ref, after_ref, spread_ref, own_ref, sibling_ref, *refs):
    keep_ref, send_ref = refs[-2:]
    count = len(refs[:-2]) // levels
    parts = []
    for piece in range(count):
        state = log = 0.0
        for level in range(levels):
            ref = refs[level * count + piece]
            upper = is_upper(ctx_ref, level)
            spread = piece_of(spread_ref, piece, ref)
            state = state + jnp.where(upper, state_of(ref), 0.0) * jnp.exp(log)
            log = log + jnp.where(upper, wide_log(logs_of(ref), spread), 0.0)
        parts.append(state)
    chip = jnp.concatenate(parts, axis=1)
    for core, first, mine, other in ((0, own_ref, 0, 1), (1, sibling_ref, 1, 0)):

        @pl.when((ctx_ref[0] & 1) == core)
        def _():
            after = chip * jnp.exp(wide_log(logs_of(first), spread_ref[...])) + state_of(first)
            both = (chip.astype(BF16), after.astype(BF16))
            keep_ref[...] = both[mine]
            send_ref[...] = both[other]


def local_kernel(groups, part_index, gate_hbm, c_hbm, w_hbm, x_ref, b_ref, step_ref, decay_ref, skip_ref, after_ref, *refs):
    if part_index:
        refs = refs[5:]
    mixed_ref, scale_ref, c_ref, state_ref, before_ref, w_ref, token_ref, gate_ref, semaphores = refs
    token_ref[...] = jnp.zeros_like(token_ref)
    channels = x_ref.shape[1]
    heads = step_ref.shape[0]
    width = channels // groups
    chunks = gate_ref.shape[0] // CHUNK
    mine = range(part_index * chunks, (part_index + 1) * chunks)
    own_rows = rows_of(part_index, chunks * CHUNK)
    small = load([(c_hbm.at[own_rows, :], c_ref.at[own_rows, :])], semaphores)
    gates = [(gate_hbm.at[rows_of(n), :], gate_ref.at[rows_of(n - mine[0]), :]) for n in mine]
    gates = load(gates, semaphores.at[pl.ds(1, chunks)])
    size = channels // WEIGHT_COPIES
    columns = rows_of(part_index, w_ref.shape[1])
    weights = [(w_hbm.at[rows_of(n, size), columns], w_ref.at[rows_of(n, size), :]) for n in range(WEIGHT_COPIES)]
    weights = load(weights, semaphores.at[pl.ds(1 + chunks, WEIGHT_COPIES)])

    spread = head_map(channels)
    row = lax.broadcasted_iota(jnp.int32, (CHUNK, CHUNK), 0)
    column = lax.broadcasted_iota(jnp.int32, (CHUNK, CHUNK), 1)
    lane = lax.broadcasted_iota(jnp.int32, (heads, CHUNK), 1)
    skip = jnp.concatenate([pieces(skip_ref[...], 0), jnp.zeros((EXTRA, 128 - heads), F32)], axis=1)
    skip = wide_log(skip.astype(BF16), spread)
    before = jnp.zeros((heads, 1), F32)
    state = [jnp.zeros((STATE, width), F32)] * groups
    if part_index:
        before = before_ref[:, 0:1]
        state = [state_ref[:, rows_of(g, width)] for g in range(groups)]
    small[0].wait()
    for n, running in zip(mine, running_sums(decay_ref[:, own_rows])):
        here = rows_of(n)
        middle, total = running[:, MIDDLE : MIDDLE + 1], running[:, CHUNK - 1 :]
        inner = running - middle
        factors = jnp.exp(jnp.where(lane == 0, total, jnp.where(lane == 1, total - middle, middle)))
        factors = jnp.concatenate(
            [
                by_row(step_ref[:, here] * jnp.exp(-inner)),
                by_row(jnp.exp(inner)),
                by_row(jnp.exp(before + running)),
                by_row(factors)[:EXTRA],
            ],
            axis=0,
        )
        before = before + total
        gates[n - mine[0]].wait()
        for g in range(groups):
            cut = slice(g * width, (g + 1) * width)
            part = slice(g * STATE, (g + 1) * STATE)
            wide = dot(factors, spread[:, cut])
            to_state, to_fresh, to_middle = (wide[3 * CHUNK + n : 3 * CHUNK + n + 1] for n in range(3))
            x = x_ref[here, cut].astype(F32)
            weighted = (x * wide[:CHUNK]).astype(BF16)
            started = jnp.concatenate([weighted, (state[g] * to_middle).astype(BF16)], axis=0)
            scores = lax.dot_general(
                c_ref[here, part], b_ref[here, part], (((1,), (1,)), ((), ())), preferred_element_type=F32
            )
            scores = jnp.where(row >= column, scores, 0.0).astype(BF16)
            within = dot(jnp.concatenate([scores, c_ref[here, part]], axis=1), started)
            if n + 1 < x_ref.shape[0] // CHUNK:
                fresh = lax.dot_general(
                    b_ref[here, part], weighted, (((0,), (0,)), ((), ())), preferred_element_type=F32
                )
                state[g] = state[g] * to_state + fresh * to_fresh
            gate = gate_ref[rows_of(n - mine[0]), cut].astype(F32)
            gate = gate / (1.0 + jnp.exp(-gate))
            mixed_ref[here, cut] = (within * wide[CHUNK : 2 * CHUNK] + x * skip[:, cut]) * gate
            scale_ref[here, cut] = wide[2 * CHUNK : 3 * CHUNK] * gate
    before_ref[...] = jnp.broadcast_to(before, before_ref.shape)
    for g in range(groups):
        state_ref[:, rows_of(g, width)] = state[g]
    for copy in weights:
        copy.wait()


def norm_group(mixed, scale, c_rows, gain, state):
    whole = mixed + scale * dot(c_rows, state)
    meansq = jnp.mean(whole * whole, axis=1, keepdims=True)
    return (whole * lax.rsqrt(meansq + 1e-05) * gain).astype(BF16)


def norm_rows(groups, state, mixed, scale, c_rows, gain):
    width = mixed.shape[1] // groups
    parts = []
    for g in range(groups):
        cut = slice(g * width, (g + 1) * width)
        of_state = c_rows[:, g * STATE : (g + 1) * STATE]
        parts.append(norm_group(mixed[:, cut], scale[:, cut], of_state, gain[:, cut], state[:, cut]))
    return parts


def fill_state(ctx_ref, keep_ref, recv_ref, state):
    half = keep_ref.shape[1]
    for core in range(2):

        @pl.when((ctx_ref[0] & 1) == core)
        def _():
            state[:, core * half : (core + 1) * half] = keep_ref[...]
            state[:, (1 - core) * half : (2 - core) * half] = recv_ref[...]


def block_at(here, position, count, size):
    block = 0
    for i in range(count):
        block = jnp.where(here == i, block_order(i, count)[position], block)
    return pl.ds(pl.multiple_of(block * size, size), size)


def one_group(group, here, mixed_ref, scale_ref, c_ref, gain_ref, state):
    width = state.shape[1]
    cut = pl.ds(pl.multiple_of(group * width, width), width)
    part = pl.ds(pl.multiple_of(group * STATE, STATE), STATE)
    return norm_group(mixed_ref[here, cut], scale_ref[here, cut], c_ref[here, part], gain_ref[:, cut], state)


def times_rows(group, normed, w_ref, columns):
    width = normed.shape[1]
    return dot(normed, w_ref[pl.ds(pl.multiple_of(group * width, width), width), :columns])


def own_group_kernel(count, ctx_ref, here_ref, mixed_ref, scale_ref, c_ref, gain_ref, w_ref, keep_ref, normed_ref, product_ref):
    size, columns = product_ref.shape
    here = block_at(here_ref[0], 0, count, size)
    group = ctx_ref[0] & 1
    normed = one_group(group, here, mixed_ref, scale_ref, c_ref, gain_ref, keep_ref[...])
    normed_ref[...] = normed
    product_ref[...] = times_rows(group, normed, w_ref, columns)


def other_group_kernel(count, ctx_ref, here_ref, mixed_ref, scale_ref, c_ref, gain_ref, w_ref, recv_ref, own_ref, product_ref,
                       out_ref, normed_ref):
    size, columns = product_ref.shape
    here = block_at(here_ref[0], 0, count, size)
    group = 1 - (ctx_ref[0] & 1)
    normed = one_group(group, here, mixed_ref, scale_ref, c_ref, gain_ref, recv_ref[...])
    out_ref[...] = (product_ref[...] + times_rows(group, normed, w_ref, columns)).astype(BF16)
    width = normed.shape[1]
    for g in range(2):

        @pl.when(group == g)
        def _():
            normed_ref[:, rows_of(g, width)] = normed
            normed_ref[:, rows_of(1 - g, width)] = own_ref[...]


def both_groups_kernel(groups, count, ctx_ref, here_ref, mixed_ref, scale_ref, c_ref, gain_ref, w_ref, keep_ref, recv_ref,
                       out_ref, normed_ref, state):
    fill_state(ctx_ref, keep_ref, recv_ref, state)
    width = normed_ref.shape[1] // groups
    here = block_at(here_ref[0], 0, count, normed_ref.shape[0])
    rows = norm_rows(groups, state, mixed_ref.at[here, :], scale_ref.at[here, :], c_ref.at[here, :], gain_ref)
    for g, part in enumerate(rows):
        normed_ref[:, g * width : (g + 1) * width] = part
    out_ref[...] = dot(normed_ref[...], w_ref[:, : out_ref.shape[1]]).astype(BF16)


def project_kernel(start, normed_ref, w_ref, *outs):
    for ref in outs:
        columns = ref.shape[1]
        ref[...] = dot(normed_ref[...], w_ref[:, start : start + columns]).astype(BF16)
        start += columns


def rest_kernel(groups, count, ctx_ref, here_ref, mixed_ref, scale_ref, c_ref, gain_ref, wa_ref, wb_ref, keep_ref, recv_ref,
                *refs):
    *first, out_ref, state, normed = refs
    size, piece = first[0].shape
    half = wa_ref.shape[1]
    blocks = [block_at(here_ref[0], n, count, size) for n in range(count)]
    for n, ref in enumerate(first):
        out_ref[blocks[0], n * piece : (n + 1) * piece] = ref[...]
    fill_state(ctx_ref, keep_ref, recv_ref, state)
    width = normed.shape[1] // groups
    for n in range(1, count):
        here = blocks[n]
        rows = norm_rows(groups, state, mixed_ref.at[here, :], scale_ref.at[here, :], c_ref.at[here, :], gain_ref)
        for g, part in enumerate(rows):
            normed[(n - 1) * size : n * size, g * width : (g + 1) * width] = part

    for first_column, w_ref in ((0, wa_ref), (half, wb_ref)):

        @pl.loop(0, half // COLUMN_TILE)
        def _(j):
            cut = pl.ds(pl.multiple_of(j * COLUMN_TILE, COLUMN_TILE), COLUMN_TILE)
            to = pl.ds(pl.multiple_of(first_column + j * COLUMN_TILE, COLUMN_TILE), COLUMN_TILE)
            product = dot(normed[...], w_ref[:, cut]).astype(BF16)
            for n in range(1, count):
                out_ref[blocks[n], to] = product[(n - 1) * size : n * size]


def pass_kernel(count, step, column, here_ref, *refs):
    sums_ref, even_out, odd_out = refs[-3:]
    arrived = refs[:-3]
    size, width = even_out.shape
    here = here_ref[0]

    def send(shift, came, out):
        block = jnp.clip(here + shift, 0, count - 1)
        rows = pl.ds(pl.multiple_of(block * size, size), size)
        own = sums_ref[rows, column : column + width].astype(F32)
        for ref in came:
            own = own + ref[...].astype(F32)
        out[...] = own.astype(BF16)

    for parity, to_right, to_left, from_left, from_right in (
        (0, even_out, odd_out, arrived[1:], arrived[:1]),
        (1, odd_out, even_out, arrived[:1], arrived[1:]),
    ):

        @pl.when((here & 1) == parity)
        def _():
            send(count - step, from_left, to_right)
            send(step - count, from_right, to_left)


def sum_kernel(column, here_ref, even_ref, odd_ref, sums_ref, *refs):
    out_hbm, total, semaphores = refs[-3:]
    size, width = even_ref.shape
    rows = pl.ds(pl.multiple_of(here_ref[0] * size, size), size)
    copies = []
    for n in range(SUM_COPIES):
        part = rows_of(n, size // SUM_COPIES)
        own = sums_ref[rows, column : column + width][part, :].astype(F32)
        total[part, :] = (own + even_ref[part, :].astype(F32) + odd_ref[part, :].astype(F32)).astype(BF16)
        to = out_hbm.at[part, column : column + width]
        copies.extend(load([(total.at[part, :], to)], semaphores.at[pl.ds(n, 1)]))
    for copy in copies:
        copy.wait()


def block_order(here, count):
    order = []
    for step in range(1, count):
        for block, sends in ((count - step + here, here <= step - 1), (step - count + here, here >= count - step)):
            if sends and block not in order:
                order.append(block)
    return order + [b for b in range(count) if b not in order]


def in_vmem(kernel, name, ins, outs, scratch=(), vmem=4, flops=1, result=None, aliases=None):
    vm = pl.BlockSpec(memory_space=pltpu.VMEM)
    specs, arrays = [], []
    for v in ins:
        if isinstance(v, tuple):
            specs.append(pl.BlockSpec(memory_space=pltpu.HBM))
            arrays.append(pltpu.with_memory_space_constraint(v[0], pltpu.HBM))
        elif v.dtype == jnp.int32:
            specs.append(pl.BlockSpec(memory_space=pltpu.SMEM))
            arrays.append(v)
        else:
            specs.append(vm)
            arrays.append(pltpu.with_memory_space_constraint(v, pltpu.VMEM))
    in_hbm = outs is None
    return pl.pallas_call(
        kernel,
        in_specs=specs,
        out_specs=[pl.BlockSpec(memory_space=pltpu.HBM)] if in_hbm else [vm for _ in outs],
        out_shape=[pltpu.HBM(*result)] if in_hbm else [pltpu.VMEM(shape, kind) for shape, kind in outs],
        scratch_shapes=list(scratch),
        input_output_aliases={len(ins) - 1: 0} if in_hbm and isinstance(ins[-1], tuple) else aliases or {},
        compiler_params=pltpu.CompilerParams(vmem_limit_bytes=vmem * 2**20),
        cost_estimate=pl.CostEstimate(flops=flops, bytes_accessed=1, transcendentals=0),
        name=name,
    )(*arrays)


def line_reduce(first, partial_sums, here, size, columns):
    count = lax.axis_size("tp")
    width = columns // PARTS
    block = ((size, width), BF16)
    even_edges = [(i, i ^ 1) for i in range(count)]
    odd_edges = [(i, ((i + 1) ^ 1) - 1) for i in range(1, count - 1)]
    arrived = [()] * PARTS
    for step in range(1, count):
        for half in range(PARTS):
            if step == 1:
                arrived[half] = (lax.ppermute(first[half], "tp", even_edges),)
                continue
            even, odd = in_vmem(
                partial(pass_kernel, count, step, half * width), "pass_on", (here, *arrived[half], partial_sums), (block, block)
            )
            arrived[half] = (lax.ppermute(even, "tp", even_edges), lax.ppermute(odd, "tp", odd_edges))
    out = ()
    for half in range(PARTS):
        ins = (here, *arrived[half], partial_sums, *out)
        scratch = [pltpu.VMEM((size, width), BF16), pltpu.SemaphoreType.DMA((SUM_COPIES,))]
        kernel = partial(sum_kernel, half * width)
        out = (tuple(in_vmem(kernel, "sum_up", ins, None, scratch, result=((size, columns), BF16))),)
    return out[0][0]


def on_device(x_in, gate_z, b_in, c_in, step_size, log_decay, skip, norm_gain, out_weight):
    rows, channels = x_in.shape
    heads = step_size.shape[1]
    groups = b_in.shape[1] // STATE
    chunks = rows // CHUNK
    columns = out_weight.shape[1]
    half = channels // 2
    devices = lax.axis_size("ctx")
    chips = devices // 2
    count = lax.axis_size("tp")
    size = rows // count
    ctx = lax.axis_index("ctx").astype(jnp.int32).reshape(1)
    here = lax.axis_index("tp").astype(jnp.int32).reshape(1)
    message = ((half + EXTRA, 128), BF16)
    whole = ((rows, channels), F32)
    by_head = ((heads, rows), F32)
    maps = ((rows, groups * STATE), BF16)
    weighted = pltpu.VMEM((rows, half), BF16)

    send, x_here, b_here, step, decay, spread = in_vmem(
        partial(send_kernel, groups),
        "end_state_sent",
        (ctx, here, (x_in,), (b_in,), (step_size.T,), (log_decay.T,)),
        (message, ((rows, channels), BF16), maps, by_head, by_head, ((128, half), BF16)),
        scratch=[weighted, pltpu.SemaphoreType.DMA((4 + chunks,))],
        vmem=6,
    )
    swap = [(i, i ^ 1) for i in range(devices)]
    sibling = lax.ppermute(send, "ctx", swap)
    (own,) = in_vmem(
        partial(keep_kernel, groups), "end_state_kept", (ctx, x_here, b_here, step, decay, spread), (message,), [weighted],
        vmem=6, flops=10**9,
    )
    piece = ((half // PIECES + EXTRA, 128), BF16)
    totals = in_vmem(pair_kernel, "pair", (ctx, spread, own, sibling), (piece,) * PIECES)
    levels = chips.bit_length() - 1

    def swap_chips(level, blocks):
        return [lax.ppermute(v, "ctx", [(i, i ^ (2 << level)) for i in range(devices)]) for v in blocks]

    def local_part(part_index, after, carried):
        return in_vmem(
            partial(local_kernel, groups, part_index),
            "local_part",
            ((gate_z,), (c_in,), (out_weight,), x_here, b_here, step, decay, skip.reshape(1, heads), after, *carried),
            (
                whole,
                whole,
                maps,
                ((STATE, channels), F32),
                ((heads, 128), F32),
                ((channels, columns // 2), BF16),
                ((EXTRA, 128), BF16),
            ),
            scratch=[
                pltpu.VMEM((rows // 2, channels), BF16),
                pltpu.SemaphoreType.DMA((1 + chunks // 2 + WEIGHT_COPIES,)),
            ],
            vmem=10,
            flops=4 * 10**9,
            aliases={9 + n: n for n in range(len(carried))},
        )

    received = swap_chips(0, totals)
    *carried, weight_a, token = local_part(0, totals[-1], ())
    arrived = list(received)
    for level in range(1, levels):
        folded = []
        for n in range(PIECES):
            kernel = partial(fold_kernel, level - 1, n)
            after = folded[-1] if folded else token
            folded.extend(in_vmem(kernel, "fold", (ctx, after, spread, totals[n], received[n]), (piece,)))
        totals = folded
        received = swap_chips(level, totals)
        arrived.extend(received)
    mixed, scale, c_here, _, _, weight_b, token = local_part(1, totals[-1], carried)
    state = ((STATE, half), BF16)
    keep, send = in_vmem(
        partial(last_kernel, levels), "incoming", (ctx, token, spread, own, sibling, *arrived), (state, state)
    )
    recv = lax.ppermute(send, "ctx", swap)

    gain = norm_gain.reshape(1, channels)
    width = columns // PARTS
    piece = ((size, width), BF16)
    row_block = ((size, channels), BF16)
    whole_state = pltpu.VMEM((STATE, channels), BF16)
    inputs = (ctx, here, mixed, scale, c_here, gain, weight_a)
    if groups == 2:
        own_group, product = in_vmem(
            partial(own_group_kernel, count), "own_group", (*inputs, keep), (((size, half), BF16), ((size, width), F32)),
            flops=10**9,
        )
        first, normed = in_vmem(
            partial(other_group_kernel, count), "other_group", (*inputs, recv, own_group, product), (piece, row_block)
        )
    else:
        first, normed = in_vmem(
            partial(both_groups_kernel, groups, count), "both_groups", (*inputs, keep, recv), (piece, row_block), [whole_state]
        )
    pieces_out = [first]
    for start, weight, number in ((1, weight_a, PARTS // 2 - 1), (0, weight_b, PARTS // 2)):
        kernel = partial(project_kernel, start * width)
        pieces_out.extend(in_vmem(kernel, "first_block_rest", (normed, weight), (piece,) * number))
    (partial_sums,) = in_vmem(
        partial(rest_kernel, groups, count),
        "other_blocks",
        (*inputs, weight_b, keep, recv, *pieces_out),
        (((rows, columns), BF16),),
        [whole_state, pltpu.VMEM((rows - size, channels), BF16)],
        vmem=6,
    )
    return line_reduce(pieces_out, partial_sums, here, size, columns)


def solution(mesh):
    placed = (
        P("ctx", "tp"),
        P("ctx", "tp"),
        P("ctx", "tp"),
        P("ctx", "tp"),
        P("ctx", "tp"),
        P("ctx", "tp"),
        P("tp"),
        P("tp"),
        P("tp", None),
    )
    return jax.shard_map(
        on_device, mesh=mesh, in_specs=placed, out_specs=P(("ctx", "tp"), None), check_vma=False
    )
```

```python
from functools import partial

import jax
import jax.numpy as jnp
from jax import lax
from jax.experimental import pallas as pl
from jax.experimental.pallas import tpu as pltpu
from jax.sharding import PartitionSpec as P

HEAD_DIM = 64
STATE = 128
CHUNK = 128
MIDDLE = CHUNK // 2 - 1
EXTRA = 16
COLUMN_TILE = 512
PARTS = 4
SUM_COPIES = 4
F32 = jnp.float32
BF16 = jnp.bfloat16


def dot(a, b):
    return jnp.dot(a, b, preferred_element_type=F32)


def dot_exact(a, b):
    return jnp.dot(a, b, preferred_element_type=F32, precision=lax.Precision.HIGHEST)


def head_map(channels):
    head = lax.broadcasted_iota(jnp.int32, (128, channels), 0) & 63
    place = lax.broadcasted_iota(jnp.int32, (128, channels), 1) >> 6
    return jnp.where(head == place, 1.0, 0.0).astype(BF16)


def padded(values):
    return jnp.concatenate([values, jnp.zeros((64 - values.shape[0], values.shape[1]), F32)], axis=0)


def by_row(values):
    high = values.astype(BF16).astype(F32)
    return jnp.transpose(jnp.concatenate([padded(high), padded(values - high)], axis=0)).astype(BF16)


def pieces(values, axis):
    first = values.astype(BF16).astype(F32)
    second = (values - first).astype(BF16).astype(F32)
    third = values - first - second
    shape = (EXTRA, values.shape[1]) if axis == 0 else (values.shape[0], 128)
    at = lax.broadcasted_iota(jnp.int32, shape, axis)
    return jnp.where(at == 0, first, jnp.where(at == 1, second, jnp.where(at == 2, third, 0.0)))


def running_sums(decay):
    row = lax.broadcasted_iota(jnp.int32, (CHUNK, CHUNK), 0)
    column = lax.broadcasted_iota(jnp.int32, (CHUNK, CHUNK), 1)
    upper = jnp.where(row <= column, 1.0, 0.0)
    return [dot_exact(decay[:, rows_of(n)], upper) for n in range(decay.shape[1] // CHUNK)]


def load(pairs, semaphores):
    copies = [pltpu.make_async_copy(src, dst, semaphores.at[n]) for n, (src, dst) in enumerate(pairs)]
    for copy in copies:
        copy.start()
    return copies


def rows_of(chunk, size=CHUNK):
    return slice(chunk * size, (chunk + 1) * size)


def put_message(ref, state, logs):
    for j in range(state.shape[1] // 128):
        ref[j * STATE : (j + 1) * STATE, :] = state[:, j * 128 : (j + 1) * 128].astype(BF16)
    ref[state.shape[1] :, :] = logs.astype(BF16)


def state_of(ref):
    count = (ref.shape[0] - EXTRA) // STATE
    return jnp.concatenate([ref[j * STATE : (j + 1) * STATE, :] for j in range(count)], axis=1).astype(F32)


def logs_of(ref):
    return ref[ref.shape[0] - EXTRA :, :]


def wide_log(logs, spread):
    return jnp.sum(dot(logs, spread), axis=0, keepdims=True)


def end_state(groups, half, x_ref, b_ref, step_ref, decay_ref, weighted, message_ref, spread, x_copies=(), b_copies=()):
    rows, width = weighted.shape
    heads = width // HEAD_DIM
    of_heads = pl.ds(pl.multiple_of(half * heads, heads), heads)
    of_channels = pl.ds(pl.multiple_of(half * width, width), width)
    of_group = pl.ds(pl.multiple_of((half * groups // 2) * STATE, STATE), STATE)
    before, running = jnp.zeros((heads, 1), F32), []
    for sums in running_sums(decay_ref[of_heads, :]):
        running.append(before + sums)
        before = before + sums[:, CHUNK - 1 :]
    factors = [by_row(step_ref[of_heads, rows_of(n)] * jnp.exp(before - sums)) for n, sums in enumerate(running)]
    for n, factor in enumerate(factors):
        here = rows_of(n)
        factor = dot(factor, spread)
        for copy in x_copies[n : n + 1]:
            copy.wait()
        weighted[here, :] = (x_ref[here, of_channels].astype(F32) * factor).astype(BF16)
    for copy in b_copies:
        copy.wait()
    state = lax.dot_general(
        b_ref[:, of_group], weighted[...], (((0,), (0,)), ((), ())), preferred_element_type=F32
    )
    logs = jnp.concatenate([pieces(before, 1), jnp.zeros((128 - heads, 128), F32)], axis=0)
    put_message(message_ref, state, jnp.transpose(logs)[:EXTRA])


def send_kernel(groups, ctx_ref, here_ref, x_hbm, b_hbm, step_hbm, decay_hbm, send_ref, x_ref, b_ref, step_ref, decay_ref,
                spread_ref, weighted, semaphores):
    width = weighted.shape[1]
    other = 1 - (ctx_ref[0] & 1)
    first, second = [pl.ds(pl.multiple_of(half * width, width), width) for half in (other, 1 - other)]
    rows = [rows_of(n) for n in range(x_ref.shape[0] // CHUNK)]
    copies = load(
        [(decay_hbm, decay_ref), (step_hbm, step_ref)]
        + [(x_hbm.at[here, first], x_ref.at[here, first]) for here in rows]
        + [(b_hbm, b_ref), (x_hbm.at[:, second], x_ref.at[:, second])],
        semaphores,
    )
    spread = head_map(width)
    spread_ref[...] = spread
    for copy in copies[:2]:
        copy.wait()
    end_state(
        groups, other, x_ref, b_ref, step_ref, decay_ref, weighted, send_ref, spread, copies[2:-2], copies[-2:-1]
    )
    copies[-1].wait()


def weight_copies(w_hbm, refs, first, semaphores):
    return load([(w_hbm.at[:, rows_of(first + n, COLUMN_TILE)], ref) for n, ref in enumerate(refs)], semaphores)


def keep_kernel(groups, tile, ctx_ref, w_hbm, x_ref, b_ref, step_ref, decay_ref, spread_ref, keep_ref, w_ref, weighted,
                semaphores):
    copies = weight_copies(w_hbm, [w_ref], tile, semaphores)
    end_state(groups, ctx_ref[0] & 1, x_ref, b_ref, step_ref, decay_ref, weighted, keep_ref, spread_ref[...])
    for copy in copies:
        copy.wait()


def pair_kernel(ctx_ref, spread_ref, own_ref, sibling_ref, *pieces_refs):
    spread = spread_ref[...]
    own_log, sibling_log = wide_log(logs_of(own_ref), spread), wide_log(logs_of(sibling_ref), spread)
    early = (ctx_ref[0] & 1) == 0
    own_scale = jnp.where(early, jnp.exp(sibling_log), 1.0)
    sibling_scale = jnp.where(early, 1.0, jnp.exp(own_log))
    logs = logs_of(own_ref).astype(F32) + logs_of(sibling_ref).astype(F32)
    logs = pieces(jnp.sum(logs, axis=0, keepdims=True), 0)
    state = state_of(own_ref) * own_scale + state_of(sibling_ref) * sibling_scale
    start = 0
    for ref in pieces_refs:
        width = ref.shape[0] - EXTRA
        put_message(ref, state[:, start : start + width], logs)
        start += width


def is_upper(ctx_ref, level):
    return ((ctx_ref[0] >> (1 + level)) & 1) == 1


def piece_of(spread_ref, start, ref):
    return spread_ref[:, start : start + ref.shape[0] - EXTRA]


def fold_kernel(level, start, ctx_ref, after_ref, spread_ref, total_ref, other_ref, out_ref):
    spread = piece_of(spread_ref, start, total_ref)
    upper = is_upper(ctx_ref, level)
    total_scale = jnp.where(upper, 1.0, jnp.exp(wide_log(logs_of(other_ref), spread)))
    other_scale = jnp.where(upper, jnp.exp(wide_log(logs_of(total_ref), spread)), 1.0)
    logs = logs_of(total_ref).astype(F32) + logs_of(other_ref).astype(F32)
    logs = pieces(jnp.sum(logs, axis=0, keepdims=True), 0)
    put_message(out_ref, state_of(total_ref) * total_scale + state_of(other_ref) * other_scale, logs)


def last_kernel(start, ctx_ref, after_ref, spread_ref, own_ref, sibling_ref, *refs):
    keep_ref, send_ref = refs[-2:]
    spread = piece_of(spread_ref, start, refs[0])
    chip = log = 0.0
    for level, ref in enumerate(refs[:-2]):
        upper = is_upper(ctx_ref, level)
        chip = chip + jnp.where(upper, state_of(ref), 0.0) * jnp.exp(log)
        log = log + jnp.where(upper, wide_log(logs_of(ref), spread), 0.0)
    width = chip.shape[1]
    for core, first, mine, other in ((0, own_ref, 0, 1), (1, sibling_ref, 1, 0)):

        @pl.when((ctx_ref[0] & 1) == core)
        def _():
            piece = state_of(first)[:, start : start + width]
            after = chip * jnp.exp(wide_log(logs_of(first), spread)) + piece
            both = (chip.astype(BF16), after.astype(BF16))
            keep_ref[...] = both[mine]
            send_ref[...] = both[other]


def scan_kernel(groups, chunks, tile, w_hbm, x_ref, b_ref, step_ref, decay_ref, after_ref, *refs):
    first = chunks[0] == 0
    if not first:
        refs = refs[2:]
    rhs_ref, state_ref, token_ref, *w_refs, semaphores = refs
    token_ref[...] = jnp.zeros_like(token_ref)
    copies = weight_copies(w_hbm, w_refs, tile, semaphores)
    channels = x_ref.shape[1]
    heads = step_ref.shape[0]
    width = channels // groups
    spread = head_map(channels)
    lane = lax.broadcasted_iota(jnp.int32, (heads, CHUNK), 1)
    if first:
        state = [jnp.zeros((STATE, width), F32)] * groups
    else:
        state = [state_ref[:, rows_of(g, width)] for g in range(groups)]
    for n in chunks:
        here = rows_of(n)
        (running,) = running_sums(decay_ref[:, here])
        middle, total = running[:, MIDDLE : MIDDLE + 1], running[:, CHUNK - 1 :]
        ends = jnp.exp(jnp.where(lane == 0, total, jnp.where(lane == 1, total - middle, middle)))
        factors = [by_row(step_ref[:, here] * jnp.exp(middle - running)), by_row(ends)[:EXTRA]]
        factors = jnp.concatenate(factors, axis=0)
        start = n * (CHUNK + STATE)
        for g in range(groups):
            cut = rows_of(g, width)
            wide = dot(factors, spread[:, cut])
            to_state, to_fresh, to_middle = (wide[CHUNK + m : CHUNK + m + 1] for m in range(3))
            weighted = (x_ref[here, cut].astype(F32) * wide[:CHUNK]).astype(BF16)
            rhs_ref[start : start + CHUNK, cut] = weighted
            rhs_ref[start + CHUNK : start + CHUNK + STATE, cut] = (state[g] * to_middle).astype(BF16)
            if n + 1 < x_ref.shape[0] // CHUNK:
                fresh = lax.dot_general(
                    b_ref[here, rows_of(g, STATE)], weighted, (((0,), (0,)), ((), ())), preferred_element_type=F32
                )
                state[g] = state[g] * to_state + fresh * to_fresh
    for g in range(groups):
        state_ref[:, rows_of(g, width)] = state[g]
    for copy in copies:
        copy.wait()


def chunk_part(groups, here, rhs_rows, running, before, gate_rows, x_ref, b_ref, c_ref, skip_ref, rhs_ref, mixed_ref, scale_ref,
               out_rows):
    channels = x_ref.shape[1]
    heads = running.shape[0]
    width = channels // groups
    spread = head_map(channels)
    row = lax.broadcasted_iota(jnp.int32, (CHUNK, CHUNK), 0)
    column = lax.broadcasted_iota(jnp.int32, (CHUNK, CHUNK), 1)
    skip = jnp.concatenate([pieces(skip_ref[...], 0), jnp.zeros((EXTRA, 128 - heads), F32)], axis=1)
    skip = wide_log(skip.astype(BF16), spread)
    middle = running[:, MIDDLE : MIDDLE + 1]
    factors = jnp.concatenate([by_row(jnp.exp(running - middle)), by_row(jnp.exp(before + running))], axis=0)
    for g in range(groups):
        cut = rows_of(g, width)
        part = rows_of(g, STATE)
        wide = dot(factors, spread[:, cut])
        scores = lax.dot_general(
            c_ref[here, part], b_ref[here, part], (((1,), (1,)), ((), ())), preferred_element_type=F32
        )
        scores = jnp.where(row >= column, scores, 0.0).astype(BF16)
        within = dot(jnp.concatenate([scores, c_ref[here, part]], axis=1), rhs_ref[rhs_rows, cut])
        gate = gate_rows[:, cut].astype(F32)
        gate = gate * (0.5 * jnp.tanh(0.5 * gate) + 0.5)
        mixed_ref[out_rows, cut] = (within * wide[:CHUNK] + x_ref[here, cut].astype(F32) * skip[:, cut]) * gate
        scale_ref[out_rows, cut] = wide[CHUNK:] * gate


def first_part_kernel(groups, count, tile, here_ref, gate_hbm, c_hbm, w_hbm, x_ref, b_ref, step_ref, decay_ref, skip_ref, rhs_ref,
                      after_ref, mixed_ref, scale_ref, c_ref, token_ref, *refs):
    *w_refs, gate_ref, semaphores = refs
    token_ref[...] = jnp.zeros_like(token_ref)
    chunk, _ = first_chunk(here_ref, count, x_ref.shape[0] // count)
    here = pl.ds(pl.multiple_of(chunk * CHUNK, CHUNK), CHUNK)
    copies = load([(c_hbm, c_ref), (gate_hbm.at[here, :], gate_ref)], semaphores)
    weights = weight_copies(w_hbm, w_refs, tile, semaphores.at[pl.ds(2, len(w_refs))])
    lane = lax.broadcasted_iota(jnp.int32, decay_ref.shape, 1)
    before = jnp.sum(jnp.where(lane < chunk * CHUNK, decay_ref[...], 0.0), axis=1, keepdims=True)
    (running,) = running_sums(decay_ref[:, here])
    rhs_rows = pl.ds(pl.multiple_of(chunk * (CHUNK + STATE), CHUNK + STATE), CHUNK + STATE)
    for copy in copies:
        copy.wait()
    chunk_part(groups, here, rhs_rows, running, before, gate_ref, x_ref, b_ref, c_ref, skip_ref, rhs_ref, mixed_ref, scale_ref,
               slice(None))
    for copy in weights:
        copy.wait()


def norm_group(mixed, scale, c_rows, gain, state):
    whole = mixed + scale * dot(c_rows, state)
    meansq = jnp.mean(whole * whole, axis=1, keepdims=True)
    return (whole * lax.rsqrt(meansq + 1e-05) * gain).astype(BF16)


def norm_rows(groups, state, mixed, scale, c_rows, gain):
    width = mixed.shape[1] // groups
    parts = []
    for g in range(groups):
        cut = slice(g * width, (g + 1) * width)
        of_state = c_rows[:, g * STATE : (g + 1) * STATE]
        parts.append(norm_group(mixed[:, cut], scale[:, cut], of_state, gain[:, cut], state[:, cut]))
    return parts


def across(refs):
    return jnp.concatenate([ref[...] for ref in refs], axis=1)


def fill_state(ctx_ref, keep_refs, recv_refs, state):
    half = state.shape[1] // 2
    for core in range(2):

        @pl.when((ctx_ref[0] & 1) == core)
        def _():
            state[:, core * half : (core + 1) * half] = across(keep_refs)
            state[:, (1 - core) * half : (2 - core) * half] = across(recv_refs)


def block_at(here, position, count):
    block = 0
    for i in range(count):
        block = jnp.where(here == i, block_order(i, count)[position], block)
    return block


def rows_at(block, size):
    return pl.ds(pl.multiple_of(block * size, size), size)


def first_chunk(here_ref, count, size):
    start = block_at(here_ref[0], 0, count) * size
    chunk = start // CHUNK
    return chunk, pl.ds(pl.multiple_of(start - chunk * CHUNK, min(size, CHUNK)), size)


def one_group(group, count, here_ref, mixed_ref, scale_ref, c_ref, gain_ref, state):
    size = c_ref.shape[0] // count
    width = state.shape[1]
    cut = pl.ds(pl.multiple_of(group * width, width), width)
    part = pl.ds(pl.multiple_of(group * STATE, STATE), STATE)
    _, rows = first_chunk(here_ref, count, size)
    c_rows = c_ref[rows_at(block_at(here_ref[0], 0, count), size), part]
    return norm_group(mixed_ref[rows, cut], scale_ref[rows, cut], c_rows, gain_ref[:, cut], state)


def times_rows(group, normed, w_refs):
    width = normed.shape[1]
    rows = pl.ds(pl.multiple_of(group * width, width), width)
    return jnp.concatenate([dot(normed, ref[rows, :]) for ref in w_refs], axis=1)


def own_group_kernel(count, tiles, ctx_ref, here_ref, mixed_ref, scale_ref, c_ref, gain_ref, *refs):
    *keep_refs, normed_ref, product_ref = refs[tiles:]
    group = ctx_ref[0] & 1
    normed = one_group(group, count, here_ref, mixed_ref, scale_ref, c_ref, gain_ref, across(keep_refs))
    normed_ref[...] = normed
    product_ref[...] = times_rows(group, normed, refs[:tiles])


def other_group_kernel(count, tiles, ctx_ref, here_ref, mixed_ref, scale_ref, c_ref, gain_ref, *refs):
    *recv_refs, own_ref, product_ref, out_ref, normed_ref = refs[tiles:]
    group = 1 - (ctx_ref[0] & 1)
    normed = one_group(group, count, here_ref, mixed_ref, scale_ref, c_ref, gain_ref, across(recv_refs))
    out_ref[...] = (product_ref[...] + times_rows(group, normed, refs[:tiles])).astype(BF16)
    width = normed.shape[1]
    for g in range(2):

        @pl.when(group == g)
        def _():
            normed_ref[:, rows_of(g, width)] = normed
            normed_ref[:, rows_of(1 - g, width)] = own_ref[...]


def both_groups_kernel(groups, count, tiles, ctx_ref, here_ref, mixed_ref, scale_ref, c_ref, gain_ref, *refs):
    *state_refs, out_ref, normed_ref, state = refs[tiles:]
    fill_state(ctx_ref, state_refs[: len(state_refs) // 2], state_refs[len(state_refs) // 2 :], state)
    size = normed_ref.shape[0]
    width = normed_ref.shape[1] // groups
    _, rows = first_chunk(here_ref, count, size)
    c_rows = c_ref.at[rows_at(block_at(here_ref[0], 0, count), size), :]
    parts = norm_rows(groups, state, mixed_ref.at[rows, :], scale_ref.at[rows, :], c_rows, gain_ref)
    for g, part in enumerate(parts):
        normed_ref[:, g * width : (g + 1) * width] = part
    for n, ref in enumerate(refs[:tiles]):
        out_ref[:, rows_of(n, COLUMN_TILE)] = dot(normed_ref[...], ref[...]).astype(BF16)


def project_kernel(tiles, normed_ref, *refs):
    outs = refs[tiles:]
    for n, ref in enumerate(refs[:tiles]):
        out, column = divmod(n * COLUMN_TILE, outs[0].shape[1])
        outs[out][:, column : column + COLUMN_TILE] = dot(normed_ref[...], ref[...]).astype(BF16)


def rest_kernel(groups, count, tiles, ctx_ref, here_ref, gate_hbm, x_ref, b_ref, step_ref, decay_ref, skip_ref, rhs_ref, c_ref,
                first_mixed_ref, first_scale_ref, gain_ref, *refs):
    w_refs = refs[:tiles]
    *inputs, out_ref, state, normed, mixed_ref, scale_ref, gate_ref, semaphores = refs[tiles:]
    state_refs, first = inputs[:-PARTS], inputs[-PARTS:]
    size, piece = first[0].shape
    chunks = x_ref.shape[0] // CHUNK
    gates = [(gate_hbm.at[rows_of(n), :], gate_ref.at[rows_of(n), :]) for n in range(chunks)]
    gates = load(gates, semaphores)
    blocks = [rows_at(block_at(here_ref[0], n, count), size) for n in range(count)]
    for n, ref in enumerate(first):
        out_ref[blocks[0], n * piece : (n + 1) * piece] = ref[...]
    fill_state(ctx_ref, state_refs[: len(state_refs) // 2], state_refs[len(state_refs) // 2 :], state)
    done, _ = first_chunk(here_ref, count, size)
    before = jnp.zeros((decay_ref.shape[0], 1), F32)
    for n, running in enumerate(running_sums(decay_ref[...])):
        here = rows_of(n)
        gates[n].wait()

        @pl.when(done == n)
        def _():
            mixed_ref[here, :] = first_mixed_ref[...]
            scale_ref[here, :] = first_scale_ref[...]

        @pl.when(done != n)
        def _():
            chunk_part(groups, here, rows_of(n, CHUNK + STATE), running, before, gate_ref.at[here, :], x_ref, b_ref, c_ref,
                       skip_ref, rhs_ref, mixed_ref, scale_ref, here)

        before = before + running[:, CHUNK - 1 :]
    width = normed.shape[1] // groups
    for n in range(1, count):
        here = blocks[n]
        rows = norm_rows(groups, state, mixed_ref.at[here, :], scale_ref.at[here, :], c_ref.at[here, :], gain_ref)
        for g, part in enumerate(rows):
            normed[(n - 1) * size : n * size, g * width : (g + 1) * width] = part
    for tile, ref in enumerate(w_refs):
        product = dot(normed[...], ref[...]).astype(BF16)
        for n in range(1, count):
            out_ref[blocks[n], rows_of(tile, COLUMN_TILE)] = product[(n - 1) * size : n * size]


def pass_kernel(count, step, column, here_ref, *refs):
    sums_ref, even_out, odd_out = refs[-3:]
    arrived = refs[:-3]
    size, width = even_out.shape
    here = here_ref[0]

    def send(shift, came, out):
        block = jnp.clip(here + shift, 0, count - 1)
        rows = pl.ds(pl.multiple_of(block * size, size), size)
        own = sums_ref[rows, column : column + width].astype(F32)
        for ref in came:
            own = own + ref[...].astype(F32)
        out[...] = own.astype(BF16)

    for parity, to_right, to_left, from_left, from_right in (
        (0, even_out, odd_out, arrived[1:], arrived[:1]),
        (1, odd_out, even_out, arrived[:1], arrived[1:]),
    ):

        @pl.when((here & 1) == parity)
        def _():
            send(count - step, from_left, to_right)
            send(step - count, from_right, to_left)


def sum_kernel(column, here_ref, even_ref, odd_ref, sums_ref, *refs):
    out_hbm, total, semaphores = refs[-3:]
    size, width = even_ref.shape
    rows = pl.ds(pl.multiple_of(here_ref[0] * size, size), size)
    copies = []
    for n in range(SUM_COPIES):
        part = rows_of(n, size // SUM_COPIES)
        own = sums_ref[rows, column : column + width][part, :].astype(F32)
        total[part, :] = (own + even_ref[part, :].astype(F32) + odd_ref[part, :].astype(F32)).astype(BF16)
        to = out_hbm.at[part, column : column + width]
        copies.extend(load([(total.at[part, :], to)], semaphores.at[pl.ds(n, 1)]))
    for copy in copies:
        copy.wait()


def block_order(here, count):
    order = []
    for step in range(1, count):
        for block, sends in ((count - step + here, here <= step - 1), (step - count + here, here >= count - step)):
            if sends and block not in order:
                order.append(block)
    return order + [b for b in range(count) if b not in order]


def in_vmem(kernel, name, ins, outs, scratch=(), vmem=4, flops=1, result=None, aliases=None):
    vm = pl.BlockSpec(memory_space=pltpu.VMEM)
    specs, arrays = [], []
    for v in ins:
        if isinstance(v, tuple):
            specs.append(pl.BlockSpec(memory_space=pltpu.HBM))
            arrays.append(pltpu.with_memory_space_constraint(v[0], pltpu.HBM))
        elif v.dtype == jnp.int32:
            specs.append(pl.BlockSpec(memory_space=pltpu.SMEM))
            arrays.append(v)
        else:
            specs.append(vm)
            arrays.append(pltpu.with_memory_space_constraint(v, pltpu.VMEM))
    in_hbm = outs is None
    return pl.pallas_call(
        kernel,
        in_specs=specs,
        out_specs=[pl.BlockSpec(memory_space=pltpu.HBM)] if in_hbm else [vm for _ in outs],
        out_shape=[pltpu.HBM(*result)] if in_hbm else [pltpu.VMEM(shape, kind) for shape, kind in outs],
        scratch_shapes=list(scratch),
        input_output_aliases={len(ins) - 1: 0} if in_hbm and isinstance(ins[-1], tuple) else aliases or {},
        compiler_params=pltpu.CompilerParams(vmem_limit_bytes=vmem * 2**20),
        cost_estimate=pl.CostEstimate(flops=flops, bytes_accessed=1, transcendentals=0),
        name=name,
    )(*arrays)


def line_reduce(first, partial_sums, here, size, columns):
    count = lax.axis_size("tp")
    width = columns // PARTS
    block = ((size, width), BF16)
    even_edges = [(i, i ^ 1) for i in range(count)]
    odd_edges = [(i, ((i + 1) ^ 1) - 1) for i in range(1, count - 1)]
    arrived = [()] * PARTS
    for step in range(1, count):
        for half in range(PARTS):
            if step == 1:
                arrived[half] = (lax.ppermute(first[half], "tp", even_edges),)
                continue
            even, odd = in_vmem(
                partial(pass_kernel, count, step, half * width), "pass_on", (here, *arrived[half], partial_sums), (block, block)
            )
            arrived[half] = (lax.ppermute(even, "tp", even_edges), lax.ppermute(odd, "tp", odd_edges))
    out = ()
    for half in range(PARTS):
        ins = (here, *arrived[half], partial_sums, *out)
        scratch = [pltpu.VMEM((size, width), BF16), pltpu.SemaphoreType.DMA((SUM_COPIES,))]
        kernel = partial(sum_kernel, half * width)
        out = (tuple(in_vmem(kernel, "sum_up", ins, None, scratch, result=((size, columns), BF16))),)
    return out[0][0]


def on_device(x_in, gate_z, b_in, c_in, step_size, log_decay, skip, norm_gain, out_weight):
    rows, channels = x_in.shape
    heads = step_size.shape[1]
    groups = b_in.shape[1] // STATE
    chunks = rows // CHUNK
    columns = out_weight.shape[1]
    half = channels // 2
    devices = lax.axis_size("ctx")
    chips = devices // 2
    count = lax.axis_size("tp")
    size = rows // count
    ctx = lax.axis_index("ctx").astype(jnp.int32).reshape(1)
    here = lax.axis_index("tp").astype(jnp.int32).reshape(1)
    message = ((half + EXTRA, 128), BF16)
    by_head = ((heads, rows), F32)
    maps = ((rows, groups * STATE), BF16)
    weighted = pltpu.VMEM((rows, half), BF16)

    send, x_here, b_here, step, decay, spread = in_vmem(
        partial(send_kernel, groups),
        "end_state_sent",
        (ctx, here, (x_in,), (b_in,), (step_size.T,), (log_decay.T,)),
        (message, ((rows, channels), BF16), maps, by_head, by_head, ((128, half), BF16)),
        scratch=[weighted, pltpu.SemaphoreType.DMA((4 + chunks,))],
        vmem=6,
    )
    swap = [(i, i ^ 1) for i in range(devices)]
    sibling = lax.ppermute(send, "ctx", swap)
    tiles = columns // COLUMN_TILE
    weight = [None] * tiles
    w_tile = ((channels, COLUMN_TILE), BF16)
    token_shape = ((EXTRA, 128), BF16)
    own, weight[-1] = in_vmem(
        partial(keep_kernel, groups, tiles - 1),
        "end_state_kept",
        (ctx, (out_weight,), x_here, b_here, step, decay, spread),
        (message, w_tile),
        [weighted, pltpu.SemaphoreType.DMA((1,))],
        vmem=6,
        flops=10**9,
    )
    blocks = half // 128
    shares = [blocks // 4, (blocks - blocks // 4) // 2]
    shares.append(blocks - sum(shares))
    starts = [128 * sum(shares[:n]) for n in range(len(shares))]
    piece = [((128 * share + EXTRA, 128), BF16) for share in shares]
    totals = in_vmem(pair_kernel, "pair", (ctx, spread, own, sibling), piece)
    levels = chips.bit_length() - 1

    def swap_chips(level, block):
        return lax.ppermute(block, "ctx", [(i, i ^ (2 << level)) for i in range(devices)])

    def scan(mine, tile, number, after, carried):
        outs = (((chunks * (CHUNK + STATE), channels), BF16), ((STATE, channels), F32), token_shape, *(w_tile,) * number)
        rhs, state, token, *w_tiles = in_vmem(
            partial(scan_kernel, groups, mine, tile),
            "chunk_states",
            ((out_weight,), x_here, b_here, step, decay, after, *carried),
            outs,
            scratch=[pltpu.SemaphoreType.DMA((number,))],
            vmem=6,
            flops=2 * 10**9,
            aliases={6 + n: n for n in range(len(carried))},
        )
        weight[tile : tile + number] = w_tiles
        return (rhs, state), token

    received = [swap_chips(0, total) for total in totals]
    arrived = [[block] for block in received]
    middle = chunks // 2
    gaps = [list(range(middle)), [middle], list(range(middle + 1, chunks))]
    carried, after, tile = (), totals[-1], 0
    for level in range(1, levels):
        folded = []
        for n, start in enumerate(starts):
            if level == 1:
                number = 2 if n == 0 else 1
                carried, after = scan(gaps[n], tile, number, after, carried)
                tile += number
            kernel = partial(fold_kernel, level - 1, start)
            folded.extend(in_vmem(kernel, "fold", (ctx, after, spread, totals[n], received[n]), (piece[n],)))
            after = folded[-1]
            received[n] = swap_chips(level, after)
            arrived[n].append(received[n])
        totals = folded
    rhs = carried[0]
    number = tiles - 1 - tile
    chunk_rows = ((CHUNK, channels), F32)
    skip = skip.reshape(1, heads)
    mixed, scale, c_here, token, *w_tiles = in_vmem(
        partial(first_part_kernel, groups, count, tile),
        "first_part",
        (here, (gate_z,), (c_in,), (out_weight,), x_here, b_here, step, decay, skip, rhs, after),
        (chunk_rows, chunk_rows, maps, token_shape, *(w_tile,) * number),
        scratch=[pltpu.VMEM((CHUNK, channels), BF16), pltpu.SemaphoreType.DMA((2 + number,))],
        vmem=6,
        flops=4 * 10**9,
    )
    weight[tile : tiles - 1] = w_tiles
    keep, recv = [], []
    for n, start in enumerate(starts):
        state = ((STATE, 128 * shares[n]), BF16)
        kernel = partial(last_kernel, start)
        mine, send = in_vmem(kernel, "incoming", (ctx, token, spread, own, sibling, *arrived[n]), (state, state))
        keep.append(mine)
        recv.append(lax.ppermute(send, "ctx", swap))

    gain = norm_gain.reshape(1, channels)
    width = columns // PARTS
    part_tiles = width // COLUMN_TILE
    part = ((size, width), BF16)
    row_block = ((size, channels), BF16)
    whole_state = pltpu.VMEM((STATE, channels), BF16)
    inputs = (ctx, here, mixed, scale, c_here, gain, *weight[:part_tiles])
    if groups == 2:
        own_group, product = in_vmem(
            partial(own_group_kernel, count, part_tiles),
            "own_group",
            (*inputs, *keep),
            (((size, half), BF16), ((size, width), F32)),
            flops=10**9,
        )
        first, normed = in_vmem(
            partial(other_group_kernel, count, part_tiles),
            "other_group",
            (*inputs, *recv, own_group, product),
            (part, row_block),
        )
    else:
        first, normed = in_vmem(
            partial(both_groups_kernel, groups, count, part_tiles),
            "both_groups",
            (*inputs, *keep, *recv),
            (part, row_block),
            [whole_state],
        )
    parts = [first]
    for begin, end in ((1, 2), (2, PARTS)):
        mine = weight[begin * part_tiles : end * part_tiles]
        kernel = partial(project_kernel, len(mine))
        parts.extend(in_vmem(kernel, "first_block_rest", (normed, *mine), (part,) * (end - begin)))
    (partial_sums,) = in_vmem(
        partial(rest_kernel, groups, count, tiles),
        "other_blocks",
        (ctx, here, (gate_z,), x_here, b_here, step, decay, skip, rhs, c_here, mixed, scale, gain, *weight, *keep, *recv, *parts),
        (((rows, columns), BF16),),
        [
            whole_state,
            pltpu.VMEM((rows - size, channels), BF16),
            pltpu.VMEM((rows, channels), F32),
            pltpu.VMEM((rows, channels), F32),
            pltpu.VMEM((rows, channels), BF16),
            pltpu.SemaphoreType.DMA((chunks,)),
        ],
        vmem=20,
    )
    return line_reduce(parts, partial_sums, here, size, columns)


def solution(mesh):
    placed = (
        P("ctx", "tp"),
        P("ctx", "tp"),
        P("ctx", "tp"),
        P("ctx", "tp"),
        P("ctx", "tp"),
        P("ctx", "tp"),
        P("tp"),
        P("tp"),
        P("tp", None),
    )
    return jax.shard_map(
        on_device, mesh=mesh, in_specs=placed, out_specs=P(("ctx", "tp"), None), check_vma=False
    )
```

```python
from functools import partial

import jax
import jax.numpy as jnp
from jax import lax
from jax.experimental import pallas as pl
from jax.experimental.pallas import tpu as pltpu
from jax.sharding import PartitionSpec as P

HEAD_DIM = 64
STATE = 128
CHUNK = 128
MIDDLE = CHUNK // 2 - 1
EXTRA = 16
COLUMN_TILE = 512
PARTS = 4
WEIGHT_COPIES = 8
SUM_COPIES = 4
PIECES = 2
F32 = jnp.float32
BF16 = jnp.bfloat16


def dot(a, b):
    return jnp.dot(a, b, preferred_element_type=F32)


def head_map(channels):
    head = lax.broadcasted_iota(jnp.int32, (128, channels), 0) & 63
    place = lax.broadcasted_iota(jnp.int32, (128, channels), 1) >> 6
    return jnp.where(head == place, 1.0, 0.0).astype(BF16)


def padded(values):
    return jnp.concatenate([values, jnp.zeros((64 - values.shape[0], values.shape[1]), F32)], axis=0)


def by_row(values):
    high = values.astype(BF16).astype(F32)
    return jnp.transpose(jnp.concatenate([padded(high), padded(values - high)], axis=0)).astype(BF16)


def pieces(values, axis):
    first = values.astype(BF16).astype(F32)
    second = (values - first).astype(BF16).astype(F32)
    third = values - first - second
    shape = (EXTRA, values.shape[1]) if axis == 0 else (values.shape[0], 128)
    at = lax.broadcasted_iota(jnp.int32, shape, axis)
    return jnp.where(at == 0, first, jnp.where(at == 1, second, jnp.where(at == 2, third, 0.0)))


def running_sums(decay):
    heads, rows = decay.shape
    chunks = rows // CHUNK
    values = jnp.concatenate([decay[:, rows_of(n)] for n in range(chunks)], axis=0)
    first = values.astype(BF16)
    rest = values - first.astype(F32)
    second = rest.astype(BF16)
    third = (rest - second.astype(F32)).astype(BF16)
    row = lax.broadcasted_iota(jnp.int32, (CHUNK, CHUNK), 0)
    column = lax.broadcasted_iota(jnp.int32, (CHUNK, CHUNK), 1)
    upper = jnp.where(row <= column, 1.0, 0.0).astype(BF16)
    sums = dot(jnp.concatenate([first, second, third], axis=1), jnp.concatenate([upper] * 3, axis=0))
    return [sums[rows_of(n, heads)] for n in range(chunks)]


def load(pairs, semaphores):
    copies = [pltpu.make_async_copy(src, dst, semaphores.at[n]) for n, (src, dst) in enumerate(pairs)]
    for copy in copies:
        copy.start()
    return copies


def rows_of(chunk, size=CHUNK):
    return slice(chunk * size, (chunk + 1) * size)


def put_message(ref, state, logs):
    for j in range(state.shape[1] // 128):
        ref[j * STATE : (j + 1) * STATE, :] = state[:, j * 128 : (j + 1) * 128].astype(BF16)
    ref[state.shape[1] :, :] = logs.astype(BF16)


def state_of(ref):
    count = (ref.shape[0] - EXTRA) // STATE
    return jnp.concatenate([ref[j * STATE : (j + 1) * STATE, :] for j in range(count)], axis=1).astype(F32)


def logs_of(ref):
    return ref[ref.shape[0] - EXTRA :, :]


def wide_log(logs, spread):
    return jnp.sum(dot(logs, spread), axis=0, keepdims=True)


def end_state(groups, half, x_ref, b_ref, step_ref, decay_ref, weighted, message_ref, spread, x_copies=(), b_copies=()):
    rows, width = weighted.shape
    heads = width // HEAD_DIM
    of_heads = pl.ds(pl.multiple_of(half * heads, heads), heads)
    of_channels = pl.ds(pl.multiple_of(half * width, width), width)
    of_group = pl.ds(pl.multiple_of((half * groups // 2) * STATE, STATE), STATE)
    before, running = jnp.zeros((heads, 1), F32), []
    for sums in running_sums(decay_ref[of_heads, :]):
        running.append(before + sums)
        before = before + sums[:, CHUNK - 1 :]
    factors = [by_row(step_ref[of_heads, rows_of(n)] * jnp.exp(before - sums)) for n, sums in enumerate(running)]
    for n, factor in enumerate(factors):
        here = rows_of(n)
        factor = dot(factor, spread)
        for copy in x_copies[n : n + 1]:
            copy.wait()
        weighted[here, :] = (x_ref[here, of_channels].astype(F32) * factor).astype(BF16)
    for copy in b_copies:
        copy.wait()
    state = lax.dot_general(
        b_ref[:, of_group], weighted[...], (((0,), (0,)), ((), ())), preferred_element_type=F32
    )
    logs = jnp.concatenate([pieces(before, 1), jnp.zeros((128 - heads, 128), F32)], axis=0)
    put_message(message_ref, state, jnp.transpose(logs)[:EXTRA])


def send_kernel(groups, ctx_ref, here_ref, x_hbm, b_hbm, step_hbm, decay_hbm, send_ref, x_ref, b_ref, step_ref, decay_ref,
                spread_ref, weighted, semaphores):
    width = weighted.shape[1]
    other = 1 - (ctx_ref[0] & 1)
    first, second = [pl.ds(pl.multiple_of(half * width, width), width) for half in (other, 1 - other)]
    rows = [rows_of(n) for n in range(x_ref.shape[0] // CHUNK)]
    copies = load(
        [(decay_hbm, decay_ref), (step_hbm, step_ref)]
        + [(x_hbm.at[here, first], x_ref.at[here, first]) for here in rows]
        + [(b_hbm, b_ref), (x_hbm.at[:, second], x_ref.at[:, second])],
        semaphores,
    )
    spread = head_map(width)
    spread_ref[...] = spread
    for copy in copies[:2]:
        copy.wait()
    end_state(
        groups, other, x_ref, b_ref, step_ref, decay_ref, weighted, send_ref, spread, copies[2:-2], copies[-2:-1]
    )
    copies[-1].wait()


def keep_kernel(groups, ctx_ref, x_ref, b_ref, step_ref, decay_ref, spread_ref, keep_ref, weighted):
    end_state(groups, (ctx_ref[0] & 1), x_ref, b_ref, step_ref, decay_ref, weighted, keep_ref, spread_ref[...])


def pair_kernel(ctx_ref, spread_ref, own_ref, sibling_ref, *pieces_refs):
    spread = spread_ref[...]
    own_log, sibling_log = wide_log(logs_of(own_ref), spread), wide_log(logs_of(sibling_ref), spread)
    early = (ctx_ref[0] & 1) == 0
    own_scale = jnp.where(early, jnp.exp(sibling_log), 1.0)
    sibling_scale = jnp.where(early, 1.0, jnp.exp(own_log))
    logs = logs_of(own_ref).astype(F32) + logs_of(sibling_ref).astype(F32)
    logs = pieces(jnp.sum(logs, axis=0, keepdims=True), 0)
    state = state_of(own_ref) * own_scale + state_of(sibling_ref) * sibling_scale
    width = state.shape[1] // len(pieces_refs)
    for n, ref in enumerate(pieces_refs):
        put_message(ref, state[:, n * width : (n + 1) * width], logs)


def is_upper(ctx_ref, level):
    return ((ctx_ref[0] >> (1 + level)) & 1) == 1


def piece_of(spread_ref, piece, ref):
    width = ref.shape[0] - EXTRA
    return spread_ref[:, piece * width : (piece + 1) * width]


def fold_kernel(level, piece, ctx_ref, after_ref, spread_ref, total_ref, other_ref, out_ref):
    spread = piece_of(spread_ref, piece, total_ref)
    upper = is_upper(ctx_ref, level)
    total_scale = jnp.where(upper, 1.0, jnp.exp(wide_log(logs_of(other_ref), spread)))
    other_scale = jnp.where(upper, jnp.exp(wide_log(logs_of(total_ref), spread)), 1.0)
    logs = logs_of(total_ref).astype(F32) + logs_of(other_ref).astype(F32)
    logs = pieces(jnp.sum(logs, axis=0, keepdims=True), 0)
    put_message(out_ref, state_of(total_ref) * total_scale + state_of(other_ref) * other_scale, logs)


def last_kernel(levels, ctx_ref, after_ref, spread_ref, own_ref, sibling_ref, *refs):
    keep_ref, send_ref = refs[-2:]
    count = len(refs[:-2]) // levels
    parts = []
    for piece in range(count):
        state = log = 0.0
        for level in range(levels):
            ref = refs[level * count + piece]
            upper = is_upper(ctx_ref, level)
            spread = piece_of(spread_ref, piece, ref)
            state = state + jnp.where(upper, state_of(ref), 0.0) * jnp.exp(log)
            log = log + jnp.where(upper, wide_log(logs_of(ref), spread), 0.0)
        parts.append(state)
    chip = jnp.concatenate(parts, axis=1)
    for core, first, mine, other in ((0, own_ref, 0, 1), (1, sibling_ref, 1, 0)):

        @pl.when((ctx_ref[0] & 1) == core)
        def _():
            after = chip * jnp.exp(wide_log(logs_of(first), spread_ref[...])) + state_of(first)
            both = (chip.astype(BF16), after.astype(BF16))
            keep_ref[...] = both[mine]
            send_ref[...] = both[other]


def local_kernel(groups, part_index, gate_hbm, c_hbm, w_hbm, x_ref, b_ref, step_ref, decay_ref, skip_ref, after_ref, *refs):
    if part_index:
        refs = refs[5:]
    mixed_ref, scale_ref, c_ref, state_ref, before_ref, w_ref, token_ref, gate_ref, semaphores = refs
    token_ref[...] = jnp.zeros_like(token_ref)
    channels = x_ref.shape[1]
    heads = step_ref.shape[0]
    width = channels // groups
    chunks = gate_ref.shape[0] // CHUNK
    mine = range(part_index * chunks, (part_index + 1) * chunks)
    own_rows = rows_of(part_index, chunks * CHUNK)
    small = load([(c_hbm.at[own_rows, :], c_ref.at[own_rows, :])], semaphores)
    gates = [(gate_hbm.at[rows_of(n), :], gate_ref.at[rows_of(n - mine[0]), :]) for n in mine]
    gates = load(gates, semaphores.at[pl.ds(1, chunks)])
    size = channels // WEIGHT_COPIES
    columns = rows_of(part_index, w_ref.shape[1])
    weights = [(w_hbm.at[rows_of(n, size), columns], w_ref.at[rows_of(n, size), :]) for n in range(WEIGHT_COPIES)]
    weights = load(weights, semaphores.at[pl.ds(1 + chunks, WEIGHT_COPIES)])

    spread = head_map(channels)
    row = lax.broadcasted_iota(jnp.int32, (CHUNK, CHUNK), 0)
    column = lax.broadcasted_iota(jnp.int32, (CHUNK, CHUNK), 1)
    lane = lax.broadcasted_iota(jnp.int32, (heads, CHUNK), 1)
    skip = jnp.concatenate([pieces(skip_ref[...], 0), jnp.zeros((EXTRA, 128 - heads), F32)], axis=1)
    skip = wide_log(skip.astype(BF16), spread)
    before = jnp.zeros((heads, 1), F32)
    state = [jnp.zeros((STATE, width), F32)] * groups
    if part_index:
        before = before_ref[:, 0:1]
        state = [state_ref[:, rows_of(g, width)] for g in range(groups)]
    small[0].wait()
    for n, running in zip(mine, running_sums(decay_ref[:, own_rows])):
        here = rows_of(n)
        middle, total = running[:, MIDDLE : MIDDLE + 1], running[:, CHUNK - 1 :]
        inner = running - middle
        factors = jnp.exp(jnp.where(lane == 0, total, jnp.where(lane == 1, total - middle, middle)))
        factors = jnp.concatenate(
            [
                by_row(step_ref[:, here] * jnp.exp(-inner)),
                by_row(jnp.exp(inner)),
                by_row(jnp.exp(before + running)),
                by_row(factors)[:EXTRA],
            ],
            axis=0,
        )
        before = before + total
        gates[n - mine[0]].wait()
        for g in range(groups):
            cut = slice(g * width, (g + 1) * width)
            part = slice(g * STATE, (g + 1) * STATE)
            wide = dot(factors, spread[:, cut])
            to_state, to_fresh, to_middle = (wide[3 * CHUNK + n : 3 * CHUNK + n + 1] for n in range(3))
            x = x_ref[here, cut].astype(F32)
            weighted = (x * wide[:CHUNK]).astype(BF16)
            started = jnp.concatenate([weighted, (state[g] * to_middle).astype(BF16)], axis=0)
            scores = lax.dot_general(
                c_ref[here, part], b_ref[here, part], (((1,), (1,)), ((), ())), preferred_element_type=F32
            )
            scores = jnp.where(row >= column, scores, 0.0).astype(BF16)
            within = dot(jnp.concatenate([scores, c_ref[here, part]], axis=1), started)
            if n + 1 < x_ref.shape[0] // CHUNK:
                fresh = lax.dot_general(
                    b_ref[here, part], weighted, (((0,), (0,)), ((), ())), preferred_element_type=F32
                )
                state[g] = state[g] * to_state + fresh * to_fresh
            gate = gate_ref[rows_of(n - mine[0]), cut].astype(F32)
            gate = gate * (0.5 * jnp.tanh(0.5 * gate) + 0.5)
            mixed_ref[here, cut] = (within * wide[CHUNK : 2 * CHUNK] + x * skip[:, cut]) * gate
            scale_ref[here, cut] = wide[2 * CHUNK : 3 * CHUNK] * gate
    before_ref[...] = jnp.broadcast_to(before, before_ref.shape)
    for g in range(groups):
        state_ref[:, rows_of(g, width)] = state[g]
    for copy in weights:
        copy.wait()


def norm_group(mixed, scale, c_rows, gain, state):
    whole = mixed + scale * dot(c_rows, state)
    meansq = jnp.mean(whole * whole, axis=1, keepdims=True)
    return (whole * lax.rsqrt(meansq + 1e-05) * gain).astype(BF16)


def norm_rows(groups, state, mixed, scale, c_rows, gain):
    width = mixed.shape[1] // groups
    parts = []
    for g in range(groups):
        cut = slice(g * width, (g + 1) * width)
        of_state = c_rows[:, g * STATE : (g + 1) * STATE]
        parts.append(norm_group(mixed[:, cut], scale[:, cut], of_state, gain[:, cut], state[:, cut]))
    return parts


def fill_state(ctx_ref, keep_ref, recv_ref, state):
    half = keep_ref.shape[1]
    for core in range(2):

        @pl.when((ctx_ref[0] & 1) == core)
        def _():
            state[:, core * half : (core + 1) * half] = keep_ref[...]
            state[:, (1 - core) * half : (2 - core) * half] = recv_ref[...]


def block_at(here, position, count, size):
    block = 0
    for i in range(count):
        block = jnp.where(here == i, block_order(i, count)[position], block)
    return pl.ds(pl.multiple_of(block * size, size), size)


def one_group(group, here, mixed_ref, scale_ref, c_ref, gain_ref, state):
    width = state.shape[1]
    cut = pl.ds(pl.multiple_of(group * width, width), width)
    part = pl.ds(pl.multiple_of(group * STATE, STATE), STATE)
    return norm_group(mixed_ref[here, cut], scale_ref[here, cut], c_ref[here, part], gain_ref[:, cut], state)


def times_rows(group, normed, w_ref, columns):
    width = normed.shape[1]
    return dot(normed, w_ref[pl.ds(pl.multiple_of(group * width, width), width), :columns])


def own_group_kernel(count, ctx_ref, here_ref, mixed_ref, scale_ref, c_ref, gain_ref, w_ref, keep_ref, normed_ref, product_ref):
    size, columns = product_ref.shape
    here = block_at(here_ref[0], 0, count, size)
    group = ctx_ref[0] & 1
    normed = one_group(group, here, mixed_ref, scale_ref, c_ref, gain_ref, keep_ref[...])
    normed_ref[...] = normed
    product_ref[...] = times_rows(group, normed, w_ref, columns)


def other_group_kernel(count, ctx_ref, here_ref, mixed_ref, scale_ref, c_ref, gain_ref, w_ref, recv_ref, own_ref, product_ref,
                       out_ref, normed_ref):
    size, columns = product_ref.shape
    here = block_at(here_ref[0], 0, count, size)
    group = 1 - (ctx_ref[0] & 1)
    normed = one_group(group, here, mixed_ref, scale_ref, c_ref, gain_ref, recv_ref[...])
    out_ref[...] = (product_ref[...] + times_rows(group, normed, w_ref, columns)).astype(BF16)
    width = normed.shape[1]
    for g in range(2):

        @pl.when(group == g)
        def _():
            normed_ref[:, rows_of(g, width)] = normed
            normed_ref[:, rows_of(1 - g, width)] = own_ref[...]


def both_groups_kernel(groups, count, ctx_ref, here_ref, mixed_ref, scale_ref, c_ref, gain_ref, w_ref, keep_ref, recv_ref,
                       out_ref, normed_ref, state):
    fill_state(ctx_ref, keep_ref, recv_ref, state)
    width = normed_ref.shape[1] // groups
    here = block_at(here_ref[0], 0, count, normed_ref.shape[0])
    rows = norm_rows(groups, state, mixed_ref.at[here, :], scale_ref.at[here, :], c_ref.at[here, :], gain_ref)
    for g, part in enumerate(rows):
        normed_ref[:, g * width : (g + 1) * width] = part
    out_ref[...] = dot(normed_ref[...], w_ref[:, : out_ref.shape[1]]).astype(BF16)


def project_kernel(start, normed_ref, w_ref, *outs):
    for ref in outs:
        columns = ref.shape[1]
        ref[...] = dot(normed_ref[...], w_ref[:, start : start + columns]).astype(BF16)
        start += columns


def rest_kernel(groups, count, ctx_ref, here_ref, mixed_ref, scale_ref, c_ref, gain_ref, wa_ref, wb_ref, keep_ref, recv_ref,
                *refs):
    *first, out_ref, state, normed = refs
    size, piece = first[0].shape
    half = wa_ref.shape[1]
    blocks = [block_at(here_ref[0], n, count, size) for n in range(count)]
    for n, ref in enumerate(first):
        out_ref[blocks[0], n * piece : (n + 1) * piece] = ref[...]
    fill_state(ctx_ref, keep_ref, recv_ref, state)
    width = normed.shape[1] // groups
    for n in range(1, count):
        here = blocks[n]
        rows = norm_rows(groups, state, mixed_ref.at[here, :], scale_ref.at[here, :], c_ref.at[here, :], gain_ref)
        for g, part in enumerate(rows):
            normed[(n - 1) * size : n * size, g * width : (g + 1) * width] = part

    for first_column, w_ref in ((0, wa_ref), (half, wb_ref)):

        @pl.loop(0, half // COLUMN_TILE)
        def _(j):
            cut = pl.ds(pl.multiple_of(j * COLUMN_TILE, COLUMN_TILE), COLUMN_TILE)
            to = pl.ds(pl.multiple_of(first_column + j * COLUMN_TILE, COLUMN_TILE), COLUMN_TILE)
            product = dot(normed[...], w_ref[:, cut]).astype(BF16)
            for n in range(1, count):
                out_ref[blocks[n], to] = product[(n - 1) * size : n * size]


def pass_kernel(count, step, column, here_ref, *refs):
    sums_ref, even_out, odd_out = refs[-3:]
    arrived = refs[:-3]
    size, width = even_out.shape
    here = here_ref[0]

    def send(shift, came, out):
        block = jnp.clip(here + shift, 0, count - 1)
        rows = pl.ds(pl.multiple_of(block * size, size), size)
        own = sums_ref[rows, column : column + width].astype(F32)
        for ref in came:
            own = own + ref[...].astype(F32)
        out[...] = own.astype(BF16)

    for parity, to_right, to_left, from_left, from_right in (
        (0, even_out, odd_out, arrived[1:], arrived[:1]),
        (1, odd_out, even_out, arrived[:1], arrived[1:]),
    ):

        @pl.when((here & 1) == parity)
        def _():
            send(count - step, from_left, to_right)
            send(step - count, from_right, to_left)


def sum_kernel(column, here_ref, even_ref, odd_ref, sums_ref, *refs):
    out_hbm, total, semaphores = refs[-3:]
    size, width = even_ref.shape
    rows = pl.ds(pl.multiple_of(here_ref[0] * size, size), size)
    copies = []
    for n in range(SUM_COPIES):
        part = rows_of(n, size // SUM_COPIES)
        own = sums_ref[rows, column : column + width][part, :].astype(F32)
        total[part, :] = (own + even_ref[part, :].astype(F32) + odd_ref[part, :].astype(F32)).astype(BF16)
        to = out_hbm.at[part, column : column + width]
        copies.extend(load([(total.at[part, :], to)], semaphores.at[pl.ds(n, 1)]))
    for copy in copies:
        copy.wait()


def block_order(here, count):
    order = []
    for step in range(1, count):
        for block, sends in ((count - step + here, here <= step - 1), (step - count + here, here >= count - step)):
            if sends and block not in order:
                order.append(block)
    return order + [b for b in range(count) if b not in order]


def in_vmem(kernel, name, ins, outs, scratch=(), vmem=4, flops=1, result=None, aliases=None):
    vm = pl.BlockSpec(memory_space=pltpu.VMEM)
    specs, arrays = [], []
    for v in ins:
        if isinstance(v, tuple):
            specs.append(pl.BlockSpec(memory_space=pltpu.HBM))
            arrays.append(pltpu.with_memory_space_constraint(v[0], pltpu.HBM))
        elif v.dtype == jnp.int32:
            specs.append(pl.BlockSpec(memory_space=pltpu.SMEM))
            arrays.append(v)
        else:
            specs.append(vm)
            arrays.append(pltpu.with_memory_space_constraint(v, pltpu.VMEM))
    in_hbm = outs is None
    return pl.pallas_call(
        kernel,
        in_specs=specs,
        out_specs=[pl.BlockSpec(memory_space=pltpu.HBM)] if in_hbm else [vm for _ in outs],
        out_shape=[pltpu.HBM(*result)] if in_hbm else [pltpu.VMEM(shape, kind) for shape, kind in outs],
        scratch_shapes=list(scratch),
        input_output_aliases={len(ins) - 1: 0} if in_hbm and isinstance(ins[-1], tuple) else aliases or {},
        compiler_params=pltpu.CompilerParams(vmem_limit_bytes=vmem * 2**20),
        cost_estimate=pl.CostEstimate(flops=flops, bytes_accessed=1, transcendentals=0),
        name=name,
    )(*arrays)


def line_reduce(first, partial_sums, here, size, columns):
    count = lax.axis_size("tp")
    width = columns // PARTS
    block = ((size, width), BF16)
    even_edges = [(i, i ^ 1) for i in range(count)]
    odd_edges = [(i, ((i + 1) ^ 1) - 1) for i in range(1, count - 1)]
    arrived = [()] * PARTS
    for step in range(1, count):
        for half in range(PARTS):
            if step == 1:
                arrived[half] = (lax.ppermute(first[half], "tp", even_edges),)
                continue
            even, odd = in_vmem(
                partial(pass_kernel, count, step, half * width), "pass_on", (here, *arrived[half], partial_sums), (block, block)
            )
            arrived[half] = (lax.ppermute(even, "tp", even_edges), lax.ppermute(odd, "tp", odd_edges))
    out = ()
    for half in range(PARTS):
        ins = (here, *arrived[half], partial_sums, *out)
        scratch = [pltpu.VMEM((size, width), BF16), pltpu.SemaphoreType.DMA((SUM_COPIES,))]
        kernel = partial(sum_kernel, half * width)
        out = (tuple(in_vmem(kernel, "sum_up", ins, None, scratch, result=((size, columns), BF16))),)
    return out[0][0]


def on_device(x_in, gate_z, b_in, c_in, step_size, log_decay, skip, norm_gain, out_weight):
    rows, channels = x_in.shape
    heads = step_size.shape[1]
    groups = b_in.shape[1] // STATE
    chunks = rows // CHUNK
    columns = out_weight.shape[1]
    half = channels // 2
    devices = lax.axis_size("ctx")
    chips = devices // 2
    count = lax.axis_size("tp")
    size = rows // count
    ctx = lax.axis_index("ctx").astype(jnp.int32).reshape(1)
    here = lax.axis_index("tp").astype(jnp.int32).reshape(1)
    message = ((half + EXTRA, 128), BF16)
    whole = ((rows, channels), F32)
    by_head = ((heads, rows), F32)
    maps = ((rows, groups * STATE), BF16)
    weighted = pltpu.VMEM((rows, half), BF16)

    send, x_here, b_here, step, decay, spread = in_vmem(
        partial(send_kernel, groups),
        "end_state_sent",
        (ctx, here, (x_in,), (b_in,), (step_size.T,), (log_decay.T,)),
        (message, ((rows, channels), BF16), maps, by_head, by_head, ((128, half), BF16)),
        scratch=[weighted, pltpu.SemaphoreType.DMA((4 + chunks,))],
        vmem=6,
    )
    swap = [(i, i ^ 1) for i in range(devices)]
    sibling = lax.ppermute(send, "ctx", swap)
    (own,) = in_vmem(
        partial(keep_kernel, groups), "end_state_kept", (ctx, x_here, b_here, step, decay, spread), (message,), [weighted],
        vmem=6, flops=10**9,
    )
    piece = ((half // PIECES + EXTRA, 128), BF16)
    totals = in_vmem(pair_kernel, "pair", (ctx, spread, own, sibling), (piece,) * PIECES)
    levels = chips.bit_length() - 1

    def swap_chips(level, blocks):
        return [lax.ppermute(v, "ctx", [(i, i ^ (2 << level)) for i in range(devices)]) for v in blocks]

    def local_part(part_index, after, carried):
        return in_vmem(
            partial(local_kernel, groups, part_index),
            "local_part",
            ((gate_z,), (c_in,), (out_weight,), x_here, b_here, step, decay, skip.reshape(1, heads), after, *carried),
            (
                whole,
                whole,
                maps,
                ((STATE, channels), F32),
                ((heads, 128), F32),
                ((channels, columns // 2), BF16),
                ((EXTRA, 128), BF16),
            ),
            scratch=[
                pltpu.VMEM((rows // 2, channels), BF16),
                pltpu.SemaphoreType.DMA((1 + chunks // 2 + WEIGHT_COPIES,)),
            ],
            vmem=10,
            flops=4 * 10**9,
            aliases={9 + n: n for n in range(len(carried))},
        )

    received = swap_chips(0, totals)
    *carried, weight_a, token = local_part(0, totals[-1], ())
    arrived = list(received)
    for level in range(1, levels):
        folded = []
        for n in range(PIECES):
            kernel = partial(fold_kernel, level - 1, n)
            after = folded[-1] if folded else token
            folded.extend(in_vmem(kernel, "fold", (ctx, after, spread, totals[n], received[n]), (piece,)))
        totals = folded
        received = swap_chips(level, totals)
        arrived.extend(received)
    mixed, scale, c_here, _, _, weight_b, token = local_part(1, totals[-1], carried)
    state = ((STATE, half), BF16)
    keep, send = in_vmem(
        partial(last_kernel, levels), "incoming", (ctx, token, spread, own, sibling, *arrived), (state, state)
    )
    recv = lax.ppermute(send, "ctx", swap)

    gain = norm_gain.reshape(1, channels)
    width = columns // PARTS
    piece = ((size, width), BF16)
    row_block = ((size, channels), BF16)
    whole_state = pltpu.VMEM((STATE, channels), BF16)
    inputs = (ctx, here, mixed, scale, c_here, gain, weight_a)
    if groups == 2:
        own_group, product = in_vmem(
            partial(own_group_kernel, count), "own_group", (*inputs, keep), (((size, half), BF16), ((size, width), F32)),
            flops=10**9,
        )
        first, normed = in_vmem(
            partial(other_group_kernel, count), "other_group", (*inputs, recv, own_group, product), (piece, row_block)
        )
    else:
        first, normed = in_vmem(
            partial(both_groups_kernel, groups, count), "both_groups", (*inputs, keep, recv), (piece, row_block), [whole_state]
        )
    pieces_out = [first]
    for start, weight, number in ((1, weight_a, PARTS // 2 - 1), (0, weight_b, PARTS // 2)):
        kernel = partial(project_kernel, start * width)
        pieces_out.extend(in_vmem(kernel, "first_block_rest", (normed, weight), (piece,) * number))
    (partial_sums,) = in_vmem(
        partial(rest_kernel, groups, count),
        "other_blocks",
        (*inputs, weight_b, keep, recv, *pieces_out),
        (((rows, columns), BF16),),
        [whole_state, pltpu.VMEM((rows - size, channels), BF16)],
        vmem=6,
    )
    return line_reduce(pieces_out, partial_sums, here, size, columns)


def solution(mesh):
    placed = (
        P("ctx", "tp"),
        P("ctx", "tp"),
        P("ctx", "tp"),
        P("ctx", "tp"),
        P("ctx", "tp"),
        P("ctx", "tp"),
        P("tp"),
        P("tp"),
        P("tp", None),
    )
    return jax.shard_map(
        on_device, mesh=mesh, in_specs=placed, out_specs=P(("ctx", "tp"), None), check_vma=False
    )
```

```python
from functools import partial

import jax
import jax.numpy as jnp
from jax import lax
from jax.experimental import pallas as pl
from jax.experimental.pallas import tpu as pltpu
from jax.sharding import PartitionSpec as P

HEAD_DIM = 64
STATE = 128
CHUNK = 128
MIDDLE = CHUNK // 2 - 1
EXTRA = 16
COLUMN_TILE = 512
PARTS = 4
WEIGHT_COPIES = 8
SUM_COPIES = 4
PIECES = 2
F32 = jnp.float32
BF16 = jnp.bfloat16


def dot(a, b):
    return jnp.dot(a, b, preferred_element_type=F32)


def head_map(channels):
    head = lax.broadcasted_iota(jnp.int32, (128, channels), 0) & 63
    place = lax.broadcasted_iota(jnp.int32, (128, channels), 1) >> 6
    return jnp.where(head == place, 1.0, 0.0).astype(BF16)


def padded(values):
    return jnp.concatenate([values, jnp.zeros((64 - values.shape[0], values.shape[1]), F32)], axis=0)


def by_row(values):
    high = values.astype(BF16).astype(F32)
    return jnp.transpose(jnp.concatenate([padded(high), padded(values - high)], axis=0)).astype(BF16)


def pieces(values, axis):
    first = values.astype(BF16).astype(F32)
    second = (values - first).astype(BF16).astype(F32)
    third = values - first - second
    shape = (EXTRA, values.shape[1]) if axis == 0 else (values.shape[0], 128)
    at = lax.broadcasted_iota(jnp.int32, shape, axis)
    return jnp.where(at == 0, first, jnp.where(at == 1, second, jnp.where(at == 2, third, 0.0)))


def running_sums(decay):
    heads, rows = decay.shape
    chunks = rows // CHUNK
    values = jnp.concatenate([decay[:, rows_of(n)] for n in range(chunks)], axis=0)
    first = values.astype(BF16)
    rest = values - first.astype(F32)
    second = rest.astype(BF16)
    third = (rest - second.astype(F32)).astype(BF16)
    row = lax.broadcasted_iota(jnp.int32, (CHUNK, CHUNK), 0)
    column = lax.broadcasted_iota(jnp.int32, (CHUNK, CHUNK), 1)
    upper = jnp.where(row <= column, 1.0, 0.0).astype(BF16)
    sums = dot(jnp.concatenate([first, second, third], axis=1), jnp.concatenate([upper] * 3, axis=0))
    return [sums[rows_of(n, heads)] for n in range(chunks)]


def load(pairs, semaphores):
    copies = [pltpu.make_async_copy(src, dst, semaphores.at[n]) for n, (src, dst) in enumerate(pairs)]
    for copy in copies:
        copy.start()
    return copies


def rows_of(chunk, size=CHUNK):
    return slice(chunk * size, (chunk + 1) * size)


def put_message(ref, state, logs):
    for j in range(state.shape[1] // 128):
        ref[j * STATE : (j + 1) * STATE, :] = state[:, j * 128 : (j + 1) * 128].astype(BF16)
    ref[state.shape[1] :, :] = logs.astype(BF16)


def state_of(ref):
    count = (ref.shape[0] - EXTRA) // STATE
    return jnp.concatenate([ref[j * STATE : (j + 1) * STATE, :] for j in range(count)], axis=1).astype(F32)


def logs_of(ref):
    return ref[ref.shape[0] - EXTRA :, :]


def wide_log(logs, spread):
    return jnp.sum(dot(logs, spread), axis=0, keepdims=True)


def end_state(groups, half, x_ref, b_ref, step_ref, decay_ref, weighted, message_ref, spread, x_copies=(), b_copies=()):
    rows, width = weighted.shape
    heads = width // HEAD_DIM
    of_heads = pl.ds(pl.multiple_of(half * heads, heads), heads)
    of_channels = pl.ds(pl.multiple_of(half * width, width), width)
    of_group = pl.ds(pl.multiple_of((half * groups // 2) * STATE, STATE), STATE)
    before, running = jnp.zeros((heads, 1), F32), []
    for sums in running_sums(decay_ref[of_heads, :]):
        running.append(before + sums)
        before = before + sums[:, CHUNK - 1 :]
    factors = [by_row(step_ref[of_heads, rows_of(n)] * jnp.exp(before - sums)) for n, sums in enumerate(running)]
    for n, factor in enumerate(factors):
        here = rows_of(n)
        factor = dot(factor, spread)
        for copy in x_copies[n : n + 1]:
            copy.wait()
        weighted[here, :] = (x_ref[here, of_channels].astype(F32) * factor).astype(BF16)
    for copy in b_copies:
        copy.wait()
    state = lax.dot_general(
        b_ref[:, of_group], weighted[...], (((0,), (0,)), ((), ())), preferred_element_type=F32
    )
    logs = jnp.concatenate([pieces(before, 1), jnp.zeros((128 - heads, 128), F32)], axis=0)
    put_message(message_ref, state, jnp.transpose(logs)[:EXTRA])


def send_kernel(groups, ctx_ref, here_ref, x_hbm, b_hbm, step_hbm, decay_hbm, send_ref, x_ref, b_ref, step_ref, decay_ref,
                spread_ref, weighted, semaphores):
    width = weighted.shape[1]
    other = 1 - (ctx_ref[0] & 1)
    first, second = [pl.ds(pl.multiple_of(half * width, width), width) for half in (other, 1 - other)]
    rows = [rows_of(n) for n in range(x_ref.shape[0] // CHUNK)]
    copies = load(
        [(decay_hbm, decay_ref), (step_hbm, step_ref)]
        + [(x_hbm.at[here, first], x_ref.at[here, first]) for here in rows]
        + [(b_hbm, b_ref), (x_hbm.at[:, second], x_ref.at[:, second])],
        semaphores,
    )
    spread = head_map(width)
    spread_ref[...] = spread
    for copy in copies[:2]:
        copy.wait()
    end_state(
        groups, other, x_ref, b_ref, step_ref, decay_ref, weighted, send_ref, spread, copies[2:-2], copies[-2:-1]
    )
    copies[-1].wait()


def keep_kernel(groups, ctx_ref, x_ref, b_ref, step_ref, decay_ref, spread_ref, keep_ref, all_spread_ref, weighted):
    all_spread_ref[...] = head_map(x_ref.shape[1])
    end_state(groups, (ctx_ref[0] & 1), x_ref, b_ref, step_ref, decay_ref, weighted, keep_ref, spread_ref[...])


def pair_kernel(ctx_ref, spread_ref, own_ref, sibling_ref, *pieces_refs):
    spread = spread_ref[...]
    own_log, sibling_log = wide_log(logs_of(own_ref), spread), wide_log(logs_of(sibling_ref), spread)
    early = (ctx_ref[0] & 1) == 0
    own_scale = jnp.where(early, jnp.exp(sibling_log), 1.0)
    sibling_scale = jnp.where(early, 1.0, jnp.exp(own_log))
    logs = logs_of(own_ref).astype(F32) + logs_of(sibling_ref).astype(F32)
    logs = pieces(jnp.sum(logs, axis=0, keepdims=True), 0)
    state = state_of(own_ref) * own_scale + state_of(sibling_ref) * sibling_scale
    width = state.shape[1] // len(pieces_refs)
    for n, ref in enumerate(pieces_refs):
        put_message(ref, state[:, n * width : (n + 1) * width], logs)


def is_upper(ctx_ref, level):
    return ((ctx_ref[0] >> (1 + level)) & 1) == 1


def piece_of(spread_ref, piece, ref):
    width = ref.shape[0] - EXTRA
    return spread_ref[:, piece * width : (piece + 1) * width]


def fold_kernel(level, piece, ctx_ref, after_ref, spread_ref, total_ref, other_ref, out_ref):
    spread = piece_of(spread_ref, piece, total_ref)
    upper = is_upper(ctx_ref, level)
    total_scale = jnp.where(upper, 1.0, jnp.exp(wide_log(logs_of(other_ref), spread)))
    other_scale = jnp.where(upper, jnp.exp(wide_log(logs_of(total_ref), spread)), 1.0)
    logs = logs_of(total_ref).astype(F32) + logs_of(other_ref).astype(F32)
    logs = pieces(jnp.sum(logs, axis=0, keepdims=True), 0)
    put_message(out_ref, state_of(total_ref) * total_scale + state_of(other_ref) * other_scale, logs)


def last_kernel(levels, ctx_ref, after_ref, spread_ref, own_ref, sibling_ref, *refs):
    keep_ref, send_ref = refs[-2:]
    count = len(refs[:-2]) // levels
    parts = []
    for piece in range(count):
        state = log = 0.0
        for level in range(levels):
            ref = refs[level * count + piece]
            upper = is_upper(ctx_ref, level)
            spread = piece_of(spread_ref, piece, ref)
            state = state + jnp.where(upper, state_of(ref), 0.0) * jnp.exp(log)
            log = log + jnp.where(upper, wide_log(logs_of(ref), spread), 0.0)
        parts.append(state)
    chip = jnp.concatenate(parts, axis=1)
    for core, first, mine, other in ((0, own_ref, 0, 1), (1, sibling_ref, 1, 0)):

        @pl.when((ctx_ref[0] & 1) == core)
        def _():
            after = chip * jnp.exp(wide_log(logs_of(first), spread_ref[...])) + state_of(first)
            both = (chip.astype(BF16), after.astype(BF16))
            keep_ref[...] = both[mine]
            send_ref[...] = both[other]


def local_kernel(groups, part_index, gate_hbm, c_hbm, w_hbm, x_ref, b_ref, step_ref, decay_ref, skip_ref, spread_ref, after_ref, *refs):
    if part_index:
        refs = refs[5:]
    mixed_ref, scale_ref, c_ref, state_ref, before_ref, w_ref, token_ref, gate_ref, semaphores = refs
    token_ref[...] = jnp.zeros_like(token_ref)
    channels = x_ref.shape[1]
    heads = step_ref.shape[0]
    width = channels // groups
    chunks = gate_ref.shape[0] // CHUNK
    mine = range(part_index * chunks, (part_index + 1) * chunks)
    own_rows = rows_of(part_index, chunks * CHUNK)
    small = load([(c_hbm.at[own_rows, :], c_ref.at[own_rows, :])], semaphores)
    gates = [(gate_hbm.at[rows_of(n), :], gate_ref.at[rows_of(n - mine[0]), :]) for n in mine]
    gates = load(gates, semaphores.at[pl.ds(1, chunks)])
    size = channels // WEIGHT_COPIES
    columns = rows_of(part_index, w_ref.shape[1])
    weights = [(w_hbm.at[rows_of(n, size), columns], w_ref.at[rows_of(n, size), :]) for n in range(WEIGHT_COPIES)]
    weights = load(weights, semaphores.at[pl.ds(1 + chunks, WEIGHT_COPIES)])

    row = lax.broadcasted_iota(jnp.int32, (CHUNK, CHUNK), 0)
    column = lax.broadcasted_iota(jnp.int32, (CHUNK, CHUNK), 1)
    lane = lax.broadcasted_iota(jnp.int32, (heads, CHUNK), 1)
    skip = jnp.concatenate([pieces(skip_ref[...], 0), jnp.zeros((EXTRA, 128 - heads), F32)], axis=1)
    skip = wide_log(skip.astype(BF16), spread_ref[...])
    before = jnp.zeros((heads, 1), F32)
    state = [jnp.zeros((STATE, width), F32)] * groups
    if part_index:
        before = before_ref[:, 0:1]
        state = [state_ref[:, rows_of(g, width)] for g in range(groups)]
    small[0].wait()
    for n, running in zip(mine, running_sums(decay_ref[:, own_rows])):
        here = rows_of(n)
        middle, total = running[:, MIDDLE : MIDDLE + 1], running[:, CHUNK - 1 :]
        inner = running - middle
        factors = jnp.exp(jnp.where(lane == 0, total, jnp.where(lane == 1, total - middle, middle)))
        factors = jnp.concatenate(
            [
                by_row(step_ref[:, here] * jnp.exp(-inner)),
                by_row(jnp.exp(inner)),
                by_row(jnp.exp(before + running)),
                by_row(factors)[:EXTRA],
            ],
            axis=0,
        )
        before = before + total
        gates[n - mine[0]].wait()
        for g in range(groups):
            cut = slice(g * width, (g + 1) * width)
            part = slice(g * STATE, (g + 1) * STATE)
            wide = dot(factors, spread_ref[:, cut])
            to_state, to_fresh, to_middle = (wide[3 * CHUNK + n : 3 * CHUNK + n + 1] for n in range(3))
            x = x_ref[here, cut].astype(F32)
            weighted = (x * wide[:CHUNK]).astype(BF16)
            started = jnp.concatenate([weighted, (state[g] * to_middle).astype(BF16)], axis=0)
            scores = lax.dot_general(
                c_ref[here, part], b_ref[here, part], (((1,), (1,)), ((), ())), preferred_element_type=F32
            )
            scores = jnp.where(row >= column, scores, 0.0).astype(BF16)
            within = dot(jnp.concatenate([scores, c_ref[here, part]], axis=1), started)
            if n + 1 < x_ref.shape[0] // CHUNK:
                fresh = lax.dot_general(
                    b_ref[here, part], weighted, (((0,), (0,)), ((), ())), preferred_element_type=F32
                )
                state[g] = state[g] * to_state + fresh * to_fresh
            gate = gate_ref[rows_of(n - mine[0]), cut].astype(F32)
            gate = gate * (0.5 * jnp.tanh(0.5 * gate) + 0.5)
            mixed_ref[here, cut] = (within * wide[CHUNK : 2 * CHUNK] + x * skip[:, cut]) * gate
            scale_ref[here, cut] = wide[2 * CHUNK : 3 * CHUNK] * gate
    before_ref[...] = jnp.broadcast_to(before, before_ref.shape)
    for g in range(groups):
        state_ref[:, rows_of(g, width)] = state[g]
    for copy in weights:
        copy.wait()


def norm_group(mixed, scale, c_rows, gain, state):
    whole = mixed + scale * dot(c_rows, state)
    meansq = jnp.mean(whole * whole, axis=1, keepdims=True)
    return (whole * lax.rsqrt(meansq + 1e-05) * gain).astype(BF16)


def norm_rows(groups, state, mixed, scale, c_rows, gain):
    width = mixed.shape[1] // groups
    parts = []
    for g in range(groups):
        cut = slice(g * width, (g + 1) * width)
        of_state = c_rows[:, g * STATE : (g + 1) * STATE]
        parts.append(norm_group(mixed[:, cut], scale[:, cut], of_state, gain[:, cut], state[:, cut]))
    return parts


def fill_state(ctx_ref, keep_ref, recv_ref, state):
    half = keep_ref.shape[1]
    for core in range(2):

        @pl.when((ctx_ref[0] & 1) == core)
        def _():
            state[:, core * half : (core + 1) * half] = keep_ref[...]
            state[:, (1 - core) * half : (2 - core) * half] = recv_ref[...]


def block_at(here, position, count, size):
    block = 0
    for i in range(count):
        block = jnp.where(here == i, block_order(i, count)[position], block)
    return pl.ds(pl.multiple_of(block * size, size), size)


def one_group(group, here, mixed_ref, scale_ref, c_ref, gain_ref, state):
    width = state.shape[1]
    cut = pl.ds(pl.multiple_of(group * width, width), width)
    part = pl.ds(pl.multiple_of(group * STATE, STATE), STATE)
    return norm_group(mixed_ref[here, cut], scale_ref[here, cut], c_ref[here, part], gain_ref[:, cut], state)


def times_rows(group, normed, w_ref, columns):
    width = normed.shape[1]
    return dot(normed, w_ref[pl.ds(pl.multiple_of(group * width, width), width), :columns])


def own_group_kernel(count, ctx_ref, here_ref, mixed_ref, scale_ref, c_ref, gain_ref, w_ref, keep_ref, normed_ref, product_ref):
    size, columns = product_ref.shape
    here = block_at(here_ref[0], 0, count, size)
    group = ctx_ref[0] & 1
    normed = one_group(group, here, mixed_ref, scale_ref, c_ref, gain_ref, keep_ref[...])
    normed_ref[...] = normed
    product_ref[...] = times_rows(group, normed, w_ref, columns)


def other_group_kernel(count, ctx_ref, here_ref, mixed_ref, scale_ref, c_ref, gain_ref, w_ref, recv_ref, own_ref, product_ref,
                       out_ref, normed_ref):
    size, columns = product_ref.shape
    here = block_at(here_ref[0], 0, count, size)
    group = 1 - (ctx_ref[0] & 1)
    normed = one_group(group, here, mixed_ref, scale_ref, c_ref, gain_ref, recv_ref[...])
    out_ref[...] = (product_ref[...] + times_rows(group, normed, w_ref, columns)).astype(BF16)
    width = normed.shape[1]
    for g in range(2):

        @pl.when(group == g)
        def _():
            normed_ref[:, rows_of(g, width)] = normed
            normed_ref[:, rows_of(1 - g, width)] = own_ref[...]


def both_groups_kernel(groups, count, ctx_ref, here_ref, mixed_ref, scale_ref, c_ref, gain_ref, w_ref, keep_ref, recv_ref,
                       out_ref, normed_ref, state):
    fill_state(ctx_ref, keep_ref, recv_ref, state)
    width = normed_ref.shape[1] // groups
    here = block_at(here_ref[0], 0, count, normed_ref.shape[0])
    rows = norm_rows(groups, state, mixed_ref.at[here, :], scale_ref.at[here, :], c_ref.at[here, :], gain_ref)
    for g, part in enumerate(rows):
        normed_ref[:, g * width : (g + 1) * width] = part
    out_ref[...] = dot(normed_ref[...], w_ref[:, : out_ref.shape[1]]).astype(BF16)


def project_kernel(start, normed_ref, w_ref, *outs):
    for ref in outs:
        columns = ref.shape[1]
        ref[...] = dot(normed_ref[...], w_ref[:, start : start + columns]).astype(BF16)
        start += columns


def rest_kernel(groups, count, ctx_ref, here_ref, mixed_ref, scale_ref, c_ref, gain_ref, wa_ref, wb_ref, keep_ref, recv_ref,
                *refs):
    *first, out_ref, state, normed = refs
    size, piece = first[0].shape
    half = wa_ref.shape[1]
    blocks = [block_at(here_ref[0], n, count, size) for n in range(count)]
    for n, ref in enumerate(first):
        out_ref[blocks[0], n * piece : (n + 1) * piece] = ref[...]
    fill_state(ctx_ref, keep_ref, recv_ref, state)
    width = normed.shape[1] // groups
    for n in range(1, count):
        here = blocks[n]
        rows = norm_rows(groups, state, mixed_ref.at[here, :], scale_ref.at[here, :], c_ref.at[here, :], gain_ref)
        for g, part in enumerate(rows):
            normed[(n - 1) * size : n * size, g * width : (g + 1) * width] = part

    for first_column, w_ref in ((0, wa_ref), (half, wb_ref)):

        @pl.loop(0, half // COLUMN_TILE)
        def _(j):
            cut = pl.ds(pl.multiple_of(j * COLUMN_TILE, COLUMN_TILE), COLUMN_TILE)
            to = pl.ds(pl.multiple_of(first_column + j * COLUMN_TILE, COLUMN_TILE), COLUMN_TILE)
            product = dot(normed[...], w_ref[:, cut]).astype(BF16)
            for n in range(1, count):
                out_ref[blocks[n], to] = product[(n - 1) * size : n * size]


def pass_kernel(count, step, column, here_ref, *refs):
    sums_ref, even_out, odd_out = refs[-3:]
    arrived = refs[:-3]
    size, width = even_out.shape
    here = here_ref[0]

    def send(shift, came, out):
        block = jnp.clip(here + shift, 0, count - 1)
        rows = pl.ds(pl.multiple_of(block * size, size), size)
        own = sums_ref[rows, column : column + width].astype(F32)
        for ref in came:
            own = own + ref[...].astype(F32)
        out[...] = own.astype(BF16)

    for parity, to_right, to_left, from_left, from_right in (
        (0, even_out, odd_out, arrived[1:], arrived[:1]),
        (1, odd_out, even_out, arrived[:1], arrived[1:]),
    ):

        @pl.when((here & 1) == parity)
        def _():
            send(count - step, from_left, to_right)
            send(step - count, from_right, to_left)


def sum_kernel(column, here_ref, even_ref, odd_ref, sums_ref, *refs):
    out_hbm, total, semaphores = refs[-3:]
    size, width = even_ref.shape
    rows = pl.ds(pl.multiple_of(here_ref[0] * size, size), size)
    copies = []
    for n in range(SUM_COPIES):
        part = rows_of(n, size // SUM_COPIES)
        own = sums_ref[rows, column : column + width][part, :].astype(F32)
        total[part, :] = (own + even_ref[part, :].astype(F32) + odd_ref[part, :].astype(F32)).astype(BF16)
        to = out_hbm.at[part, column : column + width]
        copies.extend(load([(total.at[part, :], to)], semaphores.at[pl.ds(n, 1)]))
    for copy in copies:
        copy.wait()


def block_order(here, count):
    order = []
    for step in range(1, count):
        for block, sends in ((count - step + here, here <= step - 1), (step - count + here, here >= count - step)):
            if sends and block not in order:
                order.append(block)
    return order + [b for b in range(count) if b not in order]


def in_vmem(kernel, name, ins, outs, scratch=(), vmem=4, flops=1, result=None, aliases=None):
    vm = pl.BlockSpec(memory_space=pltpu.VMEM)
    specs, arrays = [], []
    for v in ins:
        if isinstance(v, tuple):
            specs.append(pl.BlockSpec(memory_space=pltpu.HBM))
            arrays.append(pltpu.with_memory_space_constraint(v[0], pltpu.HBM))
        elif v.dtype == jnp.int32:
            specs.append(pl.BlockSpec(memory_space=pltpu.SMEM))
            arrays.append(v)
        else:
            specs.append(vm)
            arrays.append(pltpu.with_memory_space_constraint(v, pltpu.VMEM))
    in_hbm = outs is None
    return pl.pallas_call(
        kernel,
        in_specs=specs,
        out_specs=[pl.BlockSpec(memory_space=pltpu.HBM)] if in_hbm else [vm for _ in outs],
        out_shape=[pltpu.HBM(*result)] if in_hbm else [pltpu.VMEM(shape, kind) for shape, kind in outs],
        scratch_shapes=list(scratch),
        input_output_aliases={len(ins) - 1: 0} if in_hbm and isinstance(ins[-1], tuple) else aliases or {},
        compiler_params=pltpu.CompilerParams(vmem_limit_bytes=vmem * 2**20),
        cost_estimate=pl.CostEstimate(flops=flops, bytes_accessed=1, transcendentals=0),
        name=name,
    )(*arrays)


def line_reduce(first, partial_sums, here, size, columns):
    count = lax.axis_size("tp")
    width = columns // PARTS
    block = ((size, width), BF16)
    even_edges = [(i, i ^ 1) for i in range(count)]
    odd_edges = [(i, ((i + 1) ^ 1) - 1) for i in range(1, count - 1)]
    arrived = [()] * PARTS
    for step in range(1, count):
        for half in range(PARTS):
            if step == 1:
                arrived[half] = (lax.ppermute(first[half], "tp", even_edges),)
                continue
            even, odd = in_vmem(
                partial(pass_kernel, count, step, half * width), "pass_on", (here, *arrived[half], partial_sums), (block, block)
            )
            arrived[half] = (lax.ppermute(even, "tp", even_edges), lax.ppermute(odd, "tp", odd_edges))
    out = ()
    for half in range(PARTS):
        ins = (here, *arrived[half], partial_sums, *out)
        scratch = [pltpu.VMEM((size, width), BF16), pltpu.SemaphoreType.DMA((SUM_COPIES,))]
        kernel = partial(sum_kernel, half * width)
        out = (tuple(in_vmem(kernel, "sum_up", ins, None, scratch, result=((size, columns), BF16))),)
    return out[0][0]


def on_device(x_in, gate_z, b_in, c_in, step_size, log_decay, skip, norm_gain, out_weight):
    rows, channels = x_in.shape
    heads = step_size.shape[1]
    groups = b_in.shape[1] // STATE
    chunks = rows // CHUNK
    columns = out_weight.shape[1]
    half = channels // 2
    devices = lax.axis_size("ctx")
    chips = devices // 2
    count = lax.axis_size("tp")
    size = rows // count
    ctx = lax.axis_index("ctx").astype(jnp.int32).reshape(1)
    here = lax.axis_index("tp").astype(jnp.int32).reshape(1)
    message = ((half + EXTRA, 128), BF16)
    whole = ((rows, channels), F32)
    by_head = ((heads, rows), F32)
    maps = ((rows, groups * STATE), BF16)
    weighted = pltpu.VMEM((rows, half), BF16)

    send, x_here, b_here, step, decay, spread = in_vmem(
        partial(send_kernel, groups),
        "end_state_sent",
        (ctx, here, (x_in,), (b_in,), (step_size.T,), (log_decay.T,)),
        (message, ((rows, channels), BF16), maps, by_head, by_head, ((128, half), BF16)),
        scratch=[weighted, pltpu.SemaphoreType.DMA((4 + chunks,))],
        vmem=6,
    )
    swap = [(i, i ^ 1) for i in range(devices)]
    sibling = lax.ppermute(send, "ctx", swap)
    own, all_spread = in_vmem(
        partial(keep_kernel, groups), "end_state_kept", (ctx, x_here, b_here, step, decay, spread),
        (message, ((128, channels), BF16)), [weighted],
        vmem=6, flops=10**9,
    )
    piece = ((half // PIECES + EXTRA, 128), BF16)
    totals = in_vmem(pair_kernel, "pair", (ctx, spread, own, sibling), (piece,) * PIECES)
    levels = chips.bit_length() - 1

    def swap_chips(level, blocks):
        return [lax.ppermute(v, "ctx", [(i, i ^ (2 << level)) for i in range(devices)]) for v in blocks]

    def local_part(part_index, after, carried):
        return in_vmem(
            partial(local_kernel, groups, part_index),
            "local_part",
            ((gate_z,), (c_in,), (out_weight,), x_here, b_here, step, decay, skip.reshape(1, heads), all_spread, after, *carried),
            (
                whole,
                whole,
                maps,
                ((STATE, channels), F32),
                ((heads, 128), F32),
                ((channels, columns // 2), BF16),
                ((EXTRA, 128), BF16),
            ),
            scratch=[
                pltpu.VMEM((rows // 2, channels), BF16),
                pltpu.SemaphoreType.DMA((1 + chunks // 2 + WEIGHT_COPIES,)),
            ],
            vmem=10,
            flops=4 * 10**9,
            aliases={10 + n: n for n in range(len(carried))},
        )

    received = swap_chips(0, totals)
    *carried, weight_a, token = local_part(0, totals[-1], ())
    arrived = list(received)
    for level in range(1, levels):
        folded = []
        for n in range(PIECES):
            kernel = partial(fold_kernel, level - 1, n)
            after = folded[-1] if folded else token
            folded.extend(in_vmem(kernel, "fold", (ctx, after, spread, totals[n], received[n]), (piece,)))
        totals = folded
        received = swap_chips(level, totals)
        arrived.extend(received)
    mixed, scale, c_here, _, _, weight_b, token = local_part(1, totals[-1], carried)
    state = ((STATE, half), BF16)
    keep, send = in_vmem(
        partial(last_kernel, levels), "incoming", (ctx, token, spread, own, sibling, *arrived), (state, state)
    )
    recv = lax.ppermute(send, "ctx", swap)

    gain = norm_gain.reshape(1, channels)
    width = columns // PARTS
    piece = ((size, width), BF16)
    row_block = ((size, channels), BF16)
    whole_state = pltpu.VMEM((STATE, channels), BF16)
    inputs = (ctx, here, mixed, scale, c_here, gain, weight_a)
    if groups == 2:
        own_group, product = in_vmem(
            partial(own_group_kernel, count), "own_group", (*inputs, keep), (((size, half), BF16), ((size, width), F32)),
            flops=10**9,
        )
        first, normed = in_vmem(
            partial(other_group_kernel, count), "other_group", (*inputs, recv, own_group, product), (piece, row_block)
        )
    else:
        first, normed = in_vmem(
            partial(both_groups_kernel, groups, count), "both_groups", (*inputs, keep, recv), (piece, row_block), [whole_state]
        )
    pieces_out = [first]
    for start, weight, number in ((1, weight_a, PARTS // 2 - 1), (0, weight_b, PARTS // 2)):
        kernel = partial(project_kernel, start * width)
        pieces_out.extend(in_vmem(kernel, "first_block_rest", (normed, weight), (piece,) * number))
    (partial_sums,) = in_vmem(
        partial(rest_kernel, groups, count),
        "other_blocks",
        (*inputs, weight_b, keep, recv, *pieces_out),
        (((rows, columns), BF16),),
        [whole_state, pltpu.VMEM((rows - size, channels), BF16)],
        vmem=6,
    )
    return line_reduce(pieces_out, partial_sums, here, size, columns)


def solution(mesh):
    placed = (
        P("ctx", "tp"),
        P("ctx", "tp"),
        P("ctx", "tp"),
        P("ctx", "tp"),
        P("ctx", "tp"),
        P("ctx", "tp"),
        P("tp"),
        P("tp"),
        P("tp", None),
    )
    return jax.shard_map(
        on_device, mesh=mesh, in_specs=placed, out_specs=P(("ctx", "tp"), None), check_vma=False
    )
```

```python
from functools import partial

import jax
import jax.numpy as jnp
from jax import lax
from jax.experimental import pallas as pl
from jax.experimental.pallas import tpu as pltpu
from jax.sharding import PartitionSpec as P

HEAD_DIM = 64
STATE = 128
CHUNK = 128
MIDDLE = CHUNK // 2 - 1
EXTRA = 16
COLUMN_TILE = 512
PARTS = 4
WEIGHT_COPIES = 8
SUM_COPIES = 2
PIECES = 2
F32 = jnp.float32
BF16 = jnp.bfloat16


def dot(a, b):
    return jnp.dot(a, b, preferred_element_type=F32)


def head_map(channels):
    head = lax.broadcasted_iota(jnp.int32, (128, channels), 0) & 63
    place = lax.broadcasted_iota(jnp.int32, (128, channels), 1) >> 6
    return jnp.where(head == place, 1.0, 0.0).astype(BF16)


def padded(values):
    return jnp.concatenate([values, jnp.zeros((64 - values.shape[0], values.shape[1]), F32)], axis=0)


def by_row(values):
    high = values.astype(BF16).astype(F32)
    return jnp.transpose(jnp.concatenate([padded(high), padded(values - high)], axis=0)).astype(BF16)


def by_lane(values):
    return jnp.transpose(jnp.concatenate([values, jnp.zeros((128 - values.shape[0], values.shape[1]), F32)], axis=0))


def spread_heads(values, first, heads):
    lane = lax.broadcasted_iota(jnp.int32, values.shape, 1) >> 6
    pairs = range(first, first + heads, 2)
    return jnp.concatenate([jnp.take_along_axis(values, lane + pair, axis=1) for pair in pairs], axis=1)


def pieces(values, axis):
    first = values.astype(BF16).astype(F32)
    second = (values - first).astype(BF16).astype(F32)
    third = values - first - second
    shape = (EXTRA, values.shape[1]) if axis == 0 else (values.shape[0], 128)
    at = lax.broadcasted_iota(jnp.int32, shape, axis)
    return jnp.where(at == 0, first, jnp.where(at == 1, second, jnp.where(at == 2, third, 0.0)))


def running_sums(decay):
    heads, rows = decay.shape
    chunks = rows // CHUNK
    values = jnp.concatenate([decay[:, rows_of(n)] for n in range(chunks)], axis=0)
    first = values.astype(BF16)
    rest = values - first.astype(F32)
    second = rest.astype(BF16)
    third = (rest - second.astype(F32)).astype(BF16)
    row = lax.broadcasted_iota(jnp.int32, (CHUNK, CHUNK), 0)
    column = lax.broadcasted_iota(jnp.int32, (CHUNK, CHUNK), 1)
    upper = jnp.where(row <= column, 1.0, 0.0).astype(BF16)
    sums = dot(jnp.concatenate([first, second, third], axis=1), jnp.concatenate([upper] * 3, axis=0))
    return [sums[rows_of(n, heads)] for n in range(chunks)]


def load(pairs, semaphores):
    copies = [pltpu.make_async_copy(src, dst, semaphores.at[n]) for n, (src, dst) in enumerate(pairs)]
    for copy in copies:
        copy.start()
    return copies


def rows_of(chunk, size=CHUNK):
    return slice(chunk * size, (chunk + 1) * size)


def put_message(ref, state, logs):
    for j in range(state.shape[1] // 128):
        ref[j * STATE : (j + 1) * STATE, :] = state[:, j * 128 : (j + 1) * 128].astype(BF16)
    ref[state.shape[1] :, :] = logs.astype(BF16)


def state_of(ref):
    count = (ref.shape[0] - EXTRA) // STATE
    return jnp.concatenate([ref[j * STATE : (j + 1) * STATE, :] for j in range(count)], axis=1).astype(F32)


def logs_of(ref):
    return ref[ref.shape[0] - EXTRA :, :]


def wide_log(logs, spread):
    return jnp.sum(dot(logs, spread), axis=0, keepdims=True)


def end_state(groups, half, x_ref, b_ref, step_ref, decay_ref, weighted, message_ref, spread, x_copies=(), b_copies=()):
    rows, width = weighted.shape
    heads = width // HEAD_DIM
    of_heads = pl.ds(pl.multiple_of(half * heads, heads), heads)
    of_channels = pl.ds(pl.multiple_of(half * width, width), width)
    of_group = pl.ds(pl.multiple_of((half * groups // 2) * STATE, STATE), STATE)
    before, running = jnp.zeros((heads, 1), F32), []
    for sums in running_sums(decay_ref[of_heads, :]):
        running.append(before + sums)
        before = before + sums[:, CHUNK - 1 :]
    factors = [by_row(step_ref[of_heads, rows_of(n)] * jnp.exp(before - sums)) for n, sums in enumerate(running)]
    for n, factor in enumerate(factors):
        here = rows_of(n)
        factor = dot(factor, spread)
        for copy in x_copies[n : n + 1]:
            copy.wait()
        weighted[here, :] = (x_ref[here, of_channels].astype(F32) * factor).astype(BF16)
    for copy in b_copies:
        copy.wait()
    state = lax.dot_general(
        b_ref[:, of_group], weighted[...], (((0,), (0,)), ((), ())), preferred_element_type=F32
    )
    logs = jnp.concatenate([pieces(before, 1), jnp.zeros((128 - heads, 128), F32)], axis=0)
    put_message(message_ref, state, jnp.transpose(logs)[:EXTRA])


def send_kernel(groups, ctx_ref, here_ref, x_hbm, b_hbm, step_hbm, decay_hbm, send_ref, x_ref, b_ref, step_ref, decay_ref,
                spread_ref, weighted, semaphores):
    width = weighted.shape[1]
    other = 1 - (ctx_ref[0] & 1)
    first, second = [pl.ds(pl.multiple_of(half * width, width), width) for half in (other, 1 - other)]
    rows = [rows_of(n) for n in range(x_ref.shape[0] // CHUNK)]
    copies = load(
        [(decay_hbm, decay_ref), (step_hbm, step_ref)]
        + [(x_hbm.at[here, first], x_ref.at[here, first]) for here in rows]
        + [(b_hbm, b_ref), (x_hbm.at[:, second], x_ref.at[:, second])],
        semaphores,
    )
    spread = head_map(width)
    spread_ref[...] = spread
    for copy in copies[:2]:
        copy.wait()
    end_state(
        groups, other, x_ref, b_ref, step_ref, decay_ref, weighted, send_ref, spread, copies[2:-2], copies[-2:-1]
    )
    copies[-1].wait()


def keep_kernel(groups, ctx_ref, x_ref, b_ref, step_ref, decay_ref, spread_ref, keep_ref, all_spread_ref, weighted):
    all_spread_ref[...] = head_map(x_ref.shape[1])
    end_state(groups, (ctx_ref[0] & 1), x_ref, b_ref, step_ref, decay_ref, weighted, keep_ref, spread_ref[...])


def pair_kernel(ctx_ref, spread_ref, own_ref, sibling_ref, *pieces_refs):
    spread = spread_ref[...]
    own_log, sibling_log = wide_log(logs_of(own_ref), spread), wide_log(logs_of(sibling_ref), spread)
    early = (ctx_ref[0] & 1) == 0
    own_scale = jnp.where(early, jnp.exp(sibling_log), 1.0)
    sibling_scale = jnp.where(early, 1.0, jnp.exp(own_log))
    logs = logs_of(own_ref).astype(F32) + logs_of(sibling_ref).astype(F32)
    logs = pieces(jnp.sum(logs, axis=0, keepdims=True), 0)
    state = state_of(own_ref) * own_scale + state_of(sibling_ref) * sibling_scale
    width = state.shape[1] // len(pieces_refs)
    for n, ref in enumerate(pieces_refs):
        put_message(ref, state[:, n * width : (n + 1) * width], logs)


def is_upper(ctx_ref, level):
    return ((ctx_ref[0] >> (1 + level)) & 1) == 1


def piece_of(spread_ref, piece, ref):
    width = ref.shape[0] - EXTRA
    return spread_ref[:, piece * width : (piece + 1) * width]


def fold_kernel(level, piece, ctx_ref, after_ref, spread_ref, total_ref, other_ref, out_ref):
    spread = piece_of(spread_ref, piece, total_ref)
    upper = is_upper(ctx_ref, level)
    total_scale = jnp.where(upper, 1.0, jnp.exp(wide_log(logs_of(other_ref), spread)))
    other_scale = jnp.where(upper, jnp.exp(wide_log(logs_of(total_ref), spread)), 1.0)
    logs = logs_of(total_ref).astype(F32) + logs_of(other_ref).astype(F32)
    logs = pieces(jnp.sum(logs, axis=0, keepdims=True), 0)
    put_message(out_ref, state_of(total_ref) * total_scale + state_of(other_ref) * other_scale, logs)


def last_kernel(levels, ctx_ref, after_ref, spread_ref, own_ref, sibling_ref, *refs):
    keep_ref, send_ref = refs[-2:]
    count = len(refs[:-2]) // levels
    parts = []
    for piece in range(count):
        state = log = 0.0
        for level in range(levels):
            ref = refs[level * count + piece]
            upper = is_upper(ctx_ref, level)
            spread = piece_of(spread_ref, piece, ref)
            state = state + jnp.where(upper, state_of(ref), 0.0) * jnp.exp(log)
            log = log + jnp.where(upper, wide_log(logs_of(ref), spread), 0.0)
        parts.append(state)
    chip = jnp.concatenate(parts, axis=1)
    for core, first, mine, other in ((0, own_ref, 0, 1), (1, sibling_ref, 1, 0)):

        @pl.when((ctx_ref[0] & 1) == core)
        def _():
            after = chip * jnp.exp(wide_log(logs_of(first), spread_ref[...])) + state_of(first)
            both = (chip.astype(BF16), after.astype(BF16))
            keep_ref[...] = both[mine]
            send_ref[...] = both[other]


def local_kernel(groups, part_index, gate_hbm, c_hbm, w_hbm, x_ref, b_ref, step_ref, decay_ref, skip_ref, spread_ref, after_ref, *refs):
    if part_index:
        refs = refs[5:]
    mixed_ref, scale_ref, c_ref, state_ref, before_ref, w_ref, token_ref, gate_ref, semaphores = refs
    token_ref[...] = jnp.zeros_like(token_ref)
    channels = x_ref.shape[1]
    heads = step_ref.shape[0]
    width = channels // groups
    chunks = gate_ref.shape[0] // CHUNK
    mine = range(part_index * chunks, (part_index + 1) * chunks)
    own_rows = rows_of(part_index, chunks * CHUNK)
    small = load([(c_hbm.at[own_rows, :], c_ref.at[own_rows, :])], semaphores)
    gates = [(gate_hbm.at[rows_of(n), :], gate_ref.at[rows_of(n - mine[0]), :]) for n in mine]
    gates = load(gates, semaphores.at[pl.ds(1, chunks)])
    size = channels // WEIGHT_COPIES
    columns = rows_of(part_index, w_ref.shape[1])
    weights = [(w_hbm.at[rows_of(n, size), columns], w_ref.at[rows_of(n, size), :]) for n in range(WEIGHT_COPIES)]
    weights = load(weights, semaphores.at[pl.ds(1 + chunks, WEIGHT_COPIES)])

    row = lax.broadcasted_iota(jnp.int32, (CHUNK, CHUNK), 0)
    column = lax.broadcasted_iota(jnp.int32, (CHUNK, CHUNK), 1)
    lane = lax.broadcasted_iota(jnp.int32, (heads, CHUNK), 1)
    skip = jnp.concatenate([pieces(skip_ref[...], 0), jnp.zeros((EXTRA, 128 - heads), F32)], axis=1)
    skip = wide_log(skip.astype(BF16), spread_ref[...])
    before = jnp.zeros((heads, 1), F32)
    state = [jnp.zeros((STATE, width), F32)] * groups
    if part_index:
        before = before_ref[:, 0:1]
        state = [state_ref[:, rows_of(g, width)] for g in range(groups)]
    small[0].wait()
    for n, running in zip(mine, running_sums(decay_ref[:, own_rows])):
        here = rows_of(n)
        middle, total = running[:, MIDDLE : MIDDLE + 1], running[:, CHUNK - 1 :]
        inner = running - middle
        factors = jnp.exp(jnp.where(lane == 0, total, jnp.where(lane == 1, total - middle, middle)))
        weights_by_lane = by_lane(step_ref[:, here] * jnp.exp(-inner))
        inner_by_lane = by_lane(jnp.exp(inner))
        outer_by_lane = by_lane(jnp.exp(before + running))
        factors = by_row(factors)[:EXTRA]
        before = before + total
        gates[n - mine[0]].wait()
        for g in range(groups):
            cut = slice(g * width, (g + 1) * width)
            part = slice(g * STATE, (g + 1) * STATE)
            ends = dot(factors, spread_ref[:, cut])
            to_state, to_fresh, to_middle = (ends[n : n + 1] for n in range(3))
            its_heads = (g * heads // groups, heads // groups)
            x = x_ref[here, cut].astype(F32)
            weighted = (x * spread_heads(weights_by_lane, *its_heads)).astype(BF16)
            started = jnp.concatenate([weighted, (state[g] * to_middle).astype(BF16)], axis=0)
            scores = lax.dot_general(
                c_ref[here, part], b_ref[here, part], (((1,), (1,)), ((), ())), preferred_element_type=F32
            )
            scores = jnp.where(row >= column, scores, 0.0).astype(BF16)
            within = dot(jnp.concatenate([scores, c_ref[here, part]], axis=1), started)
            if n + 1 < x_ref.shape[0] // CHUNK:
                fresh = lax.dot_general(
                    b_ref[here, part], weighted, (((0,), (0,)), ((), ())), preferred_element_type=F32
                )
                state[g] = state[g] * to_state + fresh * to_fresh
            gate = gate_ref[rows_of(n - mine[0]), cut].astype(F32)
            gate = gate * (0.5 * jnp.tanh(0.5 * gate) + 0.5)
            mixed_ref[here, cut] = (within * spread_heads(inner_by_lane, *its_heads) + x * skip[:, cut]) * gate
            scale_ref[here, cut] = spread_heads(outer_by_lane, *its_heads) * gate
    before_ref[...] = jnp.broadcast_to(before, before_ref.shape)
    for g in range(groups):
        state_ref[:, rows_of(g, width)] = state[g]
    for copy in weights:
        copy.wait()


def norm_group(mixed, scale, c_rows, gain, state):
    whole = mixed + scale * dot(c_rows, state)
    meansq = jnp.mean(whole * whole, axis=1, keepdims=True)
    return (whole * lax.rsqrt(meansq + 1e-05) * gain).astype(BF16)


def norm_rows(groups, state, mixed, scale, c_rows, gain):
    width = mixed.shape[1] // groups
    parts = []
    for g in range(groups):
        cut = slice(g * width, (g + 1) * width)
        of_state = c_rows[:, g * STATE : (g + 1) * STATE]
        parts.append(norm_group(mixed[:, cut], scale[:, cut], of_state, gain[:, cut], state[:, cut]))
    return parts


def fill_state(ctx_ref, keep_ref, recv_ref, state):
    half = keep_ref.shape[1]
    for core in range(2):

        @pl.when((ctx_ref[0] & 1) == core)
        def _():
            state[:, core * half : (core + 1) * half] = keep_ref[...]
            state[:, (1 - core) * half : (2 - core) * half] = recv_ref[...]


def block_at(here, position, count, size):
    block = 0
    for i in range(count):
        block = jnp.where(here == i, block_order(i, count)[position], block)
    return pl.ds(pl.multiple_of(block * size, size), size)


def one_group(group, here, mixed_ref, scale_ref, c_ref, gain_ref, state):
    width = state.shape[1]
    cut = pl.ds(pl.multiple_of(group * width, width), width)
    part = pl.ds(pl.multiple_of(group * STATE, STATE), STATE)
    return norm_group(mixed_ref[here, cut], scale_ref[here, cut], c_ref[here, part], gain_ref[:, cut], state)


def times_rows(group, normed, w_ref, columns):
    width = normed.shape[1]
    return dot(normed, w_ref[pl.ds(pl.multiple_of(group * width, width), width), :columns])


def own_group_kernel(count, ctx_ref, here_ref, mixed_ref, scale_ref, c_ref, gain_ref, w_ref, keep_ref, normed_ref, product_ref):
    size, columns = product_ref.shape
    here = block_at(here_ref[0], 0, count, size)
    group = ctx_ref[0] & 1
    normed = one_group(group, here, mixed_ref, scale_ref, c_ref, gain_ref, keep_ref[...])
    normed_ref[...] = normed
    product_ref[...] = times_rows(group, normed, w_ref, columns)


def other_group_kernel(count, ctx_ref, here_ref, mixed_ref, scale_ref, c_ref, gain_ref, w_ref, recv_ref, own_ref, product_ref,
                       out_ref, normed_ref):
    size, columns = product_ref.shape
    here = block_at(here_ref[0], 0, count, size)
    group = 1 - (ctx_ref[0] & 1)
    normed = one_group(group, here, mixed_ref, scale_ref, c_ref, gain_ref, recv_ref[...])
    out_ref[...] = (product_ref[...] + times_rows(group, normed, w_ref, columns)).astype(BF16)
    width = normed.shape[1]
    for g in range(2):

        @pl.when(group == g)
        def _():
            normed_ref[:, rows_of(g, width)] = normed
            normed_ref[:, rows_of(1 - g, width)] = own_ref[...]


def both_groups_kernel(groups, count, ctx_ref, here_ref, mixed_ref, scale_ref, c_ref, gain_ref, w_ref, keep_ref, recv_ref,
                       out_ref, normed_ref, state):
    fill_state(ctx_ref, keep_ref, recv_ref, state)
    width = normed_ref.shape[1] // groups
    here = block_at(here_ref[0], 0, count, normed_ref.shape[0])
    rows = norm_rows(groups, state, mixed_ref.at[here, :], scale_ref.at[here, :], c_ref.at[here, :], gain_ref)
    for g, part in enumerate(rows):
        normed_ref[:, g * width : (g + 1) * width] = part
    out_ref[...] = dot(normed_ref[...], w_ref[:, : out_ref.shape[1]]).astype(BF16)


def project_kernel(start, normed_ref, w_ref, *outs):
    for ref in outs:
        columns = ref.shape[1]
        ref[...] = dot(normed_ref[...], w_ref[:, start : start + columns]).astype(BF16)
        start += columns


def rest_kernel(groups, count, ctx_ref, here_ref, mixed_ref, scale_ref, c_ref, gain_ref, wa_ref, wb_ref, keep_ref, recv_ref,
                *refs):
    *first, out_ref, state, normed = refs
    size, piece = first[0].shape
    half = wa_ref.shape[1]
    blocks = [block_at(here_ref[0], n, count, size) for n in range(count)]
    for n, ref in enumerate(first):
        out_ref[blocks[0], n * piece : (n + 1) * piece] = ref[...]
    fill_state(ctx_ref, keep_ref, recv_ref, state)
    width = normed.shape[1] // groups
    for n in range(1, count):
        here = blocks[n]
        rows = norm_rows(groups, state, mixed_ref.at[here, :], scale_ref.at[here, :], c_ref.at[here, :], gain_ref)
        for g, part in enumerate(rows):
            normed[(n - 1) * size : n * size, g * width : (g + 1) * width] = part

    for first_column, w_ref in ((0, wa_ref), (half, wb_ref)):

        @pl.loop(0, half // COLUMN_TILE)
        def _(j):
            cut = pl.ds(pl.multiple_of(j * COLUMN_TILE, COLUMN_TILE), COLUMN_TILE)
            to = pl.ds(pl.multiple_of(first_column + j * COLUMN_TILE, COLUMN_TILE), COLUMN_TILE)
            product = dot(normed[...], w_ref[:, cut]).astype(BF16)
            for n in range(1, count):
                out_ref[blocks[n], to] = product[(n - 1) * size : n * size]


def pass_kernel(count, step, column, here_ref, *refs):
    sums_ref, even_out, odd_out = refs[-3:]
    arrived = refs[:-3]
    size, width = even_out.shape
    here = here_ref[0]

    def send(shift, came, out):
        block = jnp.clip(here + shift, 0, count - 1)
        rows = pl.ds(pl.multiple_of(block * size, size), size)
        own = sums_ref[rows, column : column + width].astype(F32)
        for ref in came:
            own = own + ref[...].astype(F32)
        out[...] = own.astype(BF16)

    for parity, to_right, to_left, from_left, from_right in (
        (0, even_out, odd_out, arrived[1:], arrived[:1]),
        (1, odd_out, even_out, arrived[:1], arrived[1:]),
    ):

        @pl.when((here & 1) == parity)
        def _():
            send(count - step, from_left, to_right)
            send(step - count, from_right, to_left)


def sum_kernel(column, here_ref, even_ref, odd_ref, sums_ref, *refs):
    out_hbm, total, semaphores = refs[-3:]
    size, width = even_ref.shape
    rows = pl.ds(pl.multiple_of(here_ref[0] * size, size), size)
    copies = []
    for n in range(SUM_COPIES):
        part = rows_of(n, size // SUM_COPIES)
        own = sums_ref[rows, column : column + width][part, :].astype(F32)
        total[part, :] = (own + even_ref[part, :].astype(F32) + odd_ref[part, :].astype(F32)).astype(BF16)
        to = out_hbm.at[part, column : column + width]
        copies.extend(load([(total.at[part, :], to)], semaphores.at[pl.ds(n, 1)]))
    for copy in copies:
        copy.wait()


def block_order(here, count):
    order = []
    for step in range(1, count):
        for block, sends in ((count - step + here, here <= step - 1), (step - count + here, here >= count - step)):
            if sends and block not in order:
                order.append(block)
    return order + [b for b in range(count) if b not in order]


def in_vmem(kernel, name, ins, outs, scratch=(), vmem=4, flops=1, result=None, aliases=None):
    vm = pl.BlockSpec(memory_space=pltpu.VMEM)
    specs, arrays = [], []
    for v in ins:
        if isinstance(v, tuple):
            specs.append(pl.BlockSpec(memory_space=pltpu.HBM))
            arrays.append(pltpu.with_memory_space_constraint(v[0], pltpu.HBM))
        elif v.dtype == jnp.int32:
            specs.append(pl.BlockSpec(memory_space=pltpu.SMEM))
            arrays.append(v)
        else:
            specs.append(vm)
            arrays.append(pltpu.with_memory_space_constraint(v, pltpu.VMEM))
    in_hbm = outs is None
    return pl.pallas_call(
        kernel,
        in_specs=specs,
        out_specs=[pl.BlockSpec(memory_space=pltpu.HBM)] if in_hbm else [vm for _ in outs],
        out_shape=[pltpu.HBM(*result)] if in_hbm else [pltpu.VMEM(shape, kind) for shape, kind in outs],
        scratch_shapes=list(scratch),
        input_output_aliases={len(ins) - 1: 0} if in_hbm and isinstance(ins[-1], tuple) else aliases or {},
        compiler_params=pltpu.CompilerParams(vmem_limit_bytes=vmem * 2**20),
        cost_estimate=pl.CostEstimate(flops=flops, bytes_accessed=1, transcendentals=0),
        name=name,
    )(*arrays)


def line_reduce(first, partial_sums, here, size, columns):
    count = lax.axis_size("tp")
    width = columns // PARTS
    block = ((size, width), BF16)
    even_edges = [(i, i ^ 1) for i in range(count)]
    odd_edges = [(i, ((i + 1) ^ 1) - 1) for i in range(1, count - 1)]
    arrived = [()] * PARTS
    for step in range(1, count):
        for half in range(PARTS):
            if step == 1:
                arrived[half] = (lax.ppermute(first[half], "tp", even_edges),)
                continue
            even, odd = in_vmem(
                partial(pass_kernel, count, step, half * width), "pass_on", (here, *arrived[half], partial_sums), (block, block)
            )
            arrived[half] = (lax.ppermute(even, "tp", even_edges), lax.ppermute(odd, "tp", odd_edges))
    out = ()
    for half in range(PARTS):
        ins = (here, *arrived[half], partial_sums, *out)
        scratch = [pltpu.VMEM((size, width), BF16), pltpu.SemaphoreType.DMA((SUM_COPIES,))]
        kernel = partial(sum_kernel, half * width)
        out = (tuple(in_vmem(kernel, "sum_up", ins, None, scratch, result=((size, columns), BF16))),)
    return out[0][0]


def on_device(x_in, gate_z, b_in, c_in, step_size, log_decay, skip, norm_gain, out_weight):
    rows, channels = x_in.shape
    heads = step_size.shape[1]
    groups = b_in.shape[1] // STATE
    chunks = rows // CHUNK
    columns = out_weight.shape[1]
    half = channels // 2
    devices = lax.axis_size("ctx")
    chips = devices // 2
    count = lax.axis_size("tp")
    size = rows // count
    ctx = lax.axis_index("ctx").astype(jnp.int32).reshape(1)
    here = lax.axis_index("tp").astype(jnp.int32).reshape(1)
    message = ((half + EXTRA, 128), BF16)
    whole = ((rows, channels), F32)
    by_head = ((heads, rows), F32)
    maps = ((rows, groups * STATE), BF16)
    weighted = pltpu.VMEM((rows, half), BF16)

    send, x_here, b_here, step, decay, spread = in_vmem(
        partial(send_kernel, groups),
        "end_state_sent",
        (ctx, here, (x_in,), (b_in,), (step_size.T,), (log_decay.T,)),
        (message, ((rows, channels), BF16), maps, by_head, by_head, ((128, half), BF16)),
        scratch=[weighted, pltpu.SemaphoreType.DMA((4 + chunks,))],
        vmem=6,
    )
    swap = [(i, i ^ 1) for i in range(devices)]
    sibling = lax.ppermute(send, "ctx", swap)
    own, all_spread = in_vmem(
        partial(keep_kernel, groups), "end_state_kept", (ctx, x_here, b_here, step, decay, spread),
        (message, ((128, channels), BF16)), [weighted],
        vmem=6, flops=10**9,
    )
    piece = ((half // PIECES + EXTRA, 128), BF16)
    totals = in_vmem(pair_kernel, "pair", (ctx, spread, own, sibling), (piece,) * PIECES)
    levels = chips.bit_length() - 1

    def swap_chips(level, blocks):
        return [lax.ppermute(v, "ctx", [(i, i ^ (2 << level)) for i in range(devices)]) for v in blocks]

    def local_part(part_index, after, carried):
        return in_vmem(
            partial(local_kernel, groups, part_index),
            "local_part",
            ((gate_z,), (c_in,), (out_weight,), x_here, b_here, step, decay, skip.reshape(1, heads), all_spread, after, *carried),
            (
                whole,
                whole,
                maps,
                ((STATE, channels), F32),
                ((heads, 128), F32),
                ((channels, columns // 2), BF16),
                ((EXTRA, 128), BF16),
            ),
            scratch=[
                pltpu.VMEM((rows // 2, channels), BF16),
                pltpu.SemaphoreType.DMA((1 + chunks // 2 + WEIGHT_COPIES,)),
            ],
            vmem=10,
            flops=4 * 10**9,
            aliases={10 + n: n for n in range(len(carried))},
        )

    received = swap_chips(0, totals)
    *carried, weight_a, token = local_part(0, totals[-1], ())
    arrived = list(received)
    for level in range(1, levels):
        folded = []
        for n in range(PIECES):
            kernel = partial(fold_kernel, level - 1, n)
            after = folded[-1] if folded else token
            folded.extend(in_vmem(kernel, "fold", (ctx, after, spread, totals[n], received[n]), (piece,)))
        totals = folded
        received = swap_chips(level, totals)
        arrived.extend(received)
    mixed, scale, c_here, _, _, weight_b, token = local_part(1, totals[-1], carried)
    state = ((STATE, half), BF16)
    keep, send = in_vmem(
        partial(last_kernel, levels), "incoming", (ctx, token, spread, own, sibling, *arrived), (state, state)
    )
    recv = lax.ppermute(send, "ctx", swap)

    gain = norm_gain.reshape(1, channels)
    width = columns // PARTS
    piece = ((size, width), BF16)
    row_block = ((size, channels), BF16)
    whole_state = pltpu.VMEM((STATE, channels), BF16)
    inputs = (ctx, here, mixed, scale, c_here, gain, weight_a)
    if groups == 2:
        own_group, product = in_vmem(
            partial(own_group_kernel, count), "own_group", (*inputs, keep), (((size, half), BF16), ((size, width), F32)),
            flops=10**9,
        )
        first, normed = in_vmem(
            partial(other_group_kernel, count), "other_group", (*inputs, recv, own_group, product), (piece, row_block)
        )
    else:
        first, normed = in_vmem(
            partial(both_groups_kernel, groups, count), "both_groups", (*inputs, keep, recv), (piece, row_block), [whole_state]
        )
    pieces_out = [first]
    for start, weight, number in ((1, weight_a, PARTS // 2 - 1), (0, weight_b, PARTS // 2)):
        kernel = partial(project_kernel, start * width)
        pieces_out.extend(in_vmem(kernel, "first_block_rest", (normed, weight), (piece,) * number))
    (partial_sums,) = in_vmem(
        partial(rest_kernel, groups, count),
        "other_blocks",
        (*inputs, weight_b, keep, recv, *pieces_out),
        (((rows, columns), BF16),),
        [whole_state, pltpu.VMEM((rows - size, channels), BF16)],
        vmem=6,
    )
    return line_reduce(pieces_out, partial_sums, here, size, columns)


def solution(mesh):
    placed = (
        P("ctx", "tp"),
        P("ctx", "tp"),
        P("ctx", "tp"),
        P("ctx", "tp"),
        P("ctx", "tp"),
        P("ctx", "tp"),
        P("tp"),
        P("tp"),
        P("tp", None),
    )
    return jax.shard_map(
        on_device, mesh=mesh, in_specs=placed, out_specs=P(("ctx", "tp"), None), check_vma=False
    )
```
